768 devices in a mesh: stratum: 16 (over y_hi, x, core), inner: 48 (over z, y_lo).
Axes of the slice: x: 4, y: 8 (y_hi: 2, y_lo: 4; y = y_hi * 4 + y_lo), z: 12, core: 2. Of those that a mesh axis runs over, the one named last changes fastest.
Arguments:
- user_factors: float32 [393216, 256], P(('stratum', 'inner')), may hold values from -2 to 2
- item_factors: float32 [12288, 256], P(('stratum', 'inner')), may hold values from -3 to 3
- item_accum: float32 [12288, 256], P(('stratum', 'inner')), may hold values from 0.5 to 4
- tile_values: bfloat16 [2, 6144, 128, 128], P(None, ('stratum', 'inner')), may hold values from -6 to 6
- tile_rows: int32 [2, 6144], P(None, ('stratum', 'inner')), may hold values from 0 to 3
- tile_cols: int32 [2, 6144], P(None, ('stratum', 'inner')), may hold values from 0 to 5
- tile_count: int32 [2, 768], P(None, ('stratum', 'inner')), may hold values from 2 to 8, as said below
- neg_ids: int32 [2, 3072], P(None, ('stratum', 'inner')), may hold values from 0 to 15
Outputs:
- users_out: float32 [393216, 256], P(('stratum', 'inner'))
- items_out: float32 [12288, 256], P(('stratum', 'inner'))
- accum_out: float32 [12288, 256], P(('stratum', 'inner'))
The draws below stay inside these ranges and needn't reach their ends.
Inputs may be any that keep to these rules, and one draw needn't show every extreme that they name: Only the first tile_count slots of a device's list are live in a sub-epoch; in every sub-epoch some device fills all 8 slots.
All inputs are finite; a program needn't handle non-finite values.
Results may differ from the reference program's by a relative error of at most 0.00115.
The reference program's roundings to bfloat16 on the way count: a program that leaves them out, or rounds other values in their place, can miss the bound.
Values may be sent and summed in bfloat16 or wider, within the bound.
No kernel may reach another device: no remote copies, remote signals or barrier semaphores. Data moves between devices by JAX's collectives and lax.ppermute only.
A program may use at most 32 MiB of HBM per device.

```python
import math
import jax
import jax.numpy as jnp
from jax import lax

R = 256
UDEV = 512
IDEV = 16
TU = 128
TI = 128
NT = 8
NNEG = 4
ITERS = 2
USERS = 393216
ITEMS = 12288
ITEM_BLOCK = 768
SLOTS = 6144
NEGS = 3072
N_STRATUM = 16
N_INNER = 48


def draw_tile_count(key, part):
    key = jax.random.fold_in(key, 7)
    first, second = jax.random.split(key)
    devices = N_STRATUM * N_INNER
    counts = jax.random.randint(first, (ITERS, devices), NT // 4, NT + 1)
    fullest = jax.random.randint(second, (ITERS, 1), 0, devices)
    marks = jnp.arange(devices)[None, :] == fullest
    return jnp.where(marks, NT, counts).astype(jnp.int32)


def plant(drawn, stream_key, least, high):
    longest = drawn.shape.index(max(drawn.shape))
    spots = []
    for shift in (0, 1):
        where = [jax.random.randint(jax.random.fold_in(stream_key, axis), (), 0, length) for axis, length in enumerate(drawn.shape)]
        where[longest] = (where[longest] + shift) % drawn.shape[longest]
        spots.append(tuple(where))
    return drawn.at[spots[0]].set(least).at[spots[1]].set(high)


def steps_of(own_key, dims, shards, smallest, top_value):
    factor_of = 1.0
    for dim, parts in shards:
        steps = jax.random.uniform(jax.random.fold_in(jax.random.fold_in(own_key, 6), dim), (parts,), jnp.float32, smallest / len(shards), top_value / len(shards))
        factor_of = factor_of * jnp.repeat(jnp.exp(steps), dims[dim] // parts).reshape((-1,) + (1,) * (len(dims) - 1 - dim))
    return factor_of


def gaussian(stream_key, extent, deviation, limit, cuts=(), dtype=jnp.bfloat16):
    values = deviation * jax.random.normal(stream_key, extent, jnp.float32)
    if cuts:
        values = values * steps_of(stream_key, extent, cuts, -0.22, 0.18)
    return jnp.clip(values, -limit, limit).astype(dtype)


def setup_inputs(seed: int = 0) -> dict:
    streams_of = jax.random.split(jax.random.key(seed), 9)
    user_factors = gaussian(streams_of[0], (USERS, R), 0.3, 2.0, ((0, 768),), jnp.float32)
    item_factors = gaussian(streams_of[1], (ITEMS, R), 0.5, 3.0, ((0, 768),), jnp.float32)
    item_accum = jnp.clip(jnp.exp(math.log(4.0) - 2.0794415 * jax.random.uniform(streams_of[2], (ITEMS, R), jnp.float32) ** steps_of(streams_of[2], (ITEMS, R), ((0, 768),), -0.2, 0.2)), 0.5, 4.0)
    tile_values = gaussian(streams_of[3], (ITERS, SLOTS, TU, TI), 1.0, 6.0, ((1, 768),))
    tile_rows = plant(jax.random.randint(streams_of[4], (ITERS, SLOTS), 0, UDEV // TU), jax.random.fold_in(streams_of[4], 1), 0, (UDEV // TU) - 1).astype(jnp.int32)
    tile_cols = plant(jax.random.randint(streams_of[5], (ITERS, SLOTS), 0, ITEM_BLOCK // TI), jax.random.fold_in(streams_of[5], 1), 0, (ITEM_BLOCK // TI) - 1).astype(jnp.int32)
    tile_count = draw_tile_count(jax.random.fold_in(streams_of[8], 71), 0)
    neg_ids = plant(jax.random.randint(streams_of[7], (ITERS, NEGS), 0, IDEV), jax.random.fold_in(streams_of[7], 1), 0, IDEV - 1).astype(jnp.int32)
    return {"user_factors": user_factors, "item_factors": item_factors, "item_accum": item_accum, "tile_values": tile_values, "tile_rows": tile_rows, "tile_cols": tile_cols, "tile_count": tile_count, "neg_ids": neg_ids}


LR_USER = 0.005
LR_ITEM = 0.05
LAMBDA = 64.0

def tile_grads(user_bf, block, values, rows, cols, count):
    slots = values.shape[0]
    tile_u = values.shape[1]
    tile_i = values.shape[2]
    rank = user_bf.shape[1]
    user_tiles = user_bf.reshape(-1, tile_u, rank)[rows].astype(jnp.float32)
    item_tiles = block.reshape(-1, tile_i, rank)[cols].astype(jnp.float32)
    scores = jnp.einsum('ntr,nir->nti', user_tiles, item_tiles)
    live = jnp.arange(slots) < count
    errors = jnp.where(live[:, None, None], scores - values.astype(jnp.float32), 0.0)
    errors = errors.astype(jnp.bfloat16).astype(jnp.float32)
    user_part = jnp.einsum('nti,nir->ntr', errors, item_tiles)
    item_part = jnp.einsum('nti,ntr->nir', errors, user_tiles)
    row_hot = (jnp.arange(user_bf.shape[0] // tile_u)[:, None] == rows[None, :]).astype(jnp.float32)
    col_hot = (jnp.arange(block.shape[0] // tile_i)[:, None] == cols[None, :]).astype(jnp.float32)
    grad_users = jnp.einsum('bn,ntr->btr', row_hot, user_part, precision=lax.Precision.HIGHEST)
    grad_items = jnp.einsum('cn,nir->cir', col_hot, item_part, precision=lax.Precision.HIGHEST)
    return (grad_users.reshape(-1, rank), grad_items.reshape(-1, rank))

def reference(user_factors, item_factors, item_accum, tile_values, tile_rows, tile_cols, tile_count, neg_ids):
    strata = N_STRATUM
    inners = N_INNER
    users = user_factors.reshape(strata, inners, UDEV, R)
    held = item_factors.reshape(strata, ITEM_BLOCK, R)
    accum = item_accum.reshape(strata, ITEM_BLOCK, R)
    for step in range(ITERS):
        held_bf = held.astype(jnp.bfloat16)
        owned = held_bf.reshape(strata * inners, IDEV, R)
        picks = neg_ids[step].reshape(strata * inners, NNEG)
        picked = jnp.take_along_axis(owned, picks[:, :, None], axis=1).astype(jnp.float32)
        gram = jnp.einsum('dnr,dns->rs', picked, picked, precision=lax.Precision.HIGHEST) / NEGS
        values = tile_values[step].reshape(strata, inners, NT, TU, TI)
        rows = tile_rows[step].reshape(strata, inners, NT)
        cols = tile_cols[step].reshape(strata, inners, NT)
        counts = tile_count[step].reshape(strata, inners)

        def group(items):
            user_g, block, value_g, row_g, col_g, count_g = items

            def single(total, pieces):
                user_d, value_d, row_d, col_d, count_d = pieces
                grad_u, grad_i = tile_grads(user_d.astype(jnp.bfloat16), block, value_d, row_d, col_d, count_d)
                return (total + grad_i, grad_u)
            total, grad_u = lax.scan(single, jnp.zeros((ITEM_BLOCK, R), jnp.float32), (user_g, value_g, row_g, col_g, count_g))
            return (grad_u, total)
        grad_users, grad_items = lax.map(group, (users, held_bf, values, rows, cols, counts))
        grad_users = grad_users + LAMBDA * jnp.einsum('giur,rs->gius', users, gram, precision=lax.Precision.HIGHEST)
        users = users - LR_USER * grad_users
        accum = accum + grad_items * grad_items
        held = held - LR_ITEM * grad_items / jnp.sqrt(accum)
        held = jnp.roll(held, -1, axis=0)
        accum = jnp.roll(accum, -1, axis=0)
    return (users.reshape(USERS, R), held.reshape(ITEMS, R), accum.reshape(ITEMS, R))
```

```python
import functools

import jax
import jax.numpy as jnp
from jax import lax
from jax.experimental import pallas as pl
from jax.experimental.pallas import tpu as pltpu
from jax.sharding import PartitionSpec as P

LR_USER = 0.005
LR_ITEM = 0.05
LAMBDA = 64.0

LANES = 128
F32 = jnp.float32
BF16 = jnp.bfloat16
F16 = jnp.float16

GRAD_SCALE = 2.0**-6
ROOT_SCALE = 2.0**-9
ITEM_SCALE = 2.0**12
GRAM_SCALE = 2.0**12
GRAM_LOCAL_SCALE = 2.0**10
GRAM_INNER_SCALE = 2.0**6

VMEM = pltpu.VMEM
SMEM = pltpu.SMEM


def contract(a, b, dims):
    return lax.dot_general(a, b, ((dims[:1], dims[1:]), ((), ())), preferred_element_type=F32)


def halves(x):
    return jnp.concatenate([x[:, :LANES], x[:, LANES:]], axis=0)


def widths(x):
    rows = x.shape[0] // 2
    return jnp.concatenate([x[:rows], x[rows:]], axis=1)


def picked_rows(items, ids_ref, step):
    count = ids_ref.shape[1]
    row = lax.broadcasted_iota(jnp.int32, (8, items.shape[0]), 0)
    col = lax.broadcasted_iota(jnp.int32, (8, items.shape[0]), 1)
    hot = jnp.zeros((8, items.shape[0]), F32)
    for n in range(count):
        hot = jnp.where((row == n) & (col == ids_ref[step, n]), 1.0, hot)
    return contract(hot.astype(BF16), items, (1, 0))


def gram_parts(rows):
    left, right = rows[:, :LANES], rows[:, LANES:]
    top = contract(left, rows, (0, 0))
    low = contract(right, right, (0, 0))
    return jnp.concatenate([top[:, :LANES], top[:, LANES:], low], axis=0)


def whole_gram(parts):
    a, b, c = parts[:LANES], parts[LANES : 2 * LANES], parts[2 * LANES :]
    return jnp.concatenate(
        [jnp.concatenate([a, b], axis=1), jnp.concatenate([b.T, c], axis=1)], axis=0
    )


def split(x):
    high = x.astype(BF16)
    return high, (x - high.astype(F32)).astype(BF16)


def times_gram(users, gram):
    uh, ul = split(users)
    gh, gl = split(gram)
    return contract(uh, gh, (1, 0)) + (contract(ul, gh, (1, 0)) + contract(uh, gl, (1, 0)))


def slot_grads(step, users_bf, block, values, rows, cols, count, grad_users, sums):
    slots, tile_u, tile_i = values.shape[1:]
    chunk = 16
    live = count[step, 0]
    for k in range(slots):
        row = pl.multiple_of(rows[step, k] * tile_u, tile_u)
        col = cols[step, k]
        user_tile = users_bf[pl.ds(row, tile_u), :]
        item_tile = block[pl.ds(pl.multiple_of(col * tile_i, tile_i), tile_i), :]
        scores = contract(user_tile, item_tile, (1, 1))
        err = jnp.where(k < live, scores - values[step, k].astype(F32), 0.0).astype(BF16)
        grad_users[pl.ds(row, tile_u), :] += contract(err, item_tile, (1, 0))
        part = contract(err, user_tile, (0, 0))
        at = pl.ds(col * (tile_i // chunk), tile_i // chunk)
        sums[at, 0:chunk, :] += part[:, :LANES].reshape(-1, chunk, LANES)
        sums[at, chunk : 2 * chunk, :] += part[:, LANES:].reshape(-1, chunk, LANES)


def first_kernel(block, users, own, values, rows, cols, count, ids, sums, users_out, users_bf, grad_users):
    chunks = sums.shape[0]
    users_bf[...] = users[...].astype(BF16)
    grad_users[...] = jnp.zeros_like(grad_users)
    sums[...] = jnp.zeros_like(sums)
    slot_grads(0, users_bf, block, values, rows, cols, count, grad_users, sums)
    sums[:, 0:32, :] = sums[:, 0:32, :] * GRAD_SCALE
    picks = picked_rows(own[...].astype(BF16), ids, 0).astype(BF16)
    sums[:, 32:, :] = (gram_parts(picks) * GRAM_LOCAL_SCALE).reshape(chunks, -1, LANES)
    users_out[...] = users[...] - LR_USER * grad_users[...]


def update(held, accum, gradient):
    accum = accum + gradient * gradient
    return held - LR_ITEM * gradient / jnp.sqrt(accum), accum


def item_kernel(total, held, accum, out):
    rows = held.shape[0]
    gradient = widths(total[...] * (1.0 / GRAD_SCALE))
    out[0:rows, :], out[rows:, :] = update(held[...], accum[...], gradient)


def meet_kernel(state, ids, out):
    rows = state.shape[0] // 2
    picks = picked_rows(state[0:rows, :].astype(BF16), ids, 1)
    out[...] = halves(picks[0:4, :])


def gather_kernel(total, negs, met, state, gram_part, out):
    chunks = out.shape[0]
    piece = gram_part.shape[0]
    rows = state.shape[0] // 2
    items = halves(state[0:rows, :].astype(BF16).astype(F32)) * ITEM_SCALE
    out[:, 0:32, :] = jnp.broadcast_to(items[None], (chunks, 32, LANES))
    full = gram_part[...] * (GRAM_SCALE / GRAM_LOCAL_SCALE / total)
    out[:, 32 : 32 + piece, :] = jnp.broadcast_to(full[None], (chunks, piece, LANES))
    left = met[:, 0:negs, :].reshape(-1, LANES)
    right = met[:, negs:, :].reshape(-1, LANES)
    picks = jnp.concatenate([left, right], axis=1).astype(BF16)
    out[:, 32 + piece :, :] = (gram_parts(picks) * GRAM_INNER_SCALE).reshape(chunks, piece, LANES)


def second_kernel(
    total, got, users, mid, values, rows, cols, count, sums, users_out, mid_out, users_bf, grad_users, block
):
    chunks = sums.shape[0]
    piece = sums.shape[1] - 32
    left = (got[:, 0:16, :] * (1.0 / ITEM_SCALE)).astype(BF16).reshape(-1, LANES)
    right = (got[:, 16:32, :] * (1.0 / ITEM_SCALE)).astype(BF16).reshape(-1, LANES)
    block[:, :LANES] = left
    block[:, LANES:] = right
    gram = whole_gram(got[:, 32 : 32 + piece, :].reshape(-1, LANES) * (1.0 / GRAM_SCALE))
    now = mid[...] - (LR_USER * LAMBDA) * times_gram(users[...], gram)
    mid_out[...] = now
    users_bf[...] = now.astype(BF16)
    grad_users[...] = jnp.zeros_like(grad_users)
    sums[...] = jnp.zeros_like(sums)
    slot_grads(1, users_bf, block, values, rows, cols, count, grad_users, sums)
    raw = sums[:, 0:32, :]
    root = jnp.sqrt(jnp.abs(raw)) * ROOT_SCALE
    sums[:, 0:32, :] = jnp.where(raw < 0.0, -root, root)
    full = jnp.sum(got[:, 32 + piece :, :], axis=0) * (GRAM_SCALE / GRAM_INNER_SCALE / total)
    sums[:, 32:, :] = jnp.broadcast_to(full[None], (chunks, piece, LANES))
    users_out[...] = now - LR_USER * grad_users[...]


def last_items_kernel(total, state, out):
    rows = state.shape[0] // 2
    out[0:rows, :], out[rows:, :] = update(state[0:rows, :], state[rows:, :], widths(total[...]))


def last_users_kernel(got, users, mid, out):
    gram = whole_gram(got[...].reshape(-1, LANES) * (1.0 / GRAM_SCALE))
    out[...] = users[...] - (LR_USER * LAMBDA) * times_gram(mid[...], gram)


def call(kernel, out_shape, specs, *args, scratch=()):
    return pl.pallas_call(
        kernel,
        out_shape=out_shape,
        in_specs=specs,
        out_specs=jax.tree.map(lambda _: pl.BlockSpec(memory_space=VMEM), out_shape),
        scratch_shapes=scratch,
        compiler_params=pltpu.CompilerParams(vmem_limit_bytes=40 * 2**20),
    )(*args)


def exchanged(x, axis):
    return lax.all_to_all(x, axis, 0, 0, tiled=True)


def shards(
    user_factors, item_factors, item_accum, tile_values, tile_rows, tile_cols, tile_count, neg_ids
):
    strata = lax.axis_size("stratum")
    inners = lax.axis_size("inner")
    own, rank = item_factors.shape
    negs = neg_ids.shape[1]
    total = float(strata * inners * negs)
    piece = 3 * LANES // inners
    users_shape = jax.ShapeDtypeStruct(user_factors.shape, F32)
    state_shape = jax.ShapeDtypeStruct((2 * own, rank), F32)
    users_scratch = [pltpu.VMEM(user_factors.shape, BF16), pltpu.VMEM(user_factors.shape, F32)]
    sums_shape = jax.ShapeDtypeStruct((inners, 2 * own + piece, LANES), F32)
    vm = pl.BlockSpec(memory_space=VMEM)
    sm = pl.BlockSpec(memory_space=SMEM)
    onward = [((s + 1) % strata, s) for s in range(strata)]

    held_bf = jnp.broadcast_to(item_factors.astype(BF16)[None], (inners, own, rank))
    block = exchanged(held_bf, "inner").reshape(inners * own, rank)
    sums, mid = call(
        first_kernel,
        (sums_shape, users_shape),
        [vm, vm, vm, vm, sm, sm, sm, sm],
        block, user_factors, item_factors, tile_values, tile_rows, tile_cols, tile_count, neg_ids,
        scratch=users_scratch,
    )
    got = jnp.sum(exchanged(sums.astype(F16), "inner").astype(F32), axis=0)
    state = call(item_kernel, state_shape, [vm, vm, vm], got[: 2 * own], item_factors, item_accum)
    state = lax.ppermute(state, "stratum", onward)
    picks = call(meet_kernel, jax.ShapeDtypeStruct((2 * negs, LANES), F32), [vm, sm], state, neg_ids)
    sent = jnp.concatenate([got[2 * own :], picks], axis=0)
    met = exchanged(jnp.broadcast_to(sent[None], (strata,) + sent.shape), "stratum")
    payload = call(
        functools.partial(gather_kernel, total, negs),
        jax.ShapeDtypeStruct((inners, 2 * own + 2 * piece, LANES), F32),
        [vm, vm, vm],
        met[:, piece:], state, jnp.sum(met[:, :piece], axis=0),
    )
    got = exchanged(payload.astype(F16), "inner").astype(F32)
    sums, users, mid = call(
        functools.partial(second_kernel, total),
        (sums_shape, users_shape, users_shape),
        [vm, vm, vm, vm, sm, sm, sm],
        got, user_factors, mid, tile_values, tile_rows, tile_cols, tile_count,
        scratch=users_scratch + [pltpu.VMEM((inners * own, rank), BF16)],
    )
    got = exchanged(sums.astype(F16), "inner").astype(F32)
    root = got[:, : 2 * own]
    gradient = jnp.sum(root * jnp.abs(root), axis=0) * (ROOT_SCALE**-2)
    state = call(last_items_kernel, state_shape, [vm, vm], gradient, state)
    state = lax.ppermute(state, "stratum", onward)
    users = call(last_users_kernel, users_shape, [vm, vm, vm], got[:, 2 * own :], users, mid)
    return (users, state[:own], state[own:])


def solution(mesh):
    devices = P(("stratum", "inner"), None)
    slots = P(None, ("stratum", "inner"))
    return jax.shard_map(
        shards,
        mesh=mesh,
        in_specs=(
            devices,
            devices,
            devices,
            P(None, ("stratum", "inner"), None, None),
            slots,
            slots,
            slots,
            slots,
        ),
        out_specs=(devices, devices, devices),
        check_vma=False,
    )
```

```python
import functools

import jax
import jax.numpy as jnp
from jax import lax
from jax.experimental import pallas as pl
from jax.experimental.pallas import tpu as pltpu
from jax.sharding import PartitionSpec as P

LR_USER = 0.005
LR_ITEM = 0.05
LAMBDA = 64.0

LANES = 128
F32 = jnp.float32
BF16 = jnp.bfloat16
F16 = jnp.float16

GRAD_SCALE = 2.0**-6
ROOT_SCALE = 2.0**-9
ITEM_SCALE = 2.0**12
GRAM_SCALE = 2.0**12
GRAM_LOCAL_SCALE = 2.0**10
GRAM_STRATUM_SCALE = 2.0**5
GRAM_INNER_SCALE = 2.0**6

VMEM = pltpu.VMEM
SMEM = pltpu.SMEM


def contract(a, b, dims):
    return lax.dot_general(a, b, ((dims[:1], dims[1:]), ((), ())), preferred_element_type=F32)


def halves(x):
    return jnp.concatenate([x[:, :LANES], x[:, LANES:]], axis=0)


def widths(x):
    rows = x.shape[0] // 2
    return jnp.concatenate([x[:rows], x[rows:]], axis=1)


def picked_rows(items, ids_ref, step):
    count = ids_ref.shape[1]
    row = lax.broadcasted_iota(jnp.int32, (8, items.shape[0]), 0)
    col = lax.broadcasted_iota(jnp.int32, (8, items.shape[0]), 1)
    hot = jnp.zeros((8, items.shape[0]), F32)
    for n in range(count):
        hot = jnp.where((row == n) & (col == ids_ref[step, n]), 1.0, hot)
    return contract(hot.astype(BF16), items, (1, 0))


def gram_parts(weighed, rows):
    top = contract(weighed[:, :LANES], rows, (0, 0))
    low = contract(weighed[:, LANES:], rows[:, LANES:], (0, 0))
    return jnp.concatenate([top[:, :LANES], top[:, LANES:], low], axis=0)


def whole_gram(parts):
    a, b, c = parts[:LANES], parts[LANES : 2 * LANES], parts[2 * LANES :]
    return jnp.concatenate(
        [jnp.concatenate([a, b], axis=1), jnp.concatenate([b.T, c], axis=1)], axis=0
    )


def split(x):
    high = x.astype(BF16)
    return high, (x - high.astype(F32)).astype(BF16)


def times_gram(users, gram):
    uh, ul = split(users)
    gh, gl = split(gram)
    return contract(uh, gh, (1, 0)) + (contract(ul, gh, (1, 0)) + contract(uh, gl, (1, 0)))


def slot_grads(step, users_bf, block, values, rows, cols, count, grad_users, sums):
    slots, tile_u, tile_i = values.shape[1:]
    chunk = 16
    live = count[step, 0]
    for k in range(slots):
        row = pl.multiple_of(rows[step, k] * tile_u, tile_u)
        col = cols[step, k]
        user_tile = users_bf[pl.ds(row, tile_u), :]
        item_tile = block[pl.ds(pl.multiple_of(col * tile_i, tile_i), tile_i), :]
        scores = contract(user_tile, item_tile, (1, 1))
        err = jnp.where(k < live, scores - values[step, k].astype(F32), 0.0).astype(BF16)
        grad_users[pl.ds(row, tile_u), :] += contract(err, item_tile, (1, 0))
        part = contract(err, user_tile, (0, 0))
        at = pl.ds(col * (tile_i // chunk), tile_i // chunk)
        sums[at, 0:chunk, :] += part[:, :LANES].reshape(-1, chunk, LANES)
        sums[at, chunk : 2 * chunk, :] += part[:, LANES:].reshape(-1, chunk, LANES)


def first_kernel(block, users, own, values, rows, cols, count, ids, sums, users_out, users_bf, grad_users):
    chunks = sums.shape[0]
    users_bf[...] = users[...].astype(BF16)
    grad_users[...] = jnp.zeros_like(grad_users)
    sums[...] = jnp.zeros_like(sums)
    slot_grads(0, users_bf, block, values, rows, cols, count, grad_users, sums)
    sums[:, 0:32, :] = sums[:, 0:32, :] * GRAD_SCALE
    picks = picked_rows(own[...].astype(BF16), ids, 0).astype(BF16)
    sums[:, 32:, :] = (gram_parts(picks, picks) * GRAM_LOCAL_SCALE).reshape(chunks, -1, LANES)
    users_out[...] = users[...] - LR_USER * grad_users[...]


def update(held, accum, gradient):
    accum = accum + gradient * gradient
    return held - LR_ITEM * gradient / jnp.sqrt(accum), accum


def pick_counts(ids_ref, step):
    row = lax.broadcasted_iota(jnp.int32, (8, LANES), 0)
    lane = lax.broadcasted_iota(jnp.int32, (8, LANES), 1)
    row = jnp.where(lane < LANES // 2, row, row + 8)
    counts = jnp.zeros((8, LANES), F32)
    for n in range(ids_ref.shape[1]):
        counts = counts + jnp.where(row == ids_ref[step, n], 1.0, 0.0)
    return counts


def item_kernel(got, held, accum, ids, state, out):
    rows = held.shape[0]
    piece = got.shape[1] - 2 * rows
    total = jnp.sum(got[...], axis=0)
    gradient = widths(total[0 : 2 * rows] * (1.0 / GRAD_SCALE))
    new, state[rows:, :] = update(held[...], accum[...], gradient)
    state[0:rows, :] = new
    strata = out.shape[0]
    sent = jnp.concatenate(
        [
            halves(new.astype(BF16).astype(F32)) * ITEM_SCALE,
            pick_counts(ids, 1),
            total[2 * rows :] * (GRAM_STRATUM_SCALE / GRAM_LOCAL_SCALE),
        ],
        axis=0,
    )
    out[...] = jnp.broadcast_to(sent[None], (strata, 2 * rows + 8 + piece, LANES))


def gather_kernel(total, met, out):
    chunks = out.shape[0]
    strata = met.shape[0]
    piece = met.shape[1] - 40
    after = lax.rem(lax.axis_index("stratum") + 1, strata)
    items = met[pl.ds(after, 1), 0:32, :]
    out[:, 0:32, :] = jnp.broadcast_to(items, (chunks, 32, LANES))
    full = jnp.sum(met[:, 40:, :], axis=0) * (GRAM_SCALE / GRAM_STRATUM_SCALE / total)
    out[:, 32 : 32 + piece, :] = jnp.broadcast_to(full[None], (chunks, piece, LANES))
    counts = jnp.concatenate([met[-1:, 32:40, :], met[:-1, 32:40, :]], axis=0)
    counts = jnp.concatenate([counts[:, :, 0:1], counts[:, :, 64:65]], axis=1)
    rows = [met[:, 0:16, :] * (1.0 / ITEM_SCALE), met[:, 16:32, :] * (1.0 / ITEM_SCALE)]
    weighed = jnp.concatenate([(r * counts).reshape(-1, LANES) for r in rows], axis=1)
    plain = jnp.concatenate([r.reshape(-1, LANES) for r in rows], axis=1).astype(BF16)
    high, low = split(weighed)
    parts = gram_parts(jnp.concatenate([high, low], axis=0), jnp.concatenate([plain, plain], axis=0))
    out[:, 32 + piece :, :] = (parts * GRAM_INNER_SCALE).reshape(chunks, piece, LANES)


def second_kernel(
    total, got, users, mid, values, rows, cols, count, sums, users_out, mid_out, users_bf, grad_users, block
):
    chunks = sums.shape[0]
    piece = sums.shape[1] - 32
    left = (got[:, 0:16, :] * (1.0 / ITEM_SCALE)).astype(BF16).reshape(-1, LANES)
    right = (got[:, 16:32, :] * (1.0 / ITEM_SCALE)).astype(BF16).reshape(-1, LANES)
    block[:, :LANES] = left
    block[:, LANES:] = right
    gram = whole_gram(got[:, 32 : 32 + piece, :].reshape(-1, LANES) * (1.0 / GRAM_SCALE))
    now = mid[...] - (LR_USER * LAMBDA) * times_gram(users[...], gram)
    mid_out[...] = now
    users_bf[...] = now.astype(BF16)
    grad_users[...] = jnp.zeros_like(grad_users)
    sums[...] = jnp.zeros_like(sums)
    slot_grads(1, users_bf, block, values, rows, cols, count, grad_users, sums)
    raw = sums[:, 0:32, :]
    root = jnp.sqrt(jnp.abs(raw)) * ROOT_SCALE
    sums[:, 0:32, :] = jnp.where(raw < 0.0, -root, root)
    full = jnp.sum(got[:, 32 + piece :, :], axis=0) * (GRAM_SCALE / GRAM_INNER_SCALE / total)
    sums[:, 32:, :] = jnp.broadcast_to(full[None], (chunks, piece, LANES))
    users_out[...] = now - LR_USER * grad_users[...]


def last_items_kernel(total, state, out):
    rows = state.shape[0] // 2
    out[0:rows, :], out[rows:, :] = update(state[0:rows, :], state[rows:, :], widths(total[...]))


def last_users_kernel(got, users, mid, out):
    gram = whole_gram(got[...].reshape(-1, LANES) * (1.0 / GRAM_SCALE))
    out[...] = users[...] - (LR_USER * LAMBDA) * times_gram(mid[...], gram)


def call(kernel, out_shape, specs, *args, scratch=()):
    return pl.pallas_call(
        kernel,
        out_shape=out_shape,
        in_specs=specs,
        out_specs=jax.tree.map(lambda _: pl.BlockSpec(memory_space=VMEM), out_shape),
        scratch_shapes=scratch,
        compiler_params=pltpu.CompilerParams(vmem_limit_bytes=40 * 2**20),
    )(*args)


def exchanged(x, axis):
    return lax.all_to_all(x, axis, 0, 0, tiled=True)


def shards(
    user_factors, item_factors, item_accum, tile_values, tile_rows, tile_cols, tile_count, neg_ids
):
    strata = lax.axis_size("stratum")
    inners = lax.axis_size("inner")
    own, rank = item_factors.shape
    negs = neg_ids.shape[1]
    total = float(strata * inners * negs)
    piece = 3 * LANES // inners
    users_shape = jax.ShapeDtypeStruct(user_factors.shape, F32)
    state_shape = jax.ShapeDtypeStruct((2 * own, rank), F32)
    users_scratch = [pltpu.VMEM(user_factors.shape, BF16), pltpu.VMEM(user_factors.shape, F32)]
    sums_shape = jax.ShapeDtypeStruct((inners, 2 * own + piece, LANES), F32)
    vm = pl.BlockSpec(memory_space=VMEM)
    sm = pl.BlockSpec(memory_space=SMEM)
    onward = [((s + 1) % strata, s) for s in range(strata)]

    held_bf = jnp.broadcast_to(item_factors.astype(BF16)[None], (inners, own, rank))
    block = exchanged(held_bf, "inner").reshape(inners * own, rank)
    sums, mid = call(
        first_kernel,
        (sums_shape, users_shape),
        [vm, vm, vm, vm, sm, sm, sm, sm],
        block, user_factors, item_factors, tile_values, tile_rows, tile_cols, tile_count, neg_ids,
        scratch=users_scratch,
    )
    got = exchanged(sums.astype(F16), "inner").astype(F32)
    state, sent = call(
        item_kernel,
        (state_shape, jax.ShapeDtypeStruct((strata, 2 * own + 8 + piece, LANES), F32)),
        [vm, vm, vm, sm],
        got, item_factors, item_accum, neg_ids,
    )
    met = exchanged(sent.astype(F16), "stratum").astype(F32)
    payload = call(
        functools.partial(gather_kernel, total),
        jax.ShapeDtypeStruct((inners, 2 * own + 2 * piece, LANES), F32),
        [vm],
        met,
    ).astype(F16)
    payload, state = lax.optimization_barrier((payload, state))
    state = lax.ppermute(state, "stratum", onward)
    got = exchanged(payload, "inner").astype(F32)
    sums, users, mid = call(
        functools.partial(second_kernel, total),
        (sums_shape, users_shape, users_shape),
        [vm, vm, vm, vm, sm, sm, sm],
        got, user_factors, mid, tile_values, tile_rows, tile_cols, tile_count,
        scratch=users_scratch + [pltpu.VMEM((inners * own, rank), BF16)],
    )
    got = exchanged(sums.astype(F16), "inner").astype(F32)
    root = got[:, : 2 * own]
    gradient = jnp.sum(root * jnp.abs(root), axis=0) * (ROOT_SCALE**-2)
    state = call(last_items_kernel, state_shape, [vm, vm], gradient, state)
    state = lax.ppermute(state, "stratum", onward)
    users = call(last_users_kernel, users_shape, [vm, vm, vm], got[:, 2 * own :], users, mid)
    return (users, state[:own], state[own:])


def solution(mesh):
    devices = P(("stratum", "inner"), None)
    slots = P(None, ("stratum", "inner"))
    return jax.shard_map(
        shards,
        mesh=mesh,
        in_specs=(
            devices,
            devices,
            devices,
            P(None, ("stratum", "inner"), None, None),
            slots,
            slots,
            slots,
            slots,
        ),
        out_specs=(devices, devices, devices),
        check_vma=False,
    )
```

```python
import functools

import jax
import jax.numpy as jnp
from jax import lax
from jax.experimental import pallas as pl
from jax.experimental.pallas import tpu as pltpu
from jax.sharding import PartitionSpec as P

LR_USER = 0.005
LR_ITEM = 0.05
LAMBDA = 64.0

LANES = 128
NEAR = 4
F32 = jnp.float32
BF16 = jnp.bfloat16
F16 = jnp.float16

GRAD_SCALE = 2.0**-6
GRAD_SUM_SCALE = 2.0**-8
ROOT_SCALE = 2.0**-9
ROOT_SUM_SCALE = 2.0**-10
ITEM_SCALE = 2.0**12
GRAM_SCALE = 2.0**12
GRAM_LOCAL_SCALE = 2.0**10
GRAM_NEAR_SCALE = 2.0**8
GRAM_STRATUM_SCALE = 2.0**5
GRAM_INNER_SCALE = 2.0**6
GRAM_TAIL_SCALE = 2.0**3

VMEM = pltpu.VMEM
SMEM = pltpu.SMEM


def contract(a, b, dims):
    return lax.dot_general(a, b, ((dims[:1], dims[1:]), ((), ())), preferred_element_type=F32)


def halves(x):
    return jnp.concatenate([x[:, :LANES], x[:, LANES:]], axis=0)


def widths(x):
    rows = x.shape[0] // 2
    return jnp.concatenate([x[:rows], x[rows:]], axis=1)


def picked_rows(items, ids_ref, step):
    count = ids_ref.shape[1]
    row = lax.broadcasted_iota(jnp.int32, (8, items.shape[0]), 0)
    col = lax.broadcasted_iota(jnp.int32, (8, items.shape[0]), 1)
    hot = jnp.zeros((8, items.shape[0]), F32)
    for n in range(count):
        hot = jnp.where((row == n) & (col == ids_ref[step, n]), 1.0, hot)
    return contract(hot.astype(BF16), items, (1, 0))


def gram_parts(weighed, rows):
    top = contract(weighed[:, :LANES], rows, (0, 0))
    low = contract(weighed[:, LANES:], rows[:, LANES:], (0, 0))
    return jnp.concatenate([top[:, :LANES], top[:, LANES:], low], axis=0)


def whole_gram(parts):
    a, b, c = parts[:LANES], parts[LANES : 2 * LANES], parts[2 * LANES :]
    return jnp.concatenate(
        [jnp.concatenate([a, b], axis=1), jnp.concatenate([b.T, c], axis=1)], axis=0
    )


def split(x):
    high = x.astype(BF16)
    return high, (x - high.astype(F32)).astype(BF16)


def times_gram(users, gram):
    uh, ul = split(users)
    gh, gl = split(gram)
    return contract(uh, gh, (1, 0)) + (contract(ul, gh, (1, 0)) + contract(uh, gl, (1, 0)))


def slot_grads(step, stride, users_bf, block, values, rows, cols, count, grad_users, sums):
    slots, tile_u, tile_i = values.shape[1:]
    chunk = 16
    fars = tile_i // chunk // NEAR
    live = count[step, 0]
    for k in range(slots):
        row = pl.multiple_of(rows[step, k] * tile_u, tile_u)
        col = cols[step, k]
        user_tile = users_bf[pl.ds(row, tile_u), :]
        item_tile = block[pl.ds(pl.multiple_of(col * tile_i, tile_i), tile_i), :]
        scores = contract(user_tile, item_tile, (1, 1))
        err = jnp.where(k < live, scores - values[step, k].astype(F32), 0.0).astype(BF16)
        grad_users[pl.ds(row, tile_u), :] += contract(err, item_tile, (1, 0))
        part = contract(err, user_tile, (0, 0))
        for near in range(NEAR):
            for far in range(fars):
                at = pl.multiple_of((col * fars + far) * stride, 8)
                rows_of = part[(far * NEAR + near) * chunk :][:chunk]
                sums[near, pl.ds(at, chunk), :] += rows_of[:, :LANES]
                sums[near, pl.ds(at + chunk, chunk), :] += rows_of[:, LANES:]


def first_kernel(block, users, own, values, rows, cols, count, ids, sums, users_out, users_bf, grad_users):
    fars = block.shape[0] // (16 * NEAR)
    stride = sums.shape[1] // fars
    users_bf[...] = users[...].astype(BF16)
    grad_users[...] = jnp.zeros_like(grad_users)
    sums[...] = jnp.zeros_like(sums)
    slot_grads(0, stride, users_bf, block, values, rows, cols, count, grad_users, sums)
    picks = picked_rows(own[...].astype(BF16), ids, 0).astype(BF16)
    parts = (gram_parts(picks, picks) * GRAM_LOCAL_SCALE).reshape(fars, NEAR, -1, LANES)
    for far in range(fars):
        for near in range(NEAR):
            at = far * stride
            sums[near, at : at + 32, :] = sums[near, at : at + 32, :] * GRAD_SCALE
            sums[near, at + 32 : at + stride, :] = parts[far, near]
    users_out[...] = users[...] - LR_USER * grad_users[...]


def update(held, accum, gradient):
    accum = accum + gradient * gradient
    return held - LR_ITEM * gradient / jnp.sqrt(accum), accum


def pick_counts(ids_ref, step):
    row = lax.broadcasted_iota(jnp.int32, (8, LANES), 0)
    lane = lax.broadcasted_iota(jnp.int32, (8, LANES), 1)
    row = jnp.where(lane < LANES // 2, row, row + 8)
    counts = jnp.zeros((8, LANES), F32)
    for n in range(ids_ref.shape[1]):
        counts = counts + jnp.where(row == ids_ref[step, n], 1.0, 0.0)
    return counts


def item_kernel(got, held, accum, ids, state, out):
    rows = held.shape[0]
    piece = got.shape[1] - 2 * rows
    total = jnp.sum(got[...], axis=0)
    gradient = widths(total[0 : 2 * rows] * (1.0 / GRAD_SUM_SCALE))
    new, state[rows:, :] = update(held[...], accum[...], gradient)
    state[0:rows, :] = new
    strata = out.shape[0]
    sent = jnp.concatenate(
        [
            halves(new.astype(BF16).astype(F32)) * ITEM_SCALE,
            pick_counts(ids, 1),
            total[2 * rows :] * (GRAM_STRATUM_SCALE / GRAM_NEAR_SCALE),
        ],
        axis=0,
    )
    out[...] = jnp.broadcast_to(sent[None], (strata, 2 * rows + 8 + piece, LANES))


def gather_kernel(total, met, out):
    chunks = out.shape[0]
    strata = met.shape[0]
    piece = met.shape[1] - 40
    fars = chunks
    after = lax.rem(lax.axis_index("stratum") + 1, strata)
    items = met[pl.ds(after, 1), 0:32, :]
    out[:, 0:32, :] = jnp.broadcast_to(items, (chunks, 32, LANES))
    full = jnp.sum(met[:, 40:, :], axis=0) * (GRAM_SCALE / GRAM_STRATUM_SCALE / total)
    out[:, 32 : 32 + piece, :] = jnp.broadcast_to(full[None], (chunks, piece, LANES))
    counts = jnp.concatenate([met[-1:, 32:40, :], met[:-1, 32:40, :]], axis=0)
    counts = jnp.concatenate([counts[:, :, 0:1], counts[:, :, 64:65]], axis=1)
    rows = [met[:, 0:16, :] * (1.0 / ITEM_SCALE), met[:, 16:32, :] * (1.0 / ITEM_SCALE)]
    weighed = jnp.concatenate([(r * counts).reshape(-1, LANES) for r in rows], axis=1)
    plain = jnp.concatenate([r.reshape(-1, LANES) for r in rows], axis=1).astype(BF16)
    high, low = split(weighed)
    parts = gram_parts(jnp.concatenate([high, low], axis=0), jnp.concatenate([plain, plain], axis=0))
    out[:, 32 + piece :, :] = (parts * GRAM_INNER_SCALE).reshape(fars, NEAR * piece, LANES)


def second_kernel(
    total, got, users, mid, values, rows, cols, count, sums, users_out, mid_out, users_bf, grad_users, block
):
    fars = block.shape[0] // (16 * NEAR)
    piece = sums.shape[1] - 32 * fars
    stride = 32 + piece
    parts = []
    for far in range(fars):
        for near in range(NEAR):
            to = (far * NEAR + near) * 16
            rows_of = got[near, far * stride : (far + 1) * stride, :]
            block[to : to + 16, :LANES] = (rows_of[0:16] * (1.0 / ITEM_SCALE)).astype(BF16)
            block[to : to + 16, LANES:] = (rows_of[16:32] * (1.0 / ITEM_SCALE)).astype(BF16)
            parts.append(rows_of[32:])
    gram = whole_gram(jnp.concatenate(parts, axis=0) * (1.0 / GRAM_SCALE))
    now = mid[...] - (LR_USER * LAMBDA) * times_gram(users[...], gram)
    mid_out[...] = now
    users_bf[...] = now.astype(BF16)
    grad_users[...] = jnp.zeros_like(grad_users)
    sums[...] = jnp.zeros_like(sums)
    slot_grads(1, 32, users_bf, block, values, rows, cols, count, grad_users, sums)
    raw = sums[:, : 32 * fars, :]
    root = jnp.sqrt(jnp.abs(raw)) * ROOT_SCALE
    sums[:, : 32 * fars, :] = jnp.where(raw < 0.0, -root, root)
    full = jnp.sum(got[:, fars * stride :, :], axis=0) * (GRAM_SCALE / GRAM_TAIL_SCALE / total)
    sums[:, 32 * fars :, :] = jnp.broadcast_to(full[None], (NEAR, piece, LANES))
    users_out[...] = now - LR_USER * grad_users[...]


def last_items_kernel(got, state, out):
    rows = state.shape[0] // 2
    root = got[:, : 2 * rows, :]
    gradient = widths(jnp.sum(root * jnp.abs(root), axis=0) * ROOT_SUM_SCALE**-2)
    out[0:rows, :], out[rows:, :] = update(state[0:rows, :], state[rows:, :], gradient)


def last_users_kernel(got, users, mid, out):
    gram = whole_gram(got[:, 32:, :].reshape(-1, LANES) * (1.0 / GRAM_SCALE))
    out[...] = users[...] - (LR_USER * LAMBDA) * times_gram(mid[...], gram)


def call(kernel, out_shape, specs, *args, scratch=()):
    return pl.pallas_call(
        kernel,
        out_shape=out_shape,
        in_specs=specs,
        out_specs=jax.tree.map(lambda _: pl.BlockSpec(memory_space=VMEM), out_shape),
        scratch_shapes=scratch,
        compiler_params=pltpu.CompilerParams(vmem_limit_bytes=40 * 2**20),
    )(*args)


def exchanged(x, axis):
    return lax.all_to_all(x, axis, 0, 0, tiled=True)


def shards(
    user_factors, item_factors, item_accum, tile_values, tile_rows, tile_cols, tile_count, neg_ids
):
    strata = lax.axis_size("stratum")
    fars = lax.axis_size("far")
    inners = fars * NEAR
    own, rank = item_factors.shape
    total = float(strata * inners * neg_ids.shape[1])
    piece = 3 * LANES // inners
    pair = 2 * own
    users_shape = jax.ShapeDtypeStruct(user_factors.shape, F32)
    state_shape = jax.ShapeDtypeStruct((pair, rank), F32)
    users_scratch = [pltpu.VMEM(user_factors.shape, BF16), pltpu.VMEM(user_factors.shape, F32)]
    vm = pl.BlockSpec(memory_space=VMEM)
    sm = pl.BlockSpec(memory_space=SMEM)
    onward = [((s + 1) % strata, s) for s in range(strata)]

    held_bf = jnp.broadcast_to(item_factors.astype(BF16)[None], (inners, own, rank))
    block = exchanged(held_bf, ("far", "near")).reshape(inners * own, rank)
    sums, mid = call(
        first_kernel,
        (jax.ShapeDtypeStruct((NEAR, fars * (pair + piece), LANES), F32), users_shape),
        [vm, vm, vm, vm, sm, sm, sm, sm],
        block, user_factors, item_factors, tile_values, tile_rows, tile_cols, tile_count, neg_ids,
        scratch=users_scratch,
    )
    got = exchanged(sums.astype(F16), "near").astype(F32)
    got = (jnp.sum(got, axis=0) * 0.25).astype(F16).reshape(fars, pair + piece, LANES)
    got = exchanged(got, "far").astype(F32)
    state, sent = call(
        item_kernel,
        (state_shape, jax.ShapeDtypeStruct((strata, pair + 8 + piece, LANES), F32)),
        [vm, vm, vm, sm],
        got, item_factors, item_accum, neg_ids,
    )
    met = exchanged(sent.astype(F16), "stratum").astype(F32)
    payload = call(
        functools.partial(gather_kernel, total),
        jax.ShapeDtypeStruct((fars, pair + piece + NEAR * piece, LANES), F32),
        [vm],
        met,
    ).astype(F16)
    got = exchanged(payload, "far")
    both = got[:, : pair + piece].reshape(1, -1, LANES)
    tail = jnp.sum(got[:, pair + piece :].astype(F32), axis=0) * (GRAM_TAIL_SCALE / GRAM_INNER_SCALE)
    payload = jnp.concatenate(
        [jnp.broadcast_to(both, (NEAR,) + both.shape[1:]), tail.astype(F16).reshape(NEAR, piece, LANES)],
        axis=1,
    )
    payload, state = lax.optimization_barrier((payload, state))
    state = lax.ppermute(state, "stratum", onward)
    got = exchanged(payload, "near").astype(F32)
    sums, users, mid = call(
        functools.partial(second_kernel, total),
        (jax.ShapeDtypeStruct((NEAR, fars * pair + piece, LANES), F32), users_shape, users_shape),
        [vm, vm, vm, vm, sm, sm, sm],
        got, user_factors, mid, tile_values, tile_rows, tile_cols, tile_count,
        scratch=users_scratch + [pltpu.VMEM((inners * own, rank), BF16)],
    )
    got = exchanged(sums.astype(F16), "near")
    root = got[:, : fars * pair].astype(F32)
    square = jnp.sum(root * jnp.abs(root), axis=0)
    root = jnp.sqrt(jnp.abs(square)) * (ROOT_SUM_SCALE / ROOT_SCALE)
    root = jnp.where(square < 0.0, -root, root).astype(F16).reshape(fars, pair, LANES)
    tails = got[:, fars * pair :].reshape(1, NEAR * piece, LANES)
    payload = jnp.concatenate([root, jnp.broadcast_to(tails, (fars,) + tails.shape[1:])], axis=1)
    got = exchanged(payload, "far").astype(F32)
    state = call(last_items_kernel, state_shape, [vm, vm], got, state)
    state = lax.ppermute(state, "stratum", onward)
    users = call(last_users_kernel, users_shape, [vm, vm, vm], got, users, mid)
    return (users, state[:own], state[own:])


def solution(mesh):
    strata, inners = mesh.devices.shape
    fine = jax.sharding.Mesh(
        mesh.devices.reshape(strata, inners // NEAR, NEAR), ("stratum", "far", "near")
    )
    every = ("stratum", "far", "near")
    devices = P(every, None)
    slots = P(None, every)
    return jax.shard_map(
        shards,
        mesh=fine,
        in_specs=(
            devices,
            devices,
            devices,
            P(None, every, None, None),
            slots,
            slots,
            slots,
            slots,
        ),
        out_specs=(devices, devices, devices),
        check_vma=False,
    )
```

```python
import functools

import jax
import jax.numpy as jnp
from jax import lax
from jax.experimental import pallas as pl
from jax.experimental.pallas import tpu as pltpu
from jax.sharding import PartitionSpec as P

LR_USER = 0.005
LR_ITEM = 0.05
LAMBDA = 64.0

LANES = 128
F32 = jnp.float32
BF16 = jnp.bfloat16
F16 = jnp.float16

GRAD_SCALE = 2.0**-6
ROOT_SCALE = 2.0**-9
ITEM_SCALE = 2.0**12
GRAM_SCALE = 2.0**12
GRAM_STRATUM_SCALE = 2.0**5
GRAM_INNER_SCALE = 2.0**6

ROWS = 16
PAIR = 2 * ROWS
PACKED = 2 * LANES + 1

VMEM = pltpu.VMEM
SMEM = pltpu.SMEM


def contract(a, b, dims):
    return lax.dot_general(a, b, ((dims[:1], dims[1:]), ((), ())), preferred_element_type=F32)


def halves(x):
    return jnp.concatenate([x[:, :LANES], x[:, LANES:]], axis=0)


def widths(x):
    rows = x.shape[0] // 2
    return jnp.concatenate([x[:rows], x[rows:]], axis=1)


def piece_rows(chunks):
    return 2 * (-(-PACKED // (2 * chunks)))


def packed_gram(weighed, rows):
    gram = contract(weighed, rows, (0, 0))
    upper, beside, lower = gram[:LANES, :LANES], gram[:LANES, LANES:], gram[LANES:, LANES:]
    row = lax.broadcasted_iota(jnp.int32, (LANES, LANES), 0)
    col = lax.broadcasted_iota(jnp.int32, (LANES, LANES), 1)
    both = jnp.where(col >= row, upper, lower)
    return both, beside, jnp.sum(jnp.where(col == row, lower, 0.0), axis=0, keepdims=True)


def put_packed(packed, weighed, rows, scale):
    both, beside, diagonal = packed_gram(weighed, rows)
    packed[...] = jnp.zeros_like(packed)
    packed[0:LANES, :] = both * scale
    packed[LANES : 2 * LANES, :] = beside * scale
    packed[2 * LANES : 2 * LANES + 1, :] = diagonal * scale


def whole_gram(packed, scale):
    both = packed[0:LANES, :] * scale
    beside = packed[LANES : 2 * LANES, :] * scale
    diagonal = packed[2 * LANES : 2 * LANES + 1, :] * scale
    row = lax.broadcasted_iota(jnp.int32, (LANES, LANES), 0)
    col = lax.broadcasted_iota(jnp.int32, (LANES, LANES), 1)
    above = jnp.where(col > row, both, 0.0)
    below = jnp.where(col < row, both, 0.0)
    upper = above + above.T + jnp.where(col == row, both, 0.0)
    lower = below + below.T + jnp.where(col == row, diagonal, 0.0)
    return jnp.concatenate(
        [jnp.concatenate([upper, beside], axis=1), jnp.concatenate([beside.T, lower], axis=1)], axis=0
    )


def split(x):
    high = x.astype(BF16)
    return high, (x - high.astype(F32)).astype(BF16)


def times_gram(users, gram):
    uh, ul = split(users)
    gh, gl = split(gram)
    return contract(uh, gh, (1, 0)) + (contract(ul, gh, (1, 0)) + contract(uh, gl, (1, 0)))


def pick_row(ids_ref, step):
    row = lax.broadcasted_iota(jnp.int32, (2, LANES), 0)
    lane = lax.broadcasted_iota(jnp.int32, (2, LANES), 1)
    counts = jnp.zeros((2, LANES), F32)
    for n in range(ids_ref.shape[1]):
        counts = counts + jnp.where((lane == ids_ref[step, n]) & (row == 0), 1.0, 0.0)
    return counts


def start_kernel(held, ids, out):
    stride = PAIR + 2
    rows = halves(held[...].astype(BF16))
    counts = pick_row(ids, 0).astype(BF16)
    for chunk in range(out.shape[0] // stride):
        at = chunk * stride
        out[at : at + PAIR, :] = rows
        out[at + PAIR : at + stride, :] = counts


def item_grads(step, users_bf, block, values, rows, cols, count, errors, scale, add):
    slots, tile_u, tile_i = values.shape[1:]
    live = count[step, 0]
    for k in range(slots):
        row = pl.multiple_of(rows[step, k] * tile_u, tile_u)
        col = cols[step, k]
        user_tile = users_bf[pl.ds(row, tile_u), :]
        item_tile = block[pl.ds(pl.multiple_of(col * tile_i, tile_i), tile_i), :]
        scores = contract(user_tile, item_tile, (1, 1))
        err = jnp.where(k < live, scores - values[step, k].astype(F32), 0.0).astype(BF16)
        errors[k] = err
        if scale is not None:
            err = err * jnp.asarray(scale, BF16)
        add(col, contract(err, user_tile, (0, 0)))


def user_grads(step, block, rows, cols, errors, grad_users):
    slots, tile_u, tile_i = errors.shape
    grad_users[...] = jnp.zeros_like(grad_users)
    for k in range(slots):
        row = pl.multiple_of(rows[step, k] * tile_u, tile_u)
        col = pl.multiple_of(cols[step, k] * tile_i, tile_i)
        grad_users[pl.ds(row, tile_u), :] += contract(errors[k], block[pl.ds(col, tile_i), :], (1, 0))


def first_kernel(got, users, values, rows, cols, count, sums, block, errors, users_bf):
    stride = PAIR + 2
    for chunk in range(block.shape[0] // ROWS):
        to, at = chunk * ROWS, chunk * stride
        block[to : to + ROWS, :LANES] = got[at : at + ROWS, :]
        block[to : to + ROWS, LANES:] = got[at + ROWS : at + PAIR, :]
    users_bf[...] = users[...].astype(BF16)
    sums[...] = jnp.zeros_like(sums)

    def add(col, part):
        chunks = part.shape[0] // ROWS
        at = pl.ds(col * chunks, chunks)
        sums[at, 0:ROWS, :] += part[:, :LANES].reshape(chunks, ROWS, LANES)
        sums[at, ROWS:PAIR, :] += part[:, LANES:].reshape(chunks, ROWS, LANES)

    item_grads(0, users_bf, block, values, rows, cols, count, errors, GRAD_SCALE, add)


def first_users_kernel(got, block, users, rows, cols, errors, users_out, piece_out, counts, packed, pieces, grad_users):
    stride = PAIR + 2
    chunks = block.shape[0] // ROWS
    user_grads(0, block, rows, cols, errors, grad_users)
    users_out[...] = users[...] - LR_USER * grad_users[...]
    for chunk in range(chunks):
        at = chunk * stride + PAIR
        counts[chunk : chunk + 1, :] = got[at : at + 2, :].astype(F32)[0:1]
    shape = (chunks, ROWS, LANES)
    own = lax.broadcasted_iota(jnp.int32, shape, 1) == lax.broadcasted_iota(jnp.int32, shape, 2)
    weight = jnp.sum(jnp.where(own, counts[...][:, None, :], 0.0), axis=2, keepdims=True)
    plain = block[...]
    left = (plain[:, :LANES].astype(F32).reshape(shape) * weight).reshape(-1, LANES)
    right = (plain[:, LANES:].astype(F32).reshape(shape) * weight).reshape(-1, LANES)
    high, low = split(jnp.concatenate([left, right], axis=1))
    put_packed(
        packed,
        jnp.concatenate([high, low], axis=0),
        jnp.concatenate([plain, plain], axis=0),
        GRAM_STRATUM_SCALE,
    )
    piece = packed.shape[0] // chunks
    for chunk in range(chunks):
        pieces[chunk, 0:piece, :] = packed[chunk * piece : (chunk + 1) * piece, :]
    piece_out[...] = pieces[lax.axis_index("inner")]


def update(held, accum, gradient):
    accum = accum + gradient * gradient
    return held - LR_ITEM * gradient / jnp.sqrt(accum), accum


def pick_counts(ids_ref, step):
    row = lax.broadcasted_iota(jnp.int32, (8, LANES), 0)
    lane = lax.broadcasted_iota(jnp.int32, (8, LANES), 1)
    row = jnp.where(lane < LANES // 2, row, row + 8)
    counts = jnp.zeros((8, LANES), F32)
    for n in range(ids_ref.shape[1]):
        counts = counts + jnp.where(row == ids_ref[step, n], 1.0, 0.0)
    return counts


def item_kernel(got, held, accum, gram_piece, ids, state, out):
    strata = out.shape[0]
    gradient = widths(jnp.sum(got[...], axis=0) * (1.0 / GRAD_SCALE))
    new, state[ROWS:, :] = update(held[...], accum[...], gradient)
    state[0:ROWS, :] = new
    items = halves(new.astype(BF16).astype(F32)) * ITEM_SCALE
    sent = jnp.concatenate([items, pick_counts(ids, 1), gram_piece[...]], axis=0)
    out[...] = jnp.broadcast_to(sent[None], (strata,) + sent.shape)


def gather_kernel(total, met, out, packed):
    strata = met.shape[0]
    chunks = lax.axis_size("inner")
    piece = packed.shape[0] // chunks
    stride = PAIR + 2 * piece
    after = lax.rem(lax.axis_index("stratum") + 1, strata)
    items = met[pl.ds(after, 1), 0:PAIR, :][0]
    full = jnp.sum(met[:, 40:, :], axis=0)[0:piece] * (GRAM_SCALE / GRAM_STRATUM_SCALE / total)
    counts = jnp.concatenate([met[-1:, 32:40, :], met[:-1, 32:40, :]], axis=0)
    counts = jnp.concatenate([counts[:, :, 0:1], counts[:, :, 64:65]], axis=1)
    rows = [met[:, 0:ROWS, :] * (1.0 / ITEM_SCALE), met[:, ROWS:PAIR, :] * (1.0 / ITEM_SCALE)]
    weighed = jnp.concatenate([(r * counts).reshape(-1, LANES) for r in rows], axis=1)
    plain = jnp.concatenate([r.reshape(-1, LANES) for r in rows], axis=1).astype(BF16)
    high, low = split(weighed)
    put_packed(
        packed,
        jnp.concatenate([high, low], axis=0),
        jnp.concatenate([plain, plain], axis=0),
        GRAM_INNER_SCALE,
    )
    for chunk in range(chunks):
        at = chunk * stride
        out[at : at + PAIR, :] = items
        out[at + PAIR : at + PAIR + piece, :] = full
        out[at + PAIR + piece : at + stride, :] = packed[chunk * piece : (chunk + 1) * piece, :]


def second_kernel(
    total, got, users, mid, values, rows, cols, count, sums, mid_out, block, errors, packed, users_bf, grads
):
    chunks = block.shape[0] // ROWS
    piece = packed.shape[0] // chunks
    stride = PAIR + 2 * piece
    full = jnp.zeros((piece, LANES), F32)
    for chunk in range(chunks):
        to, at = chunk * ROWS, chunk * stride
        block[to : to + ROWS, :LANES] = (got[at : at + ROWS, :] * (1.0 / ITEM_SCALE)).astype(BF16)
        block[to : to + ROWS, LANES:] = (got[at + ROWS : at + PAIR, :] * (1.0 / ITEM_SCALE)).astype(BF16)
        packed[chunk * piece : (chunk + 1) * piece, :] = got[at + PAIR : at + PAIR + piece, :]
        full = full + got[at + PAIR + piece : at + stride, :]
    gram = whole_gram(packed, 1.0 / GRAM_SCALE)
    now = mid[...] - (LR_USER * LAMBDA) * times_gram(users[...], gram)
    mid_out[...] = now
    users_bf[...] = now.astype(BF16)
    grads[...] = jnp.zeros_like(grads)

    def add(col, part):
        at = pl.multiple_of(col * part.shape[0], part.shape[0])
        grads[pl.ds(at, part.shape[0]), :] += part

    item_grads(1, users_bf, block, values, rows, cols, count, errors, None, add)
    full = full * (GRAM_SCALE / GRAM_INNER_SCALE / total)
    for chunk in range(chunks):
        at = chunk * (PAIR + piece)
        raw = halves(grads[chunk * ROWS : (chunk + 1) * ROWS, :])
        root = jnp.sqrt(jnp.abs(raw)) * ROOT_SCALE
        sums[at : at + PAIR, :] = jnp.where(raw < 0.0, -root, root)
        sums[at + PAIR : at + PAIR + piece, :] = full


def second_users_kernel(block, now, rows, cols, errors, users_out, grad_users):
    user_grads(1, block, rows, cols, errors, grad_users)
    users_out[...] = now[...] - LR_USER * grad_users[...]


def last_items_kernel(chunks, got, state, out):
    stride = got.shape[0] // chunks
    total = jnp.zeros((PAIR, LANES), F32)
    for chunk in range(chunks):
        root = got[chunk * stride : chunk * stride + PAIR, :]
        total = total + root * jnp.abs(root)
    out[0:ROWS, :], out[ROWS:, :] = update(
        state[0:ROWS, :], state[ROWS:, :], widths(total * ROOT_SCALE**-2)
    )


def last_users_kernel(chunks, got, users, mid, out, packed):
    stride = got.shape[0] // chunks
    piece = stride - PAIR
    for chunk in range(chunks):
        packed[chunk * piece : (chunk + 1) * piece, :] = got[chunk * stride + PAIR : (chunk + 1) * stride, :]
    gram = whole_gram(packed, 1.0 / GRAM_SCALE)
    out[...] = users[...] - (LR_USER * LAMBDA) * times_gram(mid[...], gram)


def call(kernel, out_shape, specs, *args, scratch=()):
    return pl.pallas_call(
        kernel,
        out_shape=out_shape,
        in_specs=specs,
        out_specs=jax.tree.map(lambda _: pl.BlockSpec(memory_space=VMEM), out_shape),
        scratch_shapes=scratch,
        compiler_params=pltpu.CompilerParams(vmem_limit_bytes=40 * 2**20),
    )(*args)


def exchanged(x, axis):
    return lax.all_to_all(x, axis, 0, 0, tiled=True)


def chunks_exchanged(flat, chunks):
    paired = flat.reshape(chunks, -1, 2, LANES)
    return exchanged(paired, "inner").reshape(flat.shape)


def shards(
    user_factors, item_factors, item_accum, tile_values, tile_rows, tile_cols, tile_count, neg_ids
):
    strata = lax.axis_size("stratum")
    inners = lax.axis_size("inner")
    rank = item_factors.shape[1]
    total = float(strata * inners * neg_ids.shape[1])
    piece = piece_rows(inners)
    padded = -(-piece // 8) * 8
    onward = [((s + 1) % strata, s) for s in range(strata)]
    vm = pl.BlockSpec(memory_space=VMEM)
    sm = pl.BlockSpec(memory_space=SMEM)
    shape = jax.ShapeDtypeStruct
    users_shape = shape(user_factors.shape, F32)
    users_f32 = pltpu.VMEM(user_factors.shape, F32)
    users_bf = pltpu.VMEM(user_factors.shape, BF16)
    state_shape = shape((PAIR, rank), F32)
    block_shape = shape((inners * ROWS, rank), BF16)
    errors_shape = shape(tile_values.shape[1:], BF16)
    packed = pltpu.VMEM((inners * piece, LANES), F32)

    sent = call(start_kernel, shape((inners * (PAIR + 2), LANES), BF16), [vm, sm], item_factors, neg_ids)
    got = chunks_exchanged(sent, inners)
    sums, block, errors = call(
        first_kernel,
        (shape((inners, PAIR, LANES), F32), block_shape, errors_shape),
        [vm, vm, vm, sm, sm, sm],
        got, user_factors, tile_values, tile_rows, tile_cols, tile_count,
        scratch=[users_bf],
    )
    sums = exchanged(sums.astype(F16), "inner").astype(F32)
    mid, gram_piece = call(
        first_users_kernel,
        (users_shape, shape((padded, LANES), F32)),
        [vm, vm, vm, sm, sm, vm],
        got, block, user_factors, tile_rows, tile_cols, errors,
        scratch=[
            pltpu.VMEM((inners, LANES), F32),
            packed,
            pltpu.VMEM((inners, padded, LANES), F32),
            users_f32,
        ],
    )
    state, sent = call(
        item_kernel,
        (state_shape, shape((strata, PAIR + 8 + padded, LANES), F32)),
        [vm, vm, vm, vm, sm],
        sums, item_factors, item_accum, gram_piece, neg_ids,
    )
    met = exchanged(sent.astype(F16), "stratum").astype(F32)
    sent = call(
        functools.partial(gather_kernel, total),
        shape((inners * (PAIR + 2 * piece), LANES), F32),
        [vm],
        met,
        scratch=[packed],
    ).astype(F16)
    got = chunks_exchanged(sent, inners).astype(F32)
    sums, mid, block, errors = call(
        functools.partial(second_kernel, total),
        (shape((inners * (PAIR + piece), LANES), F32), users_shape, block_shape, errors_shape),
        [vm, vm, vm, vm, sm, sm, sm],
        got, user_factors, mid, tile_values, tile_rows, tile_cols, tile_count,
        scratch=[packed, users_bf, pltpu.VMEM(block_shape.shape, F32)],
    )
    sums, state = lax.optimization_barrier((sums.astype(F16), state))
    state = lax.ppermute(state, "stratum", onward)
    got = chunks_exchanged(sums, inners).astype(F32)
    users = call(
        second_users_kernel, users_shape, [vm, vm, sm, sm, vm],
        block, mid, tile_rows, tile_cols, errors, scratch=[users_f32],
    )
    state = call(functools.partial(last_items_kernel, inners), state_shape, [vm, vm], got, state)
    state = lax.ppermute(state, "stratum", onward)
    users = call(
        functools.partial(last_users_kernel, inners), users_shape, [vm, vm, vm],
        got, users, mid, scratch=[packed],
    )
    return (users, state[:ROWS], state[ROWS:])


def solution(mesh):
    devices = P(("stratum", "inner"), None)
    slots = P(None, ("stratum", "inner"))
    return jax.shard_map(
        shards,
        mesh=mesh,
        in_specs=(
            devices,
            devices,
            devices,
            P(None, ("stratum", "inner"), None, None),
            slots,
            slots,
            slots,
            slots,
        ),
        out_specs=(devices, devices, devices),
        check_vma=False,
    )
```

```python
import functools

import jax
import jax.numpy as jnp
from jax import lax
from jax.experimental import pallas as pl
from jax.experimental.pallas import tpu as pltpu
from jax.sharding import PartitionSpec as P

LR_USER = 0.005
LR_ITEM = 0.05
LAMBDA = 64.0

LANES = 128
F32 = jnp.float32
BF16 = jnp.bfloat16
F16 = jnp.float16

GRAD_SCALE = 2.0**-7
ROOT_SCALE = 2.0**-9
ITEM_SCALE = 2.0**12
GRAM_SCALE = 2.0**12
GRAM_STRATUM_SCALE = 2.0**5
GRAM_INNER_SCALE = 2.0**6

ROWS = 16
PAIR = 2 * ROWS
PACKED = 2 * LANES + 1

GROUP = ("far", "near")
INNER = ("far", "near", "pair")

VMEM = pltpu.VMEM
SMEM = pltpu.SMEM


def contract(a, b, dims):
    return lax.dot_general(a, b, ((dims[:1], dims[1:]), ((), ())), preferred_element_type=F32)


def halves(x):
    return jnp.concatenate([x[:, :LANES], x[:, LANES:]], axis=0)


def widths(x):
    rows = x.shape[0] // 2
    return jnp.concatenate([x[:rows], x[rows:]], axis=1)


def piece_rows(chunks):
    return 2 * (-(-PACKED // (2 * chunks)))


def packed_gram(weighed, rows):
    gram = contract(weighed, rows, (0, 0))
    upper, beside, lower = gram[:LANES, :LANES], gram[:LANES, LANES:], gram[LANES:, LANES:]
    row = lax.broadcasted_iota(jnp.int32, (LANES, LANES), 0)
    col = lax.broadcasted_iota(jnp.int32, (LANES, LANES), 1)
    both = jnp.where(col >= row, upper, lower)
    return both, beside, jnp.sum(jnp.where(col == row, lower, 0.0), axis=0, keepdims=True)


def put_packed(packed, weighed, rows, scale):
    both, beside, diagonal = packed_gram(weighed, rows)
    packed[...] = jnp.zeros_like(packed)
    packed[0:LANES, :] = both * scale
    packed[LANES : 2 * LANES, :] = beside * scale
    packed[2 * LANES : 2 * LANES + 1, :] = diagonal * scale


def whole_gram(packed, scale):
    both = packed[0:LANES, :] * scale
    beside = packed[LANES : 2 * LANES, :] * scale
    diagonal = packed[2 * LANES : 2 * LANES + 1, :] * scale
    row = lax.broadcasted_iota(jnp.int32, (LANES, LANES), 0)
    col = lax.broadcasted_iota(jnp.int32, (LANES, LANES), 1)
    above = jnp.where(col > row, both, 0.0)
    below = jnp.where(col < row, both, 0.0)
    upper = above + above.T + jnp.where(col == row, both, 0.0)
    lower = below + below.T + jnp.where(col == row, diagonal, 0.0)
    return jnp.concatenate(
        [jnp.concatenate([upper, beside], axis=1), jnp.concatenate([beside.T, lower], axis=1)], axis=0
    )


def split(x):
    high = x.astype(BF16)
    return high, (x - high.astype(F32)).astype(BF16)


def times_gram(users, gram):
    uh, ul = split(users)
    gh, gl = split(gram)
    return contract(uh, gh, (1, 0)) + (contract(ul, gh, (1, 0)) + contract(uh, gl, (1, 0)))


def pick_row(ids_ref, step):
    row = lax.broadcasted_iota(jnp.int32, (2, LANES), 0)
    lane = lax.broadcasted_iota(jnp.int32, (2, LANES), 1)
    counts = jnp.zeros((2, LANES), F32)
    for n in range(ids_ref.shape[1]):
        counts = counts + jnp.where((lane == ids_ref[step, n]) & (row == 0), 1.0, 0.0)
    return counts


def start_kernel(held, ids, out):
    stride = PAIR + 2
    rows = halves(held[...].astype(BF16))
    counts = pick_row(ids, 0).astype(BF16)
    for chunk in range(out.shape[0] // stride):
        at = chunk * stride
        out[at : at + PAIR, :] = rows
        out[at + PAIR : at + stride, :] = counts


def item_grads(users_bf, block, values, rows, cols, live, errors, owned, scale, add):
    slots, tile_u, tile_i = errors.shape
    for k in range(slots):
        row = pl.multiple_of(rows(k) * tile_u, tile_u)
        col = cols(k)
        user_tile = users_bf[pl.ds(row, tile_u), :]
        item_tile = block[pl.ds(pl.multiple_of(col * tile_i, tile_i), tile_i), :]
        scores = contract(user_tile, item_tile, (1, 1))
        there = k < live if owned is None else owned & (k < live)
        err = jnp.where(there, scores - values(k).astype(F32), 0.0).astype(BF16)
        errors[k] = err
        if scale is not None:
            err = err * jnp.asarray(scale, BF16)
        add(col, contract(err, user_tile, (0, 0)))


def user_grads(block, rows, cols, errors, grad_users):
    slots, tile_u, tile_i = errors.shape
    grad_users[...] = jnp.zeros_like(grad_users)
    for k in range(slots):
        row = pl.multiple_of(rows(k) * tile_u, tile_u)
        col = pl.multiple_of(cols(k) * tile_i, tile_i)
        grad_users[pl.ds(row, tile_u), :] += contract(errors[k], block[pl.ds(col, tile_i), :], (1, 0))


def at_step(ref, step):
    return lambda k: ref[step, k]


def from_list(ref, first):
    return lambda k: ref[first + k]


def pair_rows(chunk, side):
    return pl.ds(pl.multiple_of(chunk * 2 * ROWS + side * ROWS, ROWS), ROWS)


def first_kernel(
    got, users, their_users, values, their_values, rows, cols, count, theirs,
    sums, block, errors, their_errors, users_bf, grads,
):
    stride = PAIR + 2
    chunks = got.shape[0] // stride
    side = lax.axis_index("pair")
    slots, tile_u, tile_i = errors.shape
    block[...] = jnp.zeros_like(block)
    for chunk in range(chunks):
        at = chunk * stride
        block[pair_rows(chunk, side), :LANES] = got[at : at + ROWS, :]
        block[pair_rows(chunk, side), LANES:] = got[at + ROWS : at + PAIR, :]
    users_bf[...] = users[...].astype(BF16)
    grads[...] = jnp.zeros_like(grads)
    lane = lax.broadcasted_iota(jnp.int32, (tile_u, tile_i), 1)
    owned = lax.rem(lax.div(lane, ROWS), 2) == side

    def add(col, part):
        at = pl.multiple_of(col * part.shape[0], part.shape[0])
        grads[pl.ds(at, part.shape[0]), :] += part

    item_grads(
        users_bf, block, lambda k: values[0, k], at_step(rows, 0), at_step(cols, 0), count[0, 0],
        errors, owned, GRAD_SCALE, add,
    )
    item_grads(
        their_users, block, lambda k: their_values[k], from_list(theirs, 0), from_list(theirs, slots),
        theirs[2 * slots], their_errors, owned, GRAD_SCALE, add,
    )
    for chunk in range(chunks):
        sums[chunk] = halves(grads[pair_rows(chunk, side), :])


def first_users_kernel(
    got, block, users, rows, cols, errors, theirs, their_errors,
    users_out, their_grads, piece_out, their_piece, counts, packed, pieces, mine, grad_users,
):
    stride = PAIR + 2
    chunks = got.shape[0] // stride
    side = lax.axis_index("pair")
    for chunk in range(chunks):
        at = chunk * stride + PAIR
        counts[chunk : chunk + 1, :] = got[at : at + 2, :].astype(F32)[0:1]
        mine[chunk * ROWS : (chunk + 1) * ROWS, :] = block[pair_rows(chunk, side), :]
    shape = (chunks, ROWS, LANES)
    own = lax.broadcasted_iota(jnp.int32, shape, 1) == lax.broadcasted_iota(jnp.int32, shape, 2)
    weight = jnp.sum(jnp.where(own, counts[...][:, None, :], 0.0), axis=2, keepdims=True)
    plain = mine[...]
    left = (plain[:, :LANES].astype(F32).reshape(shape) * weight).reshape(-1, LANES)
    right = (plain[:, LANES:].astype(F32).reshape(shape) * weight).reshape(-1, LANES)
    high, low = split(jnp.concatenate([left, right], axis=1))
    put_packed(
        packed,
        jnp.concatenate([high, low], axis=0),
        jnp.concatenate([plain, plain], axis=0),
        GRAM_STRATUM_SCALE,
    )
    devices = pieces.shape[0]
    piece = packed.shape[0] // devices
    for device in range(devices):
        pieces[device, 0:piece, :] = packed[device * piece : (device + 1) * piece, :]
    me = lax.axis_index(INNER)
    piece_out[...] = pieces[me]
    their_piece[...] = pieces[me + 1 - 2 * side]
    slots = errors.shape[0]
    user_grads(block, from_list(theirs, 0), from_list(theirs, slots), their_errors, their_grads)
    user_grads(block, at_step(rows, 0), at_step(cols, 0), errors, grad_users)
    users_out[...] = users[...] - LR_USER * grad_users[...]


def update(held, accum, gradient):
    accum = accum + gradient * gradient
    return held - LR_ITEM * gradient / jnp.sqrt(accum), accum


def pick_counts(ids_ref, step):
    row = lax.broadcasted_iota(jnp.int32, (8, LANES), 0)
    lane = lax.broadcasted_iota(jnp.int32, (8, LANES), 1)
    row = jnp.where(lane < LANES // 2, row, row + 8)
    counts = jnp.zeros((8, LANES), F32)
    for n in range(ids_ref.shape[1]):
        counts = counts + jnp.where(row == ids_ref[step, n], 1.0, 0.0)
    return counts


def item_kernel(got, held, accum, gram_piece, their_piece, ids, state, out):
    strata = out.shape[0]
    gradient = widths(jnp.sum(got[...], axis=0) * (1.0 / GRAD_SCALE))
    new, state[ROWS:, :] = update(held[...], accum[...], gradient)
    state[0:ROWS, :] = new
    items = halves(new.astype(BF16).astype(F32)) * ITEM_SCALE
    sent = jnp.concatenate([items, pick_counts(ids, 1), gram_piece[...] + their_piece[...]], axis=0)
    out[...] = jnp.broadcast_to(sent[None], (strata,) + sent.shape)


def gather_kernel(total, met, out, packed):
    strata = met.shape[0]
    chunks = lax.axis_size(INNER)
    piece = packed.shape[0] // chunks
    stride = PAIR + 2 * piece
    after = lax.rem(lax.axis_index("stratum") + 1, strata)
    items = met[pl.ds(after, 1), 0:PAIR, :][0]
    full = jnp.sum(met[:, 40:, :], axis=0)[0:piece] * (GRAM_SCALE / GRAM_STRATUM_SCALE / total)
    counts = jnp.concatenate([met[-1:, 32:40, :], met[:-1, 32:40, :]], axis=0)
    counts = jnp.concatenate([counts[:, :, 0:1], counts[:, :, 64:65]], axis=1)
    rows = [met[:, 0:ROWS, :] * (1.0 / ITEM_SCALE), met[:, ROWS:PAIR, :] * (1.0 / ITEM_SCALE)]
    weighed = jnp.concatenate([(r * counts).reshape(-1, LANES) for r in rows], axis=1)
    plain = jnp.concatenate([r.reshape(-1, LANES) for r in rows], axis=1).astype(BF16)
    high, low = split(weighed)
    put_packed(
        packed,
        jnp.concatenate([high, low], axis=0),
        jnp.concatenate([plain, plain], axis=0),
        GRAM_INNER_SCALE,
    )
    for chunk in range(chunks):
        at = chunk * stride
        out[at : at + PAIR, :] = items
        out[at + PAIR : at + PAIR + piece, :] = full
        out[at + PAIR + piece : at + stride, :] = packed[chunk * piece : (chunk + 1) * piece, :]


def second_kernel(
    total, got, users, mid, rest, values, rows, cols, count, sums, mid_out, block, errors, packed, users_bf, grads
):
    chunks = block.shape[0] // ROWS
    piece = packed.shape[0] // chunks
    stride = PAIR + 2 * piece
    full = jnp.zeros((piece, LANES), F32)
    for chunk in range(chunks):
        to, at = chunk * ROWS, chunk * stride
        block[to : to + ROWS, :LANES] = (got[at : at + ROWS, :] * (1.0 / ITEM_SCALE)).astype(BF16)
        block[to : to + ROWS, LANES:] = (got[at + ROWS : at + PAIR, :] * (1.0 / ITEM_SCALE)).astype(BF16)
        packed[chunk * piece : (chunk + 1) * piece, :] = got[at + PAIR : at + PAIR + piece, :]
        full = full + got[at + PAIR + piece : at + stride, :]
    gram = whole_gram(packed, 1.0 / GRAM_SCALE)
    part = mid[...] - LR_USER * rest[...]
    now = part - (LR_USER * LAMBDA) * times_gram(users[...], gram)
    mid_out[...] = now
    users_bf[...] = now.astype(BF16)
    grads[...] = jnp.zeros_like(grads)

    def add(col, part):
        at = pl.multiple_of(col * part.shape[0], part.shape[0])
        grads[pl.ds(at, part.shape[0]), :] += part

    item_grads(
        users_bf, block, lambda k: values[1, k], at_step(rows, 1), at_step(cols, 1), count[1, 0],
        errors, None, None, add,
    )
    full = full * (GRAM_SCALE / GRAM_INNER_SCALE / total)
    for chunk in range(chunks):
        at = chunk * (PAIR + piece)
        raw = halves(grads[chunk * ROWS : (chunk + 1) * ROWS, :])
        root = jnp.sqrt(jnp.abs(raw)) * ROOT_SCALE
        sums[at : at + PAIR, :] = jnp.where(raw < 0.0, -root, root)
        sums[at + PAIR : at + PAIR + piece, :] = full


def second_users_kernel(block, now, rows, cols, errors, users_out, grad_users):
    user_grads(block, at_step(rows, 1), at_step(cols, 1), errors, grad_users)
    users_out[...] = now[...] - LR_USER * grad_users[...]


def last_items_kernel(chunks, got, state, out):
    stride = got.shape[0] // chunks
    total = jnp.zeros((PAIR, LANES), F32)
    for chunk in range(chunks):
        root = got[chunk * stride : chunk * stride + PAIR, :]
        total = total + root * jnp.abs(root)
    out[0:ROWS, :], out[ROWS:, :] = update(
        state[0:ROWS, :], state[ROWS:, :], widths(total * ROOT_SCALE**-2)
    )


def last_users_kernel(chunks, got, users, mid, out, packed):
    stride = got.shape[0] // chunks
    piece = stride - PAIR
    for chunk in range(chunks):
        packed[chunk * piece : (chunk + 1) * piece, :] = got[chunk * stride + PAIR : (chunk + 1) * stride, :]
    gram = whole_gram(packed, 1.0 / GRAM_SCALE)
    out[...] = users[...] - (LR_USER * LAMBDA) * times_gram(mid[...], gram)


def call(kernel, out_shape, specs, *args, scratch=()):
    return pl.pallas_call(
        kernel,
        out_shape=out_shape,
        in_specs=specs,
        out_specs=jax.tree.map(lambda _: pl.BlockSpec(memory_space=VMEM), out_shape),
        scratch_shapes=scratch,
        compiler_params=pltpu.CompilerParams(vmem_limit_bytes=44 * 2**20),
    )(*args)


def exchanged(x, axis):
    return lax.all_to_all(x, axis, 0, 0, tiled=True)


def chunks_exchanged(flat, axis):
    paired = flat.reshape(lax.axis_size(axis), -1, 2, LANES)
    return exchanged(paired, axis).reshape(flat.shape)


def swapped(x):
    return lax.ppermute(x, "pair", [(0, 1), (1, 0)])


def shards(
    user_factors, item_factors, item_accum, tile_values, tile_rows, tile_cols, tile_count, neg_ids
):
    strata = lax.axis_size("stratum")
    inners = lax.axis_size(INNER)
    group = lax.axis_size(GROUP)
    rank = item_factors.shape[1]
    total = float(strata * inners * neg_ids.shape[1])
    piece = piece_rows(inners)
    padded = -(-piece // 8) * 8
    onward = [((s + 1) % strata, s) for s in range(strata)]
    vm = pl.BlockSpec(memory_space=VMEM)
    sm = pl.BlockSpec(memory_space=SMEM)
    shape = jax.ShapeDtypeStruct
    users_shape = shape(user_factors.shape, F32)
    users_f32 = pltpu.VMEM(user_factors.shape, F32)
    users_bf = pltpu.VMEM(user_factors.shape, BF16)
    state_shape = shape((PAIR, rank), F32)
    block_shape = shape((inners * ROWS, rank), BF16)
    errors_shape = shape(tile_values.shape[1:], BF16)
    piece_shape = shape((padded, LANES), F32)
    packed = pltpu.VMEM((inners * piece, LANES), F32)

    sent = call(start_kernel, shape((group * (PAIR + 2), LANES), BF16), [vm, sm], item_factors, neg_ids)
    lists = jnp.concatenate([tile_rows[0], tile_cols[0], tile_count[0]])
    sent, near_users, near_values, lists = lax.optimization_barrier(
        (sent, user_factors.astype(BF16), tile_values[0], lists)
    )
    got = chunks_exchanged(sent, GROUP)
    theirs = swapped(lists)
    their_users = swapped(near_users)
    their_values = swapped(near_values)
    sums, block, errors, their_errors = call(
        first_kernel,
        (shape((group, PAIR, LANES), F32), block_shape, errors_shape, errors_shape),
        [vm, vm, vm, vm, vm, sm, sm, sm, sm],
        got, user_factors, their_users, tile_values, their_values, tile_rows, tile_cols, tile_count, theirs,
        scratch=[users_bf, pltpu.VMEM(block_shape.shape, F32)],
    )
    sums = exchanged(sums.astype(F16), GROUP).astype(F32)
    mid, rest, gram_piece, their_piece = call(
        first_users_kernel,
        (users_shape, users_shape, piece_shape, piece_shape),
        [vm, vm, vm, sm, sm, vm, sm, vm],
        got, block, user_factors, tile_rows, tile_cols, errors, theirs, their_errors,
        scratch=[
            pltpu.VMEM((group, LANES), F32),
            packed,
            pltpu.VMEM((inners, padded, LANES), F32),
            pltpu.VMEM((group * ROWS, rank), BF16),
            users_f32,
        ],
    )
    their_piece = swapped(their_piece)
    rest = swapped(rest)
    state, sent = call(
        item_kernel,
        (state_shape, shape((strata, PAIR + 8 + padded, LANES), F32)),
        [vm, vm, vm, vm, vm, sm],
        sums, item_factors, item_accum, gram_piece, their_piece, neg_ids,
    )
    met = exchanged(sent.astype(F16), "stratum").astype(F32)
    sent = call(
        functools.partial(gather_kernel, total),
        shape((inners * (PAIR + 2 * piece), LANES), F32),
        [vm],
        met,
        scratch=[packed],
    ).astype(F16)
    got = chunks_exchanged(sent, INNER).astype(F32)
    sums, mid, block, errors = call(
        functools.partial(second_kernel, total),
        (shape((inners * (PAIR + piece), LANES), F32), users_shape, block_shape, errors_shape),
        [vm, vm, vm, vm, vm, sm, sm, sm],
        got, user_factors, mid, rest, tile_values, tile_rows, tile_cols, tile_count,
        scratch=[packed, users_bf, pltpu.VMEM(block_shape.shape, F32)],
    )
    sums, state = lax.optimization_barrier((sums.astype(F16), state))
    state = lax.ppermute(state, "stratum", onward)
    got = chunks_exchanged(sums, INNER).astype(F32)
    users = call(
        second_users_kernel, users_shape, [vm, vm, sm, sm, vm],
        block, mid, tile_rows, tile_cols, errors, scratch=[users_f32],
    )
    state = call(functools.partial(last_items_kernel, inners), state_shape, [vm, vm], got, state)
    state = lax.ppermute(state, "stratum", onward)
    users = call(
        functools.partial(last_users_kernel, inners), users_shape, [vm, vm, vm],
        got, users, mid, scratch=[packed],
    )
    return (users, state[:ROWS], state[ROWS:])


def solution(mesh):
    strata, inners = mesh.devices.shape
    fine = jax.sharding.Mesh(
        mesh.devices.reshape(strata, inners // 4, 2, 2), ("stratum",) + INNER
    )
    every = ("stratum",) + INNER
    devices = P(every, None)
    slots = P(None, every)
    return jax.shard_map(
        shards,
        mesh=fine,
        in_specs=(
            devices,
            devices,
            devices,
            P(None, every, None, None),
            slots,
            slots,
            slots,
            slots,
        ),
        out_specs=(devices, devices, devices),
        check_vma=False,
    )
```

```python
import functools

import jax
import jax.numpy as jnp
from jax import lax
from jax.experimental import pallas as pl
from jax.experimental.pallas import tpu as pltpu
from jax.sharding import PartitionSpec as P

LR_USER = 0.005
LR_ITEM = 0.05
LAMBDA = 64.0

LANES = 128
F32 = jnp.float32
BF16 = jnp.bfloat16
F16 = jnp.float16

GRAD_SCALE = 2.0**-7
ROOT_SCALE = 2.0**-9
ITEM_SCALE = 2.0**12
GRAM_SCALE = 2.0**12
GRAM_STRATUM_SCALE = 2.0**5
GRAM_INNER_SCALE = 2.0**6

ROWS = 16
PAIR = 2 * ROWS
PACKED = 2 * LANES + 1

GROUP = ("far", "near")
INNER = ("far", "near", "pair")

VMEM = pltpu.VMEM
SMEM = pltpu.SMEM


def contract(a, b, dims):
    return lax.dot_general(a, b, ((dims[:1], dims[1:]), ((), ())), preferred_element_type=F32)


def halves(x):
    return jnp.concatenate([x[:, :LANES], x[:, LANES:]], axis=0)


def widths(x):
    rows = x.shape[0] // 2
    return jnp.concatenate([x[:rows], x[rows:]], axis=1)


def piece_rows(chunks):
    return 2 * (-(-PACKED // (2 * chunks)))


def packed_gram(weighed, rows):
    gram = contract(weighed, rows, (0, 0))
    upper, beside, lower = gram[:LANES, :LANES], gram[:LANES, LANES:], gram[LANES:, LANES:]
    row = lax.broadcasted_iota(jnp.int32, (LANES, LANES), 0)
    col = lax.broadcasted_iota(jnp.int32, (LANES, LANES), 1)
    both = jnp.where(col >= row, upper, lower)
    return both, beside, jnp.sum(jnp.where(col == row, lower, 0.0), axis=0, keepdims=True)


def put_packed(packed, weighed, rows, scale):
    both, beside, diagonal = packed_gram(weighed, rows)
    packed[...] = jnp.zeros_like(packed)
    packed[0:LANES, :] = both * scale
    packed[LANES : 2 * LANES, :] = beside * scale
    packed[2 * LANES : 2 * LANES + 1, :] = diagonal * scale


def whole_gram(packed, scale):
    both = packed[0:LANES, :] * scale
    beside = packed[LANES : 2 * LANES, :] * scale
    diagonal = packed[2 * LANES : 2 * LANES + 1, :] * scale
    row = lax.broadcasted_iota(jnp.int32, (LANES, LANES), 0)
    col = lax.broadcasted_iota(jnp.int32, (LANES, LANES), 1)
    above = jnp.where(col > row, both, 0.0)
    below = jnp.where(col < row, both, 0.0)
    upper = above + above.T + jnp.where(col == row, both, 0.0)
    lower = below + below.T + jnp.where(col == row, diagonal, 0.0)
    return jnp.concatenate(
        [jnp.concatenate([upper, beside], axis=1), jnp.concatenate([beside.T, lower], axis=1)], axis=0
    )


def split(x):
    high = x.astype(BF16)
    return high, (x - high.astype(F32)).astype(BF16)


def times_gram(users, gram):
    uh, ul = split(users)
    gh, gl = split(gram)
    return contract(uh, gh, (1, 0)) + (contract(ul, gh, (1, 0)) + contract(uh, gl, (1, 0)))


def pick_row(ids_ref, step):
    row = lax.broadcasted_iota(jnp.int32, (2, LANES), 0)
    lane = lax.broadcasted_iota(jnp.int32, (2, LANES), 1)
    counts = jnp.zeros((2, LANES), F32)
    for n in range(ids_ref.shape[1]):
        counts = counts + jnp.where((lane == ids_ref[step, n]) & (row == 0), 1.0, 0.0)
    return counts


def lane_side():
    lane = lax.broadcasted_iota(jnp.int32, (LANES, LANES), 1)
    return lax.rem(lax.div(lane, ROWS), 2)


def beside(x, side):
    return jnp.where(side == 0, pltpu.roll(x, ROWS, 1), pltpu.roll(x, LANES - ROWS, 1))


def start_kernel(held, ids, users, values, rows, cols, count, out, packet):
    stride = PAIR + 2
    held_rows = halves(held[...].astype(BF16))
    counts = pick_row(ids, 0).astype(BF16)
    for chunk in range(out.shape[0] // stride):
        at = chunk * stride
        out[at : at + PAIR, :] = held_rows
        out[at + PAIR : at + stride, :] = counts
    size = users.shape[0]
    packet[0:size, :] = users[:, :LANES].astype(BF16)
    packet[size : 2 * size, :] = users[:, LANES:].astype(BF16)
    theirs = 1 - lax.axis_index("pair")
    first = lane_side() == theirs
    slots = values.shape[1]
    for k in range(slots // 2):
        other = beside(values[0, k + slots // 2].astype(F32), theirs)
        at = 2 * size + k * LANES
        packet[at : at + LANES, :] = jnp.where(first, values[0, k].astype(F32), other).astype(BF16)
    lane = lax.broadcasted_iota(jnp.int32, (16, LANES), 1)
    lists = jnp.where(lane == 2 * slots, count[0, 0], 0)
    for k in range(slots):
        lists = jnp.where(lane == k, rows[0, k], jnp.where(lane == slots + k, cols[0, k], lists))
    at = 2 * size + slots // 2 * LANES
    packet[at : at + 16, :] = lists.astype(F32).astype(BF16)


def lists_of(packet, slots):
    size = packet.shape[0]
    line = packet[size - 16 : size, :].astype(F32)[0:1]
    lane = lax.broadcasted_iota(jnp.int32, line.shape, 1)
    return [
        jnp.sum(jnp.where(lane == k, line, 0.0)).astype(jnp.int32) for k in range(2 * slots + 1)
    ]


def item_grads(users_bf, block, values, rows, cols, live, errors, owned, scale, add):
    slots, tile_u, tile_i = errors.shape
    for k in range(slots):
        row = pl.multiple_of(rows(k) * tile_u, tile_u)
        col = cols(k)
        user_tile = users_bf[pl.ds(row, tile_u), :]
        item_tile = block[pl.ds(pl.multiple_of(col * tile_i, tile_i), tile_i), :]
        scores = contract(user_tile, item_tile, (1, 1))
        there = k < live if owned is None else owned & (k < live)
        err = jnp.where(there, scores - values(k).astype(F32), 0.0).astype(BF16)
        errors[k] = err
        if scale is not None:
            err = err * jnp.asarray(scale, BF16)
        add(col, contract(err, user_tile, (0, 0)))


def user_grads(block, rows, cols, errors, grad_users):
    slots, tile_u, tile_i = errors.shape
    grad_users[...] = jnp.zeros_like(grad_users)
    for k in range(slots):
        row = pl.multiple_of(rows(k) * tile_u, tile_u)
        col = pl.multiple_of(cols(k) * tile_i, tile_i)
        grad_users[pl.ds(row, tile_u), :] += contract(errors[k], block[pl.ds(col, tile_i), :], (1, 0))


def at_step(ref, step):
    return lambda k: ref[step, k]


def from_list(scalars, first):
    return lambda k: scalars[first + k]


def pair_rows(chunk, side):
    return pl.ds(pl.multiple_of(chunk * 2 * ROWS + side * ROWS, ROWS), ROWS)


def first_kernel(
    got, users, packet, values, rows, cols, count,
    sums, block, errors, their_errors, users_bf, their_users, grads,
):
    stride = PAIR + 2
    chunks = got.shape[0] // stride
    side = lax.axis_index("pair")
    slots, tile_u, tile_i = errors.shape
    block[...] = jnp.zeros_like(block)
    for chunk in range(chunks):
        at = chunk * stride
        block[pair_rows(chunk, side), :LANES] = got[at : at + ROWS, :]
        block[pair_rows(chunk, side), LANES:] = got[at + ROWS : at + PAIR, :]
    users_bf[...] = users[...].astype(BF16)
    grads[...] = jnp.zeros_like(grads)
    owned = lane_side() == side
    size = users.shape[0]
    their_users[:, :LANES] = packet[0:size, :]
    their_users[:, LANES:] = packet[size : 2 * size, :]
    theirs = lists_of(packet, slots)

    def their_values(k):
        at = 2 * size + k % (slots // 2) * tile_u
        shared = packet[at : at + tile_u, :].astype(F32)
        return shared if k < slots // 2 else beside(shared, 1 - side)

    def add(col, part):
        at = pl.multiple_of(col * part.shape[0], part.shape[0])
        grads[pl.ds(at, part.shape[0]), :] += part

    item_grads(
        users_bf, block, lambda k: values[0, k], at_step(rows, 0), at_step(cols, 0), count[0, 0],
        errors, owned, GRAD_SCALE, add,
    )
    item_grads(
        their_users, block, their_values, from_list(theirs, 0), from_list(theirs, slots),
        theirs[2 * slots], their_errors, owned, GRAD_SCALE, add,
    )
    for chunk in range(chunks):
        sums[chunk] = halves(grads[pair_rows(chunk, side), :])


def first_users_kernel(
    got, block, users, rows, cols, errors, packet, their_errors,
    users_out, their_grads, piece_out, their_piece, counts, packed, pieces, mine, grad_users,
):
    stride = PAIR + 2
    chunks = got.shape[0] // stride
    side = lax.axis_index("pair")
    for chunk in range(chunks):
        at = chunk * stride + PAIR
        counts[chunk : chunk + 1, :] = got[at : at + 2, :].astype(F32)[0:1]
        mine[chunk * ROWS : (chunk + 1) * ROWS, :] = block[pair_rows(chunk, side), :]
    shape = (chunks, ROWS, LANES)
    own = lax.broadcasted_iota(jnp.int32, shape, 1) == lax.broadcasted_iota(jnp.int32, shape, 2)
    weight = jnp.sum(jnp.where(own, counts[...][:, None, :], 0.0), axis=2, keepdims=True)
    plain = mine[...]
    left = (plain[:, :LANES].astype(F32).reshape(shape) * weight).reshape(-1, LANES)
    right = (plain[:, LANES:].astype(F32).reshape(shape) * weight).reshape(-1, LANES)
    high, low = split(jnp.concatenate([left, right], axis=1))
    put_packed(
        packed,
        jnp.concatenate([high, low], axis=0),
        jnp.concatenate([plain, plain], axis=0),
        GRAM_STRATUM_SCALE,
    )
    devices = pieces.shape[0]
    piece = packed.shape[0] // devices
    for device in range(devices):
        pieces[device, 0:piece, :] = packed[device * piece : (device + 1) * piece, :]
    me = lax.axis_index(INNER)
    piece_out[...] = pieces[me]
    their_piece[...] = pieces[me + 1 - 2 * side]
    slots = errors.shape[0]
    theirs = lists_of(packet, slots)
    user_grads(block, from_list(theirs, 0), from_list(theirs, slots), their_errors, their_grads)
    user_grads(block, at_step(rows, 0), at_step(cols, 0), errors, grad_users)
    users_out[...] = users[...] - LR_USER * grad_users[...]


def update(held, accum, gradient):
    accum = accum + gradient * gradient
    return held - LR_ITEM * gradient / jnp.sqrt(accum), accum


def pick_counts(ids_ref, step):
    row = lax.broadcasted_iota(jnp.int32, (8, LANES), 0)
    lane = lax.broadcasted_iota(jnp.int32, (8, LANES), 1)
    row = jnp.where(lane < LANES // 2, row, row + 8)
    counts = jnp.zeros((8, LANES), F32)
    for n in range(ids_ref.shape[1]):
        counts = counts + jnp.where(row == ids_ref[step, n], 1.0, 0.0)
    return counts


def item_kernel(got, held, accum, gram_piece, their_piece, ids, state, out):
    strata = out.shape[0]
    gradient = widths(jnp.sum(got[...], axis=0) * (1.0 / GRAD_SCALE))
    new, state[ROWS:, :] = update(held[...], accum[...], gradient)
    state[0:ROWS, :] = new
    items = halves(new.astype(BF16).astype(F32)) * ITEM_SCALE
    sent = jnp.concatenate([items, pick_counts(ids, 1), gram_piece[...] + their_piece[...]], axis=0)
    out[...] = jnp.broadcast_to(sent[None], (strata,) + sent.shape)


def gather_kernel(total, met, out, packed):
    strata = met.shape[0]
    chunks = lax.axis_size(INNER)
    piece = packed.shape[0] // chunks
    stride = PAIR + 2 * piece
    after = lax.rem(lax.axis_index("stratum") + 1, strata)
    items = met[pl.ds(after, 1), 0:PAIR, :][0]
    full = jnp.sum(met[:, 40:, :], axis=0)[0:piece] * (GRAM_SCALE / GRAM_STRATUM_SCALE / total)
    counts = jnp.concatenate([met[-1:, 32:40, :], met[:-1, 32:40, :]], axis=0)
    counts = jnp.concatenate([counts[:, :, 0:1], counts[:, :, 64:65]], axis=1)
    rows = [met[:, 0:ROWS, :] * (1.0 / ITEM_SCALE), met[:, ROWS:PAIR, :] * (1.0 / ITEM_SCALE)]
    weighed = jnp.concatenate([(r * counts).reshape(-1, LANES) for r in rows], axis=1)
    plain = jnp.concatenate([r.reshape(-1, LANES) for r in rows], axis=1).astype(BF16)
    high, low = split(weighed)
    put_packed(
        packed,
        jnp.concatenate([high, low], axis=0),
        jnp.concatenate([plain, plain], axis=0),
        GRAM_INNER_SCALE,
    )
    for chunk in range(chunks):
        at = chunk * stride
        out[at : at + PAIR, :] = items
        out[at + PAIR : at + PAIR + piece, :] = full
        out[at + PAIR + piece : at + stride, :] = packed[chunk * piece : (chunk + 1) * piece, :]


def second_kernel(
    total, got, users, mid, rest, values, rows, cols, count, sums, mid_out, block, errors, packed, users_bf, grads
):
    chunks = block.shape[0] // ROWS
    piece = packed.shape[0] // chunks
    stride = PAIR + 2 * piece
    full = jnp.zeros((piece, LANES), F32)
    for chunk in range(chunks):
        to, at = chunk * ROWS, chunk * stride
        block[to : to + ROWS, :LANES] = (got[at : at + ROWS, :] * (1.0 / ITEM_SCALE)).astype(BF16)
        block[to : to + ROWS, LANES:] = (got[at + ROWS : at + PAIR, :] * (1.0 / ITEM_SCALE)).astype(BF16)
        packed[chunk * piece : (chunk + 1) * piece, :] = got[at + PAIR : at + PAIR + piece, :]
        full = full + got[at + PAIR + piece : at + stride, :]
    gram = whole_gram(packed, 1.0 / GRAM_SCALE)
    part = mid[...] - LR_USER * rest[...]
    now = part - (LR_USER * LAMBDA) * times_gram(users[...], gram)
    mid_out[...] = now
    users_bf[...] = now.astype(BF16)
    grads[...] = jnp.zeros_like(grads)

    def add(col, part):
        at = pl.multiple_of(col * part.shape[0], part.shape[0])
        grads[pl.ds(at, part.shape[0]), :] += part

    item_grads(
        users_bf, block, lambda k: values[1, k], at_step(rows, 1), at_step(cols, 1), count[1, 0],
        errors, None, None, add,
    )
    full = full * (GRAM_SCALE / GRAM_INNER_SCALE / total)
    for chunk in range(chunks):
        at = chunk * (PAIR + piece)
        raw = halves(grads[chunk * ROWS : (chunk + 1) * ROWS, :])
        root = jnp.sqrt(jnp.abs(raw)) * ROOT_SCALE
        sums[at : at + PAIR, :] = jnp.where(raw < 0.0, -root, root)
        sums[at + PAIR : at + PAIR + piece, :] = full


def second_users_kernel(block, now, rows, cols, errors, users_out, grad_users):
    user_grads(block, at_step(rows, 1), at_step(cols, 1), errors, grad_users)
    users_out[...] = now[...] - LR_USER * grad_users[...]


def last_items_kernel(chunks, got, state, out):
    stride = got.shape[0] // chunks
    total = jnp.zeros((PAIR, LANES), F32)
    for chunk in range(chunks):
        root = got[chunk * stride : chunk * stride + PAIR, :]
        total = total + root * jnp.abs(root)
    out[0:ROWS, :], out[ROWS:, :] = update(
        state[0:ROWS, :], state[ROWS:, :], widths(total * ROOT_SCALE**-2)
    )


def last_users_kernel(chunks, got, users, mid, out, packed):
    stride = got.shape[0] // chunks
    piece = stride - PAIR
    for chunk in range(chunks):
        packed[chunk * piece : (chunk + 1) * piece, :] = got[chunk * stride + PAIR : (chunk + 1) * stride, :]
    gram = whole_gram(packed, 1.0 / GRAM_SCALE)
    out[...] = users[...] - (LR_USER * LAMBDA) * times_gram(mid[...], gram)


def call(kernel, out_shape, specs, *args, scratch=()):
    return pl.pallas_call(
        kernel,
        out_shape=out_shape,
        in_specs=specs,
        out_specs=jax.tree.map(lambda _: pl.BlockSpec(memory_space=VMEM), out_shape),
        scratch_shapes=scratch,
        compiler_params=pltpu.CompilerParams(vmem_limit_bytes=44 * 2**20),
    )(*args)


def exchanged(x, axis):
    return lax.all_to_all(x, axis, 0, 0, tiled=True)


def chunks_exchanged(flat, axis):
    paired = flat.reshape(lax.axis_size(axis), -1, 2, LANES)
    return exchanged(paired, axis).reshape(flat.shape)


def swapped(x):
    return lax.ppermute(x, "pair", [(0, 1), (1, 0)])


def shards(
    user_factors, item_factors, item_accum, tile_values, tile_rows, tile_cols, tile_count, neg_ids
):
    strata = lax.axis_size("stratum")
    inners = lax.axis_size(INNER)
    group = lax.axis_size(GROUP)
    rank = item_factors.shape[1]
    total = float(strata * inners * neg_ids.shape[1])
    piece = piece_rows(inners)
    padded = -(-piece // 8) * 8
    onward = [((s + 1) % strata, s) for s in range(strata)]
    vm = pl.BlockSpec(memory_space=VMEM)
    sm = pl.BlockSpec(memory_space=SMEM)
    shape = jax.ShapeDtypeStruct
    users_shape = shape(user_factors.shape, F32)
    users_f32 = pltpu.VMEM(user_factors.shape, F32)
    users_bf = pltpu.VMEM(user_factors.shape, BF16)
    state_shape = shape((PAIR, rank), F32)
    block_shape = shape((inners * ROWS, rank), BF16)
    errors_shape = shape(tile_values.shape[1:], BF16)
    piece_shape = shape((padded, LANES), F32)
    packed = pltpu.VMEM((inners * piece, LANES), F32)

    slots = tile_values.shape[1]
    packet_rows = 2 * user_factors.shape[0] + slots // 2 * LANES + 16
    sent, packet = call(
        start_kernel,
        (shape((group * (PAIR + 2), LANES), BF16), shape((packet_rows, LANES), BF16)),
        [vm, sm, vm, vm, sm, sm, sm],
        item_factors, neg_ids, user_factors, tile_values, tile_rows, tile_cols, tile_count,
    )
    got = chunks_exchanged(sent, GROUP)
    packet = swapped(packet)
    sums, block, errors, their_errors = call(
        first_kernel,
        (shape((group, PAIR, LANES), F32), block_shape, errors_shape, errors_shape),
        [vm, vm, vm, vm, sm, sm, sm],
        got, user_factors, packet, tile_values, tile_rows, tile_cols, tile_count,
        scratch=[users_bf, users_bf, pltpu.VMEM(block_shape.shape, F32)],
    )
    sums = exchanged(sums.astype(F16), GROUP).astype(F32)
    mid, rest, gram_piece, their_piece = call(
        first_users_kernel,
        (users_shape, users_shape, piece_shape, piece_shape),
        [vm, vm, vm, sm, sm, vm, vm, vm],
        got, block, user_factors, tile_rows, tile_cols, errors, packet, their_errors,
        scratch=[
            pltpu.VMEM((group, LANES), F32),
            packed,
            pltpu.VMEM((inners, padded, LANES), F32),
            pltpu.VMEM((group * ROWS, rank), BF16),
            users_f32,
        ],
    )
    their_piece = swapped(their_piece)
    rest = swapped(rest)
    state, sent = call(
        item_kernel,
        (state_shape, shape((strata, PAIR + 8 + padded, LANES), F32)),
        [vm, vm, vm, vm, vm, sm],
        sums, item_factors, item_accum, gram_piece, their_piece, neg_ids,
    )
    met = exchanged(sent.astype(F16), "stratum").astype(F32)
    sent = call(
        functools.partial(gather_kernel, total),
        shape((inners * (PAIR + 2 * piece), LANES), F32),
        [vm],
        met,
        scratch=[packed],
    ).astype(F16)
    got = chunks_exchanged(sent, INNER).astype(F32)
    sums, mid, block, errors = call(
        functools.partial(second_kernel, total),
        (shape((inners * (PAIR + piece), LANES), F32), users_shape, block_shape, errors_shape),
        [vm, vm, vm, vm, vm, sm, sm, sm],
        got, user_factors, mid, rest, tile_values, tile_rows, tile_cols, tile_count,
        scratch=[packed, users_bf, pltpu.VMEM(block_shape.shape, F32)],
    )
    sums, state = lax.optimization_barrier((sums.astype(F16), state))
    state = lax.ppermute(state, "stratum", onward)
    got = chunks_exchanged(sums, INNER).astype(F32)
    users = call(
        second_users_kernel, users_shape, [vm, vm, sm, sm, vm],
        block, mid, tile_rows, tile_cols, errors, scratch=[users_f32],
    )
    state = call(functools.partial(last_items_kernel, inners), state_shape, [vm, vm], got, state)
    state = lax.ppermute(state, "stratum", onward)
    users = call(
        functools.partial(last_users_kernel, inners), users_shape, [vm, vm, vm],
        got, users, mid, scratch=[packed],
    )
    return (users, state[:ROWS], state[ROWS:])


def solution(mesh):
    strata, inners = mesh.devices.shape
    fine = jax.sharding.Mesh(
        mesh.devices.reshape(strata, inners // 4, 2, 2), ("stratum",) + INNER
    )
    every = ("stratum",) + INNER
    devices = P(every, None)
    slots = P(None, every)
    return jax.shard_map(
        shards,
        mesh=fine,
        in_specs=(
            devices,
            devices,
            devices,
            P(None, every, None, None),
            slots,
            slots,
            slots,
            slots,
        ),
        out_specs=(devices, devices, devices),
        check_vma=False,
    )
```

```python
import functools

import jax
import jax.numpy as jnp
from jax import lax
from jax.experimental import pallas as pl
from jax.experimental.pallas import tpu as pltpu
from jax.sharding import PartitionSpec as P

LR_USER = 0.005
LR_ITEM = 0.05
LAMBDA = 64.0

LANES = 128
F32 = jnp.float32
BF16 = jnp.bfloat16
F16 = jnp.float16

GRAD_SCALE = 2.0**-7
REST_SCALE = 2.0**-6
ROOT_SCALE = 2.0**-9
ITEM_SCALE = 2.0**12
GRAM_SCALE = 2.0**12
GRAM_STRATUM_SCALE = 2.0**5
GRAM_INNER_SCALE = 2.0**6

ROWS = 16
PAIR = 2 * ROWS
PACKED = 2 * LANES + 1

GROUP = ("far", "near")
INNER = ("far", "near", "pair")

VMEM = pltpu.VMEM
SMEM = pltpu.SMEM


def contract(a, b, dims):
    return lax.dot_general(a, b, ((dims[:1], dims[1:]), ((), ())), preferred_element_type=F32)


def halves(x):
    return jnp.concatenate([x[:, :LANES], x[:, LANES:]], axis=0)


def widths(x):
    rows = x.shape[0] // 2
    return jnp.concatenate([x[:rows], x[rows:]], axis=1)


def piece_rows(chunks):
    return 2 * (-(-PACKED // (2 * chunks)))


def packed_gram(weighed, rows):
    gram = contract(weighed, rows, (0, 0))
    upper, beside, lower = gram[:LANES, :LANES], gram[:LANES, LANES:], gram[LANES:, LANES:]
    row = lax.broadcasted_iota(jnp.int32, (LANES, LANES), 0)
    col = lax.broadcasted_iota(jnp.int32, (LANES, LANES), 1)
    both = jnp.where(col >= row, upper, lower)
    return both, beside, jnp.sum(jnp.where(col == row, lower, 0.0), axis=0, keepdims=True)


def put_packed(packed, weighed, rows, scale):
    both, beside, diagonal = packed_gram(weighed, rows)
    packed[...] = jnp.zeros_like(packed)
    packed[0:LANES, :] = both * scale
    packed[LANES : 2 * LANES, :] = beside * scale
    packed[2 * LANES : 2 * LANES + 1, :] = diagonal * scale


def whole_gram(packed, scale):
    both = packed[0:LANES, :] * scale
    beside = packed[LANES : 2 * LANES, :] * scale
    diagonal = packed[2 * LANES : 2 * LANES + 1, :] * scale
    row = lax.broadcasted_iota(jnp.int32, (LANES, LANES), 0)
    col = lax.broadcasted_iota(jnp.int32, (LANES, LANES), 1)
    above = jnp.where(col > row, both, 0.0)
    below = jnp.where(col < row, both, 0.0)
    upper = above + above.T + jnp.where(col == row, both, 0.0)
    lower = below + below.T + jnp.where(col == row, diagonal, 0.0)
    return jnp.concatenate(
        [jnp.concatenate([upper, beside], axis=1), jnp.concatenate([beside.T, lower], axis=1)], axis=0
    )


def split(x):
    high = x.astype(BF16)
    return high, (x - high.astype(F32)).astype(BF16)


def times_gram(users, gram):
    uh, ul = split(users)
    gh, gl = split(gram)
    return contract(uh, gh, (1, 0)) + (contract(ul, gh, (1, 0)) + contract(uh, gl, (1, 0)))


def pick_row(ids_ref, step):
    row = lax.broadcasted_iota(jnp.int32, (2, LANES), 0)
    lane = lax.broadcasted_iota(jnp.int32, (2, LANES), 1)
    counts = jnp.zeros((2, LANES), F32)
    for n in range(ids_ref.shape[1]):
        counts = counts + jnp.where((lane == ids_ref[step, n]) & (row == 0), 1.0, 0.0)
    return counts


def lane_side():
    lane = lax.broadcasted_iota(jnp.int32, (LANES, LANES), 1)
    return lax.rem(lax.div(lane, ROWS), 2)


def beside(x, side):
    return jnp.where(side == 0, pltpu.roll(x, ROWS, 1), pltpu.roll(x, LANES - ROWS, 1))


def start_kernel(*refs):
    given, (out, packet), taken, done = refs[:7], refs[7:9], refs[9:16], refs[16]
    held, ids, users, values, rows, cols, count = taken
    copies = []
    for i, (source, target) in enumerate(zip(given, taken, strict=True)):
        source = source.at[0] if target is values else source
        copies.append(pltpu.make_async_copy(source, target, done.at[i]))
    for copy in copies:
        copy.start()
    for copy in copies[:2]:
        copy.wait()
    stride = PAIR + 2
    held_rows = halves(held[...].astype(BF16))
    counts = pick_row(ids, 0).astype(BF16)
    for chunk in range(out.shape[0] // stride):
        at = chunk * stride
        out[at : at + PAIR, :] = held_rows
        out[at + PAIR : at + stride, :] = counts
    for copy in copies[2:]:
        copy.wait()
    size = users.shape[0]
    packet[0:size, :] = users[:, :LANES].astype(BF16)
    packet[size : 2 * size, :] = users[:, LANES:].astype(BF16)
    theirs = 1 - lax.axis_index("pair")
    first = lane_side() == theirs
    slots = values.shape[0]
    for k in range(slots // 2):
        other = beside(values[k + slots // 2].astype(F32), theirs)
        at = 2 * size + k * LANES
        packet[at : at + LANES, :] = jnp.where(first, values[k].astype(F32), other).astype(BF16)
    lane = lax.broadcasted_iota(jnp.int32, (16, LANES), 1)
    lists = jnp.where(lane == 2 * slots, count[0, 0], 0)
    for k in range(slots):
        lists = jnp.where(lane == k, rows[0, k], jnp.where(lane == slots + k, cols[0, k], lists))
    at = 2 * size + slots // 2 * LANES
    packet[at : at + 16, :] = lists.astype(F32).astype(BF16)


def lists_of(packet, slots):
    size = packet.shape[0]
    line = packet[size - 16 : size, :].astype(F32)[0:1]
    lane = lax.broadcasted_iota(jnp.int32, line.shape, 1)
    return [
        jnp.sum(jnp.where(lane == k, line, 0.0)).astype(jnp.int32) for k in range(2 * slots + 1)
    ]


def item_grads(users_bf, block, values, rows, cols, live, errors, owned, scale, add):
    slots, tile_u, tile_i = errors.shape
    for k in range(slots):
        row = pl.multiple_of(rows(k) * tile_u, tile_u)
        col = cols(k)
        user_tile = users_bf[pl.ds(row, tile_u), :]
        item_tile = block[pl.ds(pl.multiple_of(col * tile_i, tile_i), tile_i), :]
        scores = contract(user_tile, item_tile, (1, 1))
        there = k < live if owned is None else owned & (k < live)
        err = jnp.where(there, scores - values(k).astype(F32), 0.0).astype(BF16)
        errors[k] = err
        if scale is not None:
            err = err * jnp.asarray(scale, BF16)
        add(col, contract(err, user_tile, (0, 0)))


def user_grads(block, rows, cols, errors, grad_users):
    slots, tile_u, tile_i = errors.shape
    grad_users[...] = jnp.zeros_like(grad_users)
    for k in range(slots):
        row = pl.multiple_of(rows(k) * tile_u, tile_u)
        col = pl.multiple_of(cols(k) * tile_i, tile_i)
        grad_users[pl.ds(row, tile_u), :] += contract(errors[k], block[pl.ds(col, tile_i), :], (1, 0))


def at_step(ref, step):
    return lambda k: ref[step, k]


def from_list(scalars, first):
    return lambda k: scalars[first + k]


def pair_rows(chunk, side):
    return pl.ds(pl.multiple_of(chunk * 2 * ROWS + side * ROWS, ROWS), ROWS)


def first_kernel(
    got, users, packet, values, rows, cols, count,
    sums, block, errors, their_errors, users_bf, their_users, grads,
):
    stride = PAIR + 2
    chunks = got.shape[0] // stride
    side = lax.axis_index("pair")
    slots, tile_u, tile_i = errors.shape
    block[...] = jnp.zeros_like(block)
    for chunk in range(chunks):
        at = chunk * stride
        block[pair_rows(chunk, side), :LANES] = got[at : at + ROWS, :]
        block[pair_rows(chunk, side), LANES:] = got[at + ROWS : at + PAIR, :]
    users_bf[...] = users[...].astype(BF16)
    grads[...] = jnp.zeros_like(grads)
    owned = lane_side() == side
    size = users.shape[0]
    their_users[:, :LANES] = packet[0:size, :]
    their_users[:, LANES:] = packet[size : 2 * size, :]
    theirs = lists_of(packet, slots)

    def their_values(k):
        at = 2 * size + k % (slots // 2) * tile_u
        shared = packet[at : at + tile_u, :].astype(F32)
        return shared if k < slots // 2 else beside(shared, 1 - side)

    def add(col, part):
        at = pl.multiple_of(col * part.shape[0], part.shape[0])
        grads[pl.ds(at, part.shape[0]), :] += part

    item_grads(
        users_bf, block, lambda k: values[0, k], at_step(rows, 0), at_step(cols, 0), count[0, 0],
        errors, owned, GRAD_SCALE, add,
    )
    item_grads(
        their_users, block, their_values, from_list(theirs, 0), from_list(theirs, slots),
        theirs[2 * slots], their_errors, owned, GRAD_SCALE, add,
    )
    for chunk in range(chunks):
        sums[chunk] = halves(grads[pair_rows(chunk, side), :])


def first_users_kernel(
    got, block, users, rows, cols, errors, packet, their_errors,
    users_out, their_grads, piece_out, their_piece, counts, packed, pieces, mine, grad_users,
):
    stride = PAIR + 2
    chunks = got.shape[0] // stride
    side = lax.axis_index("pair")
    for chunk in range(chunks):
        at = chunk * stride + PAIR
        counts[chunk : chunk + 1, :] = got[at : at + 2, :].astype(F32)[0:1]
        mine[chunk * ROWS : (chunk + 1) * ROWS, :] = block[pair_rows(chunk, side), :]
    shape = (chunks, ROWS, LANES)
    own = lax.broadcasted_iota(jnp.int32, shape, 1) == lax.broadcasted_iota(jnp.int32, shape, 2)
    weight = jnp.sum(jnp.where(own, counts[...][:, None, :], 0.0), axis=2, keepdims=True)
    plain = mine[...]
    left = (plain[:, :LANES].astype(F32).reshape(shape) * weight).reshape(-1, LANES)
    right = (plain[:, LANES:].astype(F32).reshape(shape) * weight).reshape(-1, LANES)
    high, low = split(jnp.concatenate([left, right], axis=1))
    put_packed(
        packed,
        jnp.concatenate([high, low], axis=0),
        jnp.concatenate([plain, plain], axis=0),
        GRAM_STRATUM_SCALE,
    )
    devices = pieces.shape[0]
    piece = packed.shape[0] // devices
    for device in range(devices):
        pieces[device, 0:piece, :] = packed[device * piece : (device + 1) * piece, :]
    me = lax.axis_index(INNER)
    piece_out[...] = pieces[me]
    their_piece[...] = pieces[me + 1 - 2 * side]
    slots = errors.shape[0]
    theirs = lists_of(packet, slots)
    user_grads(block, from_list(theirs, 0), from_list(theirs, slots), their_errors, their_grads)
    user_grads(block, at_step(rows, 0), at_step(cols, 0), errors, grad_users)
    users_out[...] = users[...] - LR_USER * grad_users[...]


def update(held, accum, gradient):
    accum = accum + gradient * gradient
    return held - LR_ITEM * gradient / jnp.sqrt(accum), accum


def pick_counts(ids_ref, step):
    row = lax.broadcasted_iota(jnp.int32, (8, LANES), 0)
    lane = lax.broadcasted_iota(jnp.int32, (8, LANES), 1)
    row = jnp.where(lane < LANES // 2, row, row + 8)
    counts = jnp.zeros((8, LANES), F32)
    for n in range(ids_ref.shape[1]):
        counts = counts + jnp.where(row == ids_ref[step, n], 1.0, 0.0)
    return counts


def item_kernel(got, held, accum, gram_piece, their_piece, ids, state, out):
    strata = out.shape[0]
    gradient = widths(jnp.sum(got[...], axis=0) * (1.0 / GRAD_SCALE))
    new, state[ROWS:, :] = update(held[...], accum[...], gradient)
    state[0:ROWS, :] = new
    items = halves(new.astype(BF16).astype(F32)) * ITEM_SCALE
    sent = jnp.concatenate([items, pick_counts(ids, 1), gram_piece[...] + their_piece[...]], axis=0)
    out[...] = jnp.broadcast_to(sent[None], (strata,) + sent.shape)


def gather_kernel(total, met, out, packed):
    strata = met.shape[0]
    chunks = lax.axis_size(INNER)
    piece = packed.shape[0] // chunks
    stride = PAIR + 2 * piece
    after = lax.rem(lax.axis_index("stratum") + 1, strata)
    items = met[pl.ds(after, 1), 0:PAIR, :][0]
    full = jnp.sum(met[:, 40:, :], axis=0)[0:piece] * (GRAM_SCALE / GRAM_STRATUM_SCALE / total)
    counts = jnp.concatenate([met[-1:, 32:40, :], met[:-1, 32:40, :]], axis=0)
    counts = jnp.concatenate([counts[:, :, 0:1], counts[:, :, 64:65]], axis=1)
    rows = [met[:, 0:ROWS, :] * (1.0 / ITEM_SCALE), met[:, ROWS:PAIR, :] * (1.0 / ITEM_SCALE)]
    weighed = jnp.concatenate([(r * counts).reshape(-1, LANES) for r in rows], axis=1)
    plain = jnp.concatenate([r.reshape(-1, LANES) for r in rows], axis=1).astype(BF16)
    high, low = split(weighed)
    put_packed(
        packed,
        jnp.concatenate([high, low], axis=0),
        jnp.concatenate([plain, plain], axis=0),
        GRAM_INNER_SCALE,
    )
    for chunk in range(chunks):
        at = chunk * stride
        out[at : at + PAIR, :] = items
        out[at + PAIR : at + PAIR + piece, :] = full
        out[at + PAIR + piece : at + stride, :] = packed[chunk * piece : (chunk + 1) * piece, :]


def second_kernel(
    total, got, users, mid, rest, values, rows, cols, count, sums, mid_out, block, errors, packed, users_bf, grads
):
    chunks = block.shape[0] // ROWS
    piece = packed.shape[0] // chunks
    stride = PAIR + 2 * piece
    full = jnp.zeros((piece, LANES), F32)
    for chunk in range(chunks):
        to, at = chunk * ROWS, chunk * stride
        block[to : to + ROWS, :LANES] = (got[at : at + ROWS, :] * (1.0 / ITEM_SCALE)).astype(BF16)
        block[to : to + ROWS, LANES:] = (got[at + ROWS : at + PAIR, :] * (1.0 / ITEM_SCALE)).astype(BF16)
        packed[chunk * piece : (chunk + 1) * piece, :] = got[at + PAIR : at + PAIR + piece, :]
        full = full + got[at + PAIR + piece : at + stride, :]
    gram = whole_gram(packed, 1.0 / GRAM_SCALE)
    part = mid[...] - (LR_USER / REST_SCALE) * rest[...]
    now = part - (LR_USER * LAMBDA) * times_gram(users[...], gram)
    mid_out[...] = now
    users_bf[...] = now.astype(BF16)
    grads[...] = jnp.zeros_like(grads)

    def add(col, part):
        at = pl.multiple_of(col * part.shape[0], part.shape[0])
        grads[pl.ds(at, part.shape[0]), :] += part

    item_grads(
        users_bf, block, lambda k: values[1, k], at_step(rows, 1), at_step(cols, 1), count[1, 0],
        errors, None, None, add,
    )
    full = full * (GRAM_SCALE / GRAM_INNER_SCALE / total)
    for chunk in range(chunks):
        at = chunk * (PAIR + piece)
        raw = halves(grads[chunk * ROWS : (chunk + 1) * ROWS, :])
        root = jnp.sqrt(jnp.abs(raw)) * ROOT_SCALE
        sums[at : at + PAIR, :] = jnp.where(raw < 0.0, -root, root)
        sums[at + PAIR : at + PAIR + piece, :] = full


def second_users_kernel(block, now, rows, cols, errors, users_out, grad_users):
    user_grads(block, at_step(rows, 1), at_step(cols, 1), errors, grad_users)
    users_out[...] = now[...] - LR_USER * grad_users[...]


def last_items_kernel(chunks, got, state, out):
    stride = got.shape[0] // chunks
    total = jnp.zeros((PAIR, LANES), F32)
    for chunk in range(chunks):
        root = got[chunk * stride : chunk * stride + PAIR, :]
        total = total + root * jnp.abs(root)
    out[0:ROWS, :], out[ROWS:, :] = update(
        state[0:ROWS, :], state[ROWS:, :], widths(total * ROOT_SCALE**-2)
    )


def last_users_kernel(chunks, got, users, mid, out, packed):
    stride = got.shape[0] // chunks
    piece = stride - PAIR
    for chunk in range(chunks):
        packed[chunk * piece : (chunk + 1) * piece, :] = got[chunk * stride + PAIR : (chunk + 1) * stride, :]
    gram = whole_gram(packed, 1.0 / GRAM_SCALE)
    out[...] = users[...] - (LR_USER * LAMBDA) * times_gram(mid[...], gram)


def call(kernel, out_shape, specs, *args, scratch=(), vmem=44):
    return pl.pallas_call(
        kernel,
        out_shape=out_shape,
        in_specs=specs,
        out_specs=jax.tree.map(lambda _: pl.BlockSpec(memory_space=VMEM), out_shape),
        scratch_shapes=scratch,
        compiler_params=pltpu.CompilerParams(vmem_limit_bytes=vmem * 2**20),
    )(*args)


def exchanged(x, axis):
    return lax.all_to_all(x, axis, 0, 0, tiled=True)


def chunks_exchanged(flat, axis):
    paired = flat.reshape(lax.axis_size(axis), -1, 2, LANES)
    return exchanged(paired, axis).reshape(flat.shape)


def swapped(x):
    return lax.ppermute(x, "pair", [(0, 1), (1, 0)])


def shards(
    user_factors, item_factors, item_accum, tile_values, tile_rows, tile_cols, tile_count, neg_ids
):
    strata = lax.axis_size("stratum")
    inners = lax.axis_size(INNER)
    group = lax.axis_size(GROUP)
    rank = item_factors.shape[1]
    total = float(strata * inners * neg_ids.shape[1])
    piece = piece_rows(inners)
    padded = -(-piece // 8) * 8
    onward = [((s + 1) % strata, s) for s in range(strata)]
    vm = pl.BlockSpec(memory_space=VMEM)
    sm = pl.BlockSpec(memory_space=SMEM)
    shape = jax.ShapeDtypeStruct
    users_shape = shape(user_factors.shape, F32)
    users_f32 = pltpu.VMEM(user_factors.shape, F32)
    users_bf = pltpu.VMEM(user_factors.shape, BF16)
    state_shape = shape((PAIR, rank), F32)
    block_shape = shape((inners * ROWS, rank), BF16)
    errors_shape = shape(tile_values.shape[1:], BF16)
    piece_shape = shape((padded, LANES), F32)
    packed = pltpu.VMEM((inners * piece, LANES), F32)

    slots = tile_values.shape[1]
    packet_rows = 2 * user_factors.shape[0] + slots // 2 * LANES + 16
    sent, packet = call(
        start_kernel,
        (shape((group * (PAIR + 2), LANES), BF16), shape((packet_rows, LANES), BF16)),
        [pl.BlockSpec(memory_space=pltpu.HBM)] * 7,
        item_factors, neg_ids, user_factors, tile_values, tile_rows, tile_cols, tile_count,
        scratch=[
            pltpu.VMEM(item_factors.shape, F32),
            pltpu.SMEM(neg_ids.shape, jnp.int32),
            users_f32,
            pltpu.VMEM(tile_values.shape[1:], BF16),
            pltpu.SMEM(tile_rows.shape, jnp.int32),
            pltpu.SMEM(tile_cols.shape, jnp.int32),
            pltpu.SMEM(tile_count.shape, jnp.int32),
            pltpu.SemaphoreType.DMA((7,)),
        ],
        vmem=62,
    )
    got = chunks_exchanged(sent, GROUP)
    packet = swapped(packet)
    sums, block, errors, their_errors = call(
        first_kernel,
        (shape((group, PAIR, LANES), F32), block_shape, errors_shape, errors_shape),
        [vm, vm, vm, vm, sm, sm, sm],
        got, user_factors, packet, tile_values, tile_rows, tile_cols, tile_count,
        scratch=[users_bf, users_bf, pltpu.VMEM(block_shape.shape, F32)],
    )
    sums = exchanged(sums.astype(F16), GROUP).astype(F32)
    mid, rest, gram_piece, their_piece = call(
        first_users_kernel,
        (users_shape, users_shape, piece_shape, piece_shape),
        [vm, vm, vm, sm, sm, vm, vm, vm],
        got, block, user_factors, tile_rows, tile_cols, errors, packet, their_errors,
        scratch=[
            pltpu.VMEM((group, LANES), F32),
            packed,
            pltpu.VMEM((inners, padded, LANES), F32),
            pltpu.VMEM((group * ROWS, rank), BF16),
            users_f32,
        ],
    )
    their_piece = swapped(their_piece)
    rest = swapped((rest * REST_SCALE).astype(F16))
    state, sent = call(
        item_kernel,
        (state_shape, shape((strata, PAIR + 8 + padded, LANES), F32)),
        [vm, vm, vm, vm, vm, sm],
        sums, item_factors, item_accum, gram_piece, their_piece, neg_ids,
    )
    met = exchanged(sent.astype(F16), "stratum")
    met, rest = lax.optimization_barrier((met, rest))
    met, rest = met.astype(F32), rest.astype(F32)
    sent = call(
        functools.partial(gather_kernel, total),
        shape((inners * (PAIR + 2 * piece), LANES), F32),
        [vm],
        met,
        scratch=[packed],
    ).astype(F16)
    got = chunks_exchanged(sent, INNER).astype(F32)
    sums, mid, block, errors = call(
        functools.partial(second_kernel, total),
        (shape((inners * (PAIR + piece), LANES), F32), users_shape, block_shape, errors_shape),
        [vm, vm, vm, vm, vm, sm, sm, sm],
        got, user_factors, mid, rest, tile_values, tile_rows, tile_cols, tile_count,
        scratch=[packed, users_bf, pltpu.VMEM(block_shape.shape, F32)],
    )
    sums, state = lax.optimization_barrier((sums.astype(F16), state))
    state = lax.ppermute(state, "stratum", onward)
    got = chunks_exchanged(sums, INNER).astype(F32)
    users = call(
        second_users_kernel, users_shape, [vm, vm, sm, sm, vm],
        block, mid, tile_rows, tile_cols, errors, scratch=[users_f32],
    )
    state = call(functools.partial(last_items_kernel, inners), state_shape, [vm, vm], got, state)
    state = lax.ppermute(state, "stratum", onward)
    users = call(
        functools.partial(last_users_kernel, inners), users_shape, [vm, vm, vm],
        got, users, mid, scratch=[packed],
    )
    return (users, state[:ROWS], state[ROWS:])


def solution(mesh):
    strata, inners = mesh.devices.shape
    fine = jax.sharding.Mesh(
        mesh.devices.reshape(strata, inners // 4, 2, 2), ("stratum",) + INNER
    )
    every = ("stratum",) + INNER
    devices = P(every, None)
    slots = P(None, every)
    return jax.shard_map(
        shards,
        mesh=fine,
        in_specs=(
            devices,
            devices,
            devices,
            P(None, every, None, None),
            slots,
            slots,
            slots,
            slots,
        ),
        out_specs=(devices, devices, devices),
        check_vma=False,
    )
```

```python
import functools

import jax
import jax.numpy as jnp
from jax import lax
from jax.experimental import pallas as pl
from jax.experimental.pallas import tpu as pltpu
from jax.sharding import PartitionSpec as P

LR_USER = 0.005
LR_ITEM = 0.05
LAMBDA = 64.0

LANES = 128
F32 = jnp.float32
BF16 = jnp.bfloat16
F16 = jnp.float16

GRAD_SCALE = 2.0**-7
REST_SCALE = 2.0**-6
ROOT_SCALE = 2.0**-9
ITEM_SCALE = 2.0**12
GRAM_SCALE = 2.0**12
GRAM_STRATUM_SCALE = 2.0**5
GRAM_INNER_SCALE = 2.0**6

ROWS = 16
PAIR = 2 * ROWS
PACKED = 2 * LANES + 1

GROUP = ("far", "near")
INNER = ("far", "near", "pair")

VMEM = pltpu.VMEM
SMEM = pltpu.SMEM


def contract(a, b, dims):
    return lax.dot_general(a, b, ((dims[:1], dims[1:]), ((), ())), preferred_element_type=F32)


def halves(x):
    return jnp.concatenate([x[:, :LANES], x[:, LANES:]], axis=0)


def widths(x):
    rows = x.shape[0] // 2
    return jnp.concatenate([x[:rows], x[rows:]], axis=1)


def piece_rows(chunks):
    return 2 * (-(-PACKED // (2 * chunks)))


def packed_gram(weighed, rows):
    gram = contract(weighed, rows, (0, 0))
    upper, beside, lower = gram[:LANES, :LANES], gram[:LANES, LANES:], gram[LANES:, LANES:]
    row = lax.broadcasted_iota(jnp.int32, (LANES, LANES), 0)
    col = lax.broadcasted_iota(jnp.int32, (LANES, LANES), 1)
    both = jnp.where(col >= row, upper, lower)
    return both, beside, jnp.sum(jnp.where(col == row, lower, 0.0), axis=0, keepdims=True)


def put_packed(packed, weighed, rows, scale):
    both, beside, diagonal = packed_gram(weighed, rows)
    packed[...] = jnp.zeros_like(packed)
    packed[0:LANES, :] = both * scale
    packed[LANES : 2 * LANES, :] = beside * scale
    packed[2 * LANES : 2 * LANES + 1, :] = diagonal * scale


def whole_gram(packed, scale):
    both = packed[0:LANES, :] * scale
    beside = packed[LANES : 2 * LANES, :] * scale
    diagonal = packed[2 * LANES : 2 * LANES + 1, :] * scale
    row = lax.broadcasted_iota(jnp.int32, (LANES, LANES), 0)
    col = lax.broadcasted_iota(jnp.int32, (LANES, LANES), 1)
    above = jnp.where(col > row, both, 0.0)
    below = jnp.where(col < row, both, 0.0)
    upper = above + above.T + jnp.where(col == row, both, 0.0)
    lower = below + below.T + jnp.where(col == row, diagonal, 0.0)
    return jnp.concatenate(
        [jnp.concatenate([upper, beside], axis=1), jnp.concatenate([beside.T, lower], axis=1)], axis=0
    )


def split(x):
    high = x.astype(BF16)
    return high, (x - high.astype(F32)).astype(BF16)


def times_gram(users, gram):
    uh, ul = split(users)
    gh, gl = split(gram)
    return contract(uh, gh, (1, 0)) + (contract(ul, gh, (1, 0)) + contract(uh, gl, (1, 0)))


def pick_row(ids_ref, step):
    row = lax.broadcasted_iota(jnp.int32, (2, LANES), 0)
    lane = lax.broadcasted_iota(jnp.int32, (2, LANES), 1)
    counts = jnp.zeros((2, LANES), F32)
    for n in range(ids_ref.shape[1]):
        counts = counts + jnp.where((lane == ids_ref[step, n]) & (row == 0), 1.0, 0.0)
    return counts


def lane_side():
    lane = lax.broadcasted_iota(jnp.int32, (LANES, LANES), 1)
    return lax.rem(lax.div(lane, ROWS), 2)


def beside(x, side):
    return jnp.where(side == 0, pltpu.roll(x, ROWS, 1), pltpu.roll(x, LANES - ROWS, 1))


def start_kernel(*refs):
    given, (out, *packets), taken, done = refs[:7], refs[7:10], refs[10:17], refs[17]
    held, ids, users, values, rows, cols, count = taken
    copies = []
    for i, (source, target) in enumerate(zip(given, taken, strict=True)):
        source = source.at[0] if target is values else source
        copies.append(pltpu.make_async_copy(source, target, done.at[i]))
    for copy in copies:
        copy.start()
    for copy in copies[:2]:
        copy.wait()
    stride = PAIR + 2
    held_rows = halves(held[...].astype(BF16))
    counts = pick_row(ids, 0).astype(BF16)
    for chunk in range(out.shape[0] // stride):
        at = chunk * stride
        out[at : at + PAIR, :] = held_rows
        out[at + PAIR : at + stride, :] = counts
    for copy in copies[2:]:
        copy.wait()
    size = users.shape[0]
    packets[0][0:size, :] = users[:, :LANES].astype(BF16)
    packets[1][0:size, :] = users[:, LANES:].astype(BF16)
    theirs = 1 - lax.axis_index("pair")
    first = lane_side() == theirs
    slots = values.shape[0]
    for k in range(slots // 2):
        other = beside(values[k + slots // 2].astype(F32), theirs)
        at = size + k // 2 * LANES
        packets[k % 2][at : at + LANES, :] = jnp.where(first, values[k].astype(F32), other).astype(BF16)
    lane = lax.broadcasted_iota(jnp.int32, (16, LANES), 1)
    lists = jnp.where(lane == 2 * slots, count[0, 0], 0)
    for k in range(slots):
        lists = jnp.where(lane == k, rows[0, k], jnp.where(lane == slots + k, cols[0, k], lists))
    at = size + slots // 4 * LANES
    packets[0][at : at + 16, :] = lists.astype(F32).astype(BF16)


def lists_of(packet, slots):
    size = packet.shape[0]
    line = packet[size - 16 : size, :].astype(F32)[0:1]
    lane = lax.broadcasted_iota(jnp.int32, line.shape, 1)
    return [
        jnp.sum(jnp.where(lane == k, line, 0.0)).astype(jnp.int32) for k in range(2 * slots + 1)
    ]


def item_grads(users_bf, block, values, rows, cols, live, errors, owned, scale, add):
    slots, tile_u, tile_i = errors.shape
    for k in range(slots):
        row = pl.multiple_of(rows(k) * tile_u, tile_u)
        col = cols(k)
        user_tile = users_bf[pl.ds(row, tile_u), :]
        item_tile = block[pl.ds(pl.multiple_of(col * tile_i, tile_i), tile_i), :]
        scores = contract(user_tile, item_tile, (1, 1))
        there = k < live if owned is None else owned & (k < live)
        err = jnp.where(there, scores - values(k).astype(F32), 0.0).astype(BF16)
        errors[k] = err
        if scale is not None:
            err = err * jnp.asarray(scale, BF16)
        add(col, contract(err, user_tile, (0, 0)))


def user_grads(block, rows, cols, errors, grad_users):
    slots, tile_u, tile_i = errors.shape
    grad_users[...] = jnp.zeros_like(grad_users)
    for k in range(slots):
        row = pl.multiple_of(rows(k) * tile_u, tile_u)
        col = pl.multiple_of(cols(k) * tile_i, tile_i)
        grad_users[pl.ds(row, tile_u), :] += contract(errors[k], block[pl.ds(col, tile_i), :], (1, 0))


def at_step(ref, step):
    return lambda k: ref[step, k]


def from_list(scalars, first):
    return lambda k: scalars[first + k]


def pair_rows(chunk, side):
    return pl.ds(pl.multiple_of(chunk * 2 * ROWS + side * ROWS, ROWS), ROWS)


def first_kernel(
    got, users, packet, packet_too, values, rows, cols, count,
    sums, block, errors, their_errors, users_bf, their_users, grads,
):
    stride = PAIR + 2
    chunks = got.shape[0] // stride
    side = lax.axis_index("pair")
    slots, tile_u, tile_i = errors.shape
    block[...] = jnp.zeros_like(block)
    for chunk in range(chunks):
        at = chunk * stride
        block[pair_rows(chunk, side), :LANES] = got[at : at + ROWS, :]
        block[pair_rows(chunk, side), LANES:] = got[at + ROWS : at + PAIR, :]
    users_bf[...] = users[...].astype(BF16)
    grads[...] = jnp.zeros_like(grads)
    owned = lane_side() == side
    size = users.shape[0]
    their_users[:, :LANES] = packet[0:size, :]
    their_users[:, LANES:] = packet_too[0:size, :]
    theirs = lists_of(packet, slots)

    def their_values(k):
        at = size + k % (slots // 2) // 2 * tile_u
        shared = (packet, packet_too)[k % 2][at : at + tile_u, :].astype(F32)
        return shared if k < slots // 2 else beside(shared, 1 - side)

    def add(col, part):
        at = pl.multiple_of(col * part.shape[0], part.shape[0])
        grads[pl.ds(at, part.shape[0]), :] += part

    item_grads(
        users_bf, block, lambda k: values[0, k], at_step(rows, 0), at_step(cols, 0), count[0, 0],
        errors, owned, GRAD_SCALE, add,
    )
    item_grads(
        their_users, block, their_values, from_list(theirs, 0), from_list(theirs, slots),
        theirs[2 * slots], their_errors, owned, GRAD_SCALE, add,
    )
    for chunk in range(chunks):
        sums[chunk] = halves(grads[pair_rows(chunk, side), :])


def first_users_kernel(
    got, block, users, rows, cols, errors, packet, their_errors,
    users_out, their_grads, piece_out, their_piece, counts, packed, pieces, mine, grad_users,
):
    stride = PAIR + 2
    chunks = got.shape[0] // stride
    side = lax.axis_index("pair")
    for chunk in range(chunks):
        at = chunk * stride + PAIR
        counts[chunk : chunk + 1, :] = got[at : at + 2, :].astype(F32)[0:1]
        mine[chunk * ROWS : (chunk + 1) * ROWS, :] = block[pair_rows(chunk, side), :]
    shape = (chunks, ROWS, LANES)
    own = lax.broadcasted_iota(jnp.int32, shape, 1) == lax.broadcasted_iota(jnp.int32, shape, 2)
    weight = jnp.sum(jnp.where(own, counts[...][:, None, :], 0.0), axis=2, keepdims=True)
    plain = mine[...]
    left = (plain[:, :LANES].astype(F32).reshape(shape) * weight).reshape(-1, LANES)
    right = (plain[:, LANES:].astype(F32).reshape(shape) * weight).reshape(-1, LANES)
    high, low = split(jnp.concatenate([left, right], axis=1))
    put_packed(
        packed,
        jnp.concatenate([high, low], axis=0),
        jnp.concatenate([plain, plain], axis=0),
        GRAM_STRATUM_SCALE,
    )
    devices = pieces.shape[0]
    piece = packed.shape[0] // devices
    for device in range(devices):
        pieces[device, 0:piece, :] = packed[device * piece : (device + 1) * piece, :]
    me = lax.axis_index(INNER)
    piece_out[...] = pieces[me]
    their_piece[...] = pieces[me + 1 - 2 * side]
    slots = errors.shape[0]
    theirs = lists_of(packet, slots)
    user_grads(block, from_list(theirs, 0), from_list(theirs, slots), their_errors, their_grads)
    user_grads(block, at_step(rows, 0), at_step(cols, 0), errors, grad_users)
    users_out[...] = users[...] - LR_USER * grad_users[...]


def update(held, accum, gradient):
    accum = accum + gradient * gradient
    return held - LR_ITEM * gradient / jnp.sqrt(accum), accum


def pick_counts(ids_ref, step):
    row = lax.broadcasted_iota(jnp.int32, (8, LANES), 0)
    lane = lax.broadcasted_iota(jnp.int32, (8, LANES), 1)
    row = jnp.where(lane < LANES // 2, row, row + 8)
    counts = jnp.zeros((8, LANES), F32)
    for n in range(ids_ref.shape[1]):
        counts = counts + jnp.where(row == ids_ref[step, n], 1.0, 0.0)
    return counts


def item_kernel(got, held, accum, gram_piece, their_piece, ids, state, out):
    strata = out.shape[0]
    gradient = widths(jnp.sum(got[...], axis=0) * (1.0 / GRAD_SCALE))
    new, state[ROWS:, :] = update(held[...], accum[...], gradient)
    state[0:ROWS, :] = new
    items = halves(new.astype(BF16).astype(F32)) * ITEM_SCALE
    sent = jnp.concatenate([items, pick_counts(ids, 1), gram_piece[...] + their_piece[...]], axis=0)
    out[...] = jnp.broadcast_to(sent[None], (strata,) + sent.shape)


def gather_kernel(total, met, out, packed):
    strata = met.shape[0]
    chunks = lax.axis_size(INNER)
    piece = packed.shape[0] // chunks
    stride = PAIR + 2 * piece
    after = lax.rem(lax.axis_index("stratum") + 1, strata)
    items = met[pl.ds(after, 1), 0:PAIR, :][0]
    full = jnp.sum(met[:, 40:, :], axis=0)[0:piece] * (GRAM_SCALE / GRAM_STRATUM_SCALE / total)
    counts = jnp.concatenate([met[-1:, 32:40, :], met[:-1, 32:40, :]], axis=0)
    counts = jnp.concatenate([counts[:, :, 0:1], counts[:, :, 64:65]], axis=1)
    rows = [met[:, 0:ROWS, :] * (1.0 / ITEM_SCALE), met[:, ROWS:PAIR, :] * (1.0 / ITEM_SCALE)]
    weighed = jnp.concatenate([(r * counts).reshape(-1, LANES) for r in rows], axis=1)
    plain = jnp.concatenate([r.reshape(-1, LANES) for r in rows], axis=1).astype(BF16)
    high, low = split(weighed)
    put_packed(
        packed,
        jnp.concatenate([high, low], axis=0),
        jnp.concatenate([plain, plain], axis=0),
        GRAM_INNER_SCALE,
    )
    for chunk in range(chunks):
        at = chunk * stride
        out[at : at + PAIR, :] = items
        out[at + PAIR : at + PAIR + piece, :] = full
        out[at + PAIR + piece : at + stride, :] = packed[chunk * piece : (chunk + 1) * piece, :]


def second_kernel(
    total, got, users, mid, rest, values, rows, cols, count, sums, mid_out, block, errors, packed, users_bf, grads
):
    chunks = block.shape[0] // ROWS
    piece = packed.shape[0] // chunks
    stride = PAIR + 2 * piece
    full = jnp.zeros((piece, LANES), F32)
    for chunk in range(chunks):
        to, at = chunk * ROWS, chunk * stride
        block[to : to + ROWS, :LANES] = (got[at : at + ROWS, :] * (1.0 / ITEM_SCALE)).astype(BF16)
        block[to : to + ROWS, LANES:] = (got[at + ROWS : at + PAIR, :] * (1.0 / ITEM_SCALE)).astype(BF16)
        packed[chunk * piece : (chunk + 1) * piece, :] = got[at + PAIR : at + PAIR + piece, :]
        full = full + got[at + PAIR + piece : at + stride, :]
    gram = whole_gram(packed, 1.0 / GRAM_SCALE)
    part = mid[...] - (LR_USER / REST_SCALE) * rest[...]
    now = part - (LR_USER * LAMBDA) * times_gram(users[...], gram)
    mid_out[...] = now
    users_bf[...] = now.astype(BF16)
    grads[...] = jnp.zeros_like(grads)

    def add(col, part):
        at = pl.multiple_of(col * part.shape[0], part.shape[0])
        grads[pl.ds(at, part.shape[0]), :] += part

    item_grads(
        users_bf, block, lambda k: values[1, k], at_step(rows, 1), at_step(cols, 1), count[1, 0],
        errors, None, None, add,
    )
    full = full * (GRAM_SCALE / GRAM_INNER_SCALE / total)
    for chunk in range(chunks):
        at = chunk * (PAIR + piece)
        raw = halves(grads[chunk * ROWS : (chunk + 1) * ROWS, :])
        root = jnp.sqrt(jnp.abs(raw)) * ROOT_SCALE
        sums[at : at + PAIR, :] = jnp.where(raw < 0.0, -root, root)
        sums[at + PAIR : at + PAIR + piece, :] = full


def second_users_kernel(block, now, rows, cols, errors, users_out, grad_users):
    user_grads(block, at_step(rows, 1), at_step(cols, 1), errors, grad_users)
    users_out[...] = now[...] - LR_USER * grad_users[...]


def last_items_kernel(chunks, got, state, out):
    stride = got.shape[0] // chunks
    total = jnp.zeros((PAIR, LANES), F32)
    for chunk in range(chunks):
        root = got[chunk * stride : chunk * stride + PAIR, :]
        total = total + root * jnp.abs(root)
    out[0:ROWS, :], out[ROWS:, :] = update(
        state[0:ROWS, :], state[ROWS:, :], widths(total * ROOT_SCALE**-2)
    )


def last_users_kernel(chunks, got, users, mid, out, packed):
    stride = got.shape[0] // chunks
    piece = stride - PAIR
    for chunk in range(chunks):
        packed[chunk * piece : (chunk + 1) * piece, :] = got[chunk * stride + PAIR : (chunk + 1) * stride, :]
    gram = whole_gram(packed, 1.0 / GRAM_SCALE)
    out[...] = users[...] - (LR_USER * LAMBDA) * times_gram(mid[...], gram)


def call(kernel, out_shape, specs, *args, scratch=(), vmem=44):
    return pl.pallas_call(
        kernel,
        out_shape=out_shape,
        in_specs=specs,
        out_specs=jax.tree.map(lambda _: pl.BlockSpec(memory_space=VMEM), out_shape),
        scratch_shapes=scratch,
        compiler_params=pltpu.CompilerParams(vmem_limit_bytes=vmem * 2**20),
    )(*args)


def exchanged(x, axis):
    return lax.all_to_all(x, axis, 0, 0, tiled=True)


def chunks_exchanged(flat, axis):
    paired = flat.reshape(lax.axis_size(axis), -1, 2, LANES)
    return exchanged(paired, axis).reshape(flat.shape)


def swapped(x):
    return lax.ppermute(x, "pair", [(0, 1), (1, 0)])


def shards(
    user_factors, item_factors, item_accum, tile_values, tile_rows, tile_cols, tile_count, neg_ids
):
    strata = lax.axis_size("stratum")
    inners = lax.axis_size(INNER)
    group = lax.axis_size(GROUP)
    rank = item_factors.shape[1]
    total = float(strata * inners * neg_ids.shape[1])
    piece = piece_rows(inners)
    padded = -(-piece // 8) * 8
    onward = [((s + 1) % strata, s) for s in range(strata)]
    vm = pl.BlockSpec(memory_space=VMEM)
    sm = pl.BlockSpec(memory_space=SMEM)
    shape = jax.ShapeDtypeStruct
    users_shape = shape(user_factors.shape, F32)
    users_f32 = pltpu.VMEM(user_factors.shape, F32)
    users_bf = pltpu.VMEM(user_factors.shape, BF16)
    state_shape = shape((PAIR, rank), F32)
    block_shape = shape((inners * ROWS, rank), BF16)
    errors_shape = shape(tile_values.shape[1:], BF16)
    piece_shape = shape((padded, LANES), F32)
    packed = pltpu.VMEM((inners * piece, LANES), F32)

    slots = tile_values.shape[1]
    packet_rows = user_factors.shape[0] + slots // 4 * LANES
    sent, packet, packet_too = call(
        start_kernel,
        (
            shape((group * (PAIR + 2), LANES), BF16),
            shape((packet_rows + 16, LANES), BF16),
            shape((packet_rows, LANES), BF16),
        ),
        [pl.BlockSpec(memory_space=pltpu.HBM)] * 7,
        item_factors, neg_ids, user_factors, tile_values, tile_rows, tile_cols, tile_count,
        scratch=[
            pltpu.VMEM(item_factors.shape, F32),
            pltpu.SMEM(neg_ids.shape, jnp.int32),
            users_f32,
            pltpu.VMEM(tile_values.shape[1:], BF16),
            pltpu.SMEM(tile_rows.shape, jnp.int32),
            pltpu.SMEM(tile_cols.shape, jnp.int32),
            pltpu.SMEM(tile_count.shape, jnp.int32),
            pltpu.SemaphoreType.DMA((7,)),
        ],
        vmem=62,
    )
    got = chunks_exchanged(sent, GROUP)
    packet, packet_too = swapped(packet), swapped(packet_too)
    sums, block, errors, their_errors = call(
        first_kernel,
        (shape((group, PAIR, LANES), F32), block_shape, errors_shape, errors_shape),
        [vm, vm, vm, vm, vm, sm, sm, sm],
        got, user_factors, packet, packet_too, tile_values, tile_rows, tile_cols, tile_count,
        scratch=[users_bf, users_bf, pltpu.VMEM(block_shape.shape, F32)],
    )
    sums = exchanged(sums.astype(F16), GROUP).astype(F32)
    mid, rest, gram_piece, their_piece = call(
        first_users_kernel,
        (users_shape, users_shape, piece_shape, piece_shape),
        [vm, vm, vm, sm, sm, vm, vm, vm],
        got, block, user_factors, tile_rows, tile_cols, errors, packet, their_errors,
        scratch=[
            pltpu.VMEM((group, LANES), F32),
            packed,
            pltpu.VMEM((inners, padded, LANES), F32),
            pltpu.VMEM((group * ROWS, rank), BF16),
            users_f32,
        ],
    )
    their_piece = swapped(their_piece)
    rest = swapped((rest * REST_SCALE).astype(F16))
    state, sent = call(
        item_kernel,
        (state_shape, shape((strata, PAIR + 8 + padded, LANES), F32)),
        [vm, vm, vm, vm, vm, sm],
        sums, item_factors, item_accum, gram_piece, their_piece, neg_ids,
    )
    met = exchanged(sent.astype(F16), "stratum")
    met = met.astype(F32)
    sent = call(
        functools.partial(gather_kernel, total),
        shape((inners * (PAIR + 2 * piece), LANES), F32),
        [vm],
        met,
        scratch=[packed],
    ).astype(F16)
    got = chunks_exchanged(sent, INNER).astype(F32)
    sums, mid, block, errors = call(
        functools.partial(second_kernel, total),
        (shape((inners * (PAIR + piece), LANES), F32), users_shape, block_shape, errors_shape),
        [vm, vm, vm, vm, vm, sm, sm, sm],
        got, user_factors, mid, rest.astype(F32), tile_values, tile_rows, tile_cols, tile_count,
        scratch=[packed, users_bf, pltpu.VMEM(block_shape.shape, F32)],
    )
    sums, state = lax.optimization_barrier((sums.astype(F16), state))
    state = lax.ppermute(state, "stratum", onward)
    got = chunks_exchanged(sums, INNER).astype(F32)
    users = call(
        second_users_kernel, users_shape, [vm, vm, sm, sm, vm],
        block, mid, tile_rows, tile_cols, errors, scratch=[users_f32],
    )
    state = call(functools.partial(last_items_kernel, inners), state_shape, [vm, vm], got, state)
    state = lax.ppermute(state, "stratum", onward)
    users = call(
        functools.partial(last_users_kernel, inners), users_shape, [vm, vm, vm],
        got, users, mid, scratch=[packed],
    )
    return (users, state[:ROWS], state[ROWS:])


def solution(mesh):
    strata, inners = mesh.devices.shape
    fine = jax.sharding.Mesh(
        mesh.devices.reshape(strata, inners // 4, 2, 2), ("stratum",) + INNER
    )
    every = ("stratum",) + INNER
    devices = P(every, None)
    slots = P(None, every)
    return jax.shard_map(
        shards,
        mesh=fine,
        in_specs=(
            devices,
            devices,
            devices,
            P(None, every, None, None),
            slots,
            slots,
            slots,
            slots,
        ),
        out_specs=(devices, devices, devices),
        check_vma=False,
    )
```

```python
import functools

import jax
import jax.numpy as jnp
from jax import lax
from jax.experimental import pallas as pl
from jax.experimental.pallas import tpu as pltpu
from jax.sharding import PartitionSpec as P

LR_USER = 0.005
LR_ITEM = 0.05
LAMBDA = 64.0

LANES = 128
F32 = jnp.float32
BF16 = jnp.bfloat16
F16 = jnp.float16

GRAD_SCALE = 2.0**-7
REST_SCALE = 2.0**-6
ROOT_SCALE = 2.0**-9
ITEM_SCALE = 2.0**12
GRAM_SCALE = 2.0**12
GRAM_STRATUM_SCALE = 2.0**5
GRAM_INNER_SCALE = 2.0**6

ROWS = 16
PAIR = 2 * ROWS
PACKED = 2 * LANES + 1

GROUP = ("far", "near")
INNER = ("far", "near", "pair")

VMEM = pltpu.VMEM
SMEM = pltpu.SMEM


def contract(a, b, dims):
    return lax.dot_general(a, b, ((dims[:1], dims[1:]), ((), ())), preferred_element_type=F32)


def halves(x):
    return jnp.concatenate([x[:, :LANES], x[:, LANES:]], axis=0)


def widths(x):
    rows = x.shape[0] // 2
    return jnp.concatenate([x[:rows], x[rows:]], axis=1)


def piece_rows(chunks):
    return 2 * (-(-PACKED // (2 * chunks)))


def packed_gram(weighed, rows):
    gram = contract(weighed, rows, (0, 0))
    upper, beside, lower = gram[:LANES, :LANES], gram[:LANES, LANES:], gram[LANES:, LANES:]
    row = lax.broadcasted_iota(jnp.int32, (LANES, LANES), 0)
    col = lax.broadcasted_iota(jnp.int32, (LANES, LANES), 1)
    both = jnp.where(col >= row, upper, lower)
    return both, beside, jnp.sum(jnp.where(col == row, lower, 0.0), axis=0, keepdims=True)


def put_packed(packed, weighed, rows, scale):
    both, beside, diagonal = packed_gram(weighed, rows)
    packed[...] = jnp.zeros_like(packed)
    packed[0:LANES, :] = both * scale
    packed[LANES : 2 * LANES, :] = beside * scale
    packed[2 * LANES : 2 * LANES + 1, :] = diagonal * scale


def whole_gram(packed, scale):
    both = packed[0:LANES, :] * scale
    beside = packed[LANES : 2 * LANES, :] * scale
    diagonal = packed[2 * LANES : 2 * LANES + 1, :] * scale
    row = lax.broadcasted_iota(jnp.int32, (LANES, LANES), 0)
    col = lax.broadcasted_iota(jnp.int32, (LANES, LANES), 1)
    above = jnp.where(col > row, both, 0.0)
    below = jnp.where(col < row, both, 0.0)
    upper = above + above.T + jnp.where(col == row, both, 0.0)
    lower = below + below.T + jnp.where(col == row, diagonal, 0.0)
    return jnp.concatenate(
        [jnp.concatenate([upper, beside], axis=1), jnp.concatenate([beside.T, lower], axis=1)], axis=0
    )


def split(x):
    high = x.astype(BF16)
    return high, (x - high.astype(F32)).astype(BF16)


def times_gram(users, gram):
    uh, ul = split(users)
    gh, gl = split(gram)
    return contract(uh, gh, (1, 0)) + (contract(ul, gh, (1, 0)) + contract(uh, gl, (1, 0)))


def pick_row(ids_ref, step):
    row = lax.broadcasted_iota(jnp.int32, (2, LANES), 0)
    lane = lax.broadcasted_iota(jnp.int32, (2, LANES), 1)
    counts = jnp.zeros((2, LANES), F32)
    for n in range(ids_ref.shape[1]):
        counts = counts + jnp.where((lane == ids_ref[step, n]) & (row == 0), 1.0, 0.0)
    return counts


def lane_side():
    lane = lax.broadcasted_iota(jnp.int32, (LANES, LANES), 1)
    return lax.rem(lax.div(lane, ROWS), 2)


def beside(x, side):
    return jnp.where(side == 0, pltpu.roll(x, ROWS, 1), pltpu.roll(x, LANES - ROWS, 1))


def start_kernel(*refs):
    given, (out, *packets), taken, done = refs[:7], refs[7:10], refs[10:17], refs[17]
    held, ids, users, values, rows, cols, count = taken
    copies = []
    for i, (source, target) in enumerate(zip(given, taken, strict=True)):
        source = source.at[0] if target is values else source
        copies.append(pltpu.make_async_copy(source, target, done.at[i]))
    for copy in copies:
        copy.start()
    for copy in copies[:2]:
        copy.wait()
    stride = PAIR + 2
    held_rows = halves(held[...].astype(BF16))
    counts = pick_row(ids, 0).astype(BF16)
    for chunk in range(out.shape[0] // stride):
        at = chunk * stride
        out[at : at + PAIR, :] = held_rows
        out[at + PAIR : at + stride, :] = counts
    for copy in copies[2:]:
        copy.wait()
    size = users.shape[0]
    packets[0][0:size, :] = users[:, :LANES].astype(BF16)
    packets[1][0:size, :] = users[:, LANES:].astype(BF16)
    theirs = 1 - lax.axis_index("pair")
    first = lane_side() == theirs
    slots = values.shape[0]
    for k in range(slots // 2):
        other = beside(values[k + slots // 2].astype(F32), theirs)
        at = size + k // 2 * LANES
        packets[k % 2][at : at + LANES, :] = jnp.where(first, values[k].astype(F32), other).astype(BF16)
    lane = lax.broadcasted_iota(jnp.int32, (16, LANES), 1)
    lists = jnp.where(lane == 2 * slots, count[0], 0)
    for k in range(slots):
        lists = jnp.where(lane == k, rows[0, k], jnp.where(lane == slots + k, cols[0, k], lists))
    at = size + slots // 4 * LANES
    packets[0][at : at + 16, :] = lists.astype(F32).astype(BF16)


def lists_of(packet, slots):
    size = packet.shape[0]
    line = packet[size - 16 : size, :].astype(F32)[0:1]
    lane = lax.broadcasted_iota(jnp.int32, line.shape, 1)
    return [
        jnp.sum(jnp.where(lane == k, line, 0.0)).astype(jnp.int32) for k in range(2 * slots + 1)
    ]


def item_grads(users_bf, block, values, rows, cols, live, errors, owned, scale, add):
    slots, tile_u, tile_i = errors.shape
    for k in range(slots):
        row = pl.multiple_of(rows(k) * tile_u, tile_u)
        col = cols(k)
        user_tile = users_bf[pl.ds(row, tile_u), :]
        item_tile = block[pl.ds(pl.multiple_of(col * tile_i, tile_i), tile_i), :]
        scores = contract(user_tile, item_tile, (1, 1))
        there = k < live if owned is None else owned & (k < live)
        err = jnp.where(there, scores - values(k).astype(F32), 0.0).astype(BF16)
        errors[k] = err
        if scale is not None:
            err = err * jnp.asarray(scale, BF16)
        add(col, contract(err, user_tile, (0, 0)))


def user_grads(block, rows, cols, errors, grad_users):
    slots, tile_u, tile_i = errors.shape
    grad_users[...] = jnp.zeros_like(grad_users)
    for k in range(slots):
        row = pl.multiple_of(rows(k) * tile_u, tile_u)
        col = pl.multiple_of(cols(k) * tile_i, tile_i)
        grad_users[pl.ds(row, tile_u), :] += contract(errors[k], block[pl.ds(col, tile_i), :], (1, 0))


def at_step(ref, step):
    return lambda k: ref[step, k]


def from_list(scalars, first):
    return lambda k: scalars[first + k]


def pair_rows(chunk, side):
    return pl.ds(pl.multiple_of(chunk * 2 * ROWS + side * ROWS, ROWS), ROWS)


def first_kernel(
    got, users, packet, packet_too, values, rows, cols, count,
    sums, block, errors, their_errors, users_bf, their_users, grads,
):
    stride = PAIR + 2
    chunks = got.shape[0] // stride
    side = lax.axis_index("pair")
    slots, tile_u, tile_i = errors.shape
    block[...] = jnp.zeros_like(block)
    for chunk in range(chunks):
        at = chunk * stride
        block[pair_rows(chunk, side), :LANES] = got[at : at + ROWS, :]
        block[pair_rows(chunk, side), LANES:] = got[at + ROWS : at + PAIR, :]
    users_bf[...] = users[...].astype(BF16)
    grads[...] = jnp.zeros_like(grads)
    owned = lane_side() == side
    size = users.shape[0]
    their_users[:, :LANES] = packet[0:size, :]
    their_users[:, LANES:] = packet_too[0:size, :]
    theirs = lists_of(packet, slots)

    def their_values(k):
        at = size + k % (slots // 2) // 2 * tile_u
        shared = (packet, packet_too)[k % 2][at : at + tile_u, :].astype(F32)
        return shared if k < slots // 2 else beside(shared, 1 - side)

    def add(col, part):
        at = pl.multiple_of(col * part.shape[0], part.shape[0])
        grads[pl.ds(at, part.shape[0]), :] += part

    item_grads(
        users_bf, block, lambda k: values[0, k], at_step(rows, 0), at_step(cols, 0), count[0],
        errors, owned, GRAD_SCALE, add,
    )
    item_grads(
        their_users, block, their_values, from_list(theirs, 0), from_list(theirs, slots),
        theirs[2 * slots], their_errors, owned, GRAD_SCALE, add,
    )
    for chunk in range(chunks):
        sums[chunk] = halves(grads[pair_rows(chunk, side), :])


def first_users_kernel(
    got, block, users, rows, cols, errors, packet, their_errors,
    users_out, their_grads, piece_out, their_piece, counts, packed, pieces, mine, grad_users,
):
    stride = PAIR + 2
    chunks = got.shape[0] // stride
    side = lax.axis_index("pair")
    for chunk in range(chunks):
        at = chunk * stride + PAIR
        counts[chunk : chunk + 1, :] = got[at : at + 2, :].astype(F32)[0:1]
        mine[chunk * ROWS : (chunk + 1) * ROWS, :] = block[pair_rows(chunk, side), :]
    shape = (chunks, ROWS, LANES)
    own = lax.broadcasted_iota(jnp.int32, shape, 1) == lax.broadcasted_iota(jnp.int32, shape, 2)
    weight = jnp.sum(jnp.where(own, counts[...][:, None, :], 0.0), axis=2, keepdims=True)
    plain = mine[...]
    left = (plain[:, :LANES].astype(F32).reshape(shape) * weight).reshape(-1, LANES)
    right = (plain[:, LANES:].astype(F32).reshape(shape) * weight).reshape(-1, LANES)
    high, low = split(jnp.concatenate([left, right], axis=1))
    put_packed(
        packed,
        jnp.concatenate([high, low], axis=0),
        jnp.concatenate([plain, plain], axis=0),
        GRAM_STRATUM_SCALE,
    )
    devices = pieces.shape[0]
    piece = packed.shape[0] // devices
    for device in range(devices):
        pieces[device, 0:piece, :] = packed[device * piece : (device + 1) * piece, :]
    me = lax.axis_index(INNER)
    piece_out[...] = pieces[me]
    their_piece[...] = pieces[me + 1 - 2 * side]
    slots = errors.shape[0]
    theirs = lists_of(packet, slots)
    user_grads(block, from_list(theirs, 0), from_list(theirs, slots), their_errors, their_grads)
    user_grads(block, at_step(rows, 0), at_step(cols, 0), errors, grad_users)
    users_out[...] = users[...] - LR_USER * grad_users[...]


def update(held, accum, gradient):
    accum = accum + gradient * gradient
    return held - LR_ITEM * gradient / jnp.sqrt(accum), accum


def pick_counts(ids_ref, step):
    row = lax.broadcasted_iota(jnp.int32, (8, LANES), 0)
    lane = lax.broadcasted_iota(jnp.int32, (8, LANES), 1)
    row = jnp.where(lane < LANES // 2, row, row + 8)
    counts = jnp.zeros((8, LANES), F32)
    for n in range(ids_ref.shape[1]):
        counts = counts + jnp.where(row == ids_ref[step, n], 1.0, 0.0)
    return counts


def item_kernel(got, held, accum, gram_piece, their_piece, ids, state, out):
    strata = out.shape[0]
    gradient = widths(jnp.sum(got[...], axis=0) * (1.0 / GRAD_SCALE))
    new, state[ROWS:, :] = update(held[...], accum[...], gradient)
    state[0:ROWS, :] = new
    items = halves(new.astype(BF16).astype(F32)) * ITEM_SCALE
    sent = jnp.concatenate([items, pick_counts(ids, 1), gram_piece[...] + their_piece[...]], axis=0)
    out[...] = jnp.broadcast_to(sent[None], (strata,) + sent.shape)


def gather_kernel(total, met, out, packed):
    strata = met.shape[0]
    chunks = lax.axis_size(INNER)
    piece = packed.shape[0] // chunks
    stride = PAIR + 2 * piece
    after = lax.rem(lax.axis_index("stratum") + 1, strata)
    items = met[pl.ds(after, 1), 0:PAIR, :][0]
    full = jnp.sum(met[:, 40:, :], axis=0)[0:piece] * (GRAM_SCALE / GRAM_STRATUM_SCALE / total)
    counts = jnp.concatenate([met[-1:, 32:40, :], met[:-1, 32:40, :]], axis=0)
    counts = jnp.concatenate([counts[:, :, 0:1], counts[:, :, 64:65]], axis=1)
    rows = [met[:, 0:ROWS, :] * (1.0 / ITEM_SCALE), met[:, ROWS:PAIR, :] * (1.0 / ITEM_SCALE)]
    weighed = jnp.concatenate([(r * counts).reshape(-1, LANES) for r in rows], axis=1)
    plain = jnp.concatenate([r.reshape(-1, LANES) for r in rows], axis=1).astype(BF16)
    high, low = split(weighed)
    put_packed(
        packed,
        jnp.concatenate([high, low], axis=0),
        jnp.concatenate([plain, plain], axis=0),
        GRAM_INNER_SCALE,
    )
    for chunk in range(chunks):
        at = chunk * stride
        out[at : at + PAIR, :] = items
        out[at + PAIR : at + PAIR + piece, :] = full
        out[at + PAIR + piece : at + stride, :] = packed[chunk * piece : (chunk + 1) * piece, :]


def second_kernel(
    total, got, users, mid, rest, values, rows, cols, count, sums, mid_out, block, errors, packed, users_bf, grads
):
    chunks = block.shape[0] // ROWS
    piece = packed.shape[0] // chunks
    stride = PAIR + 2 * piece
    full = jnp.zeros((piece, LANES), F32)
    for chunk in range(chunks):
        to, at = chunk * ROWS, chunk * stride
        block[to : to + ROWS, :LANES] = (got[at : at + ROWS, :] * (1.0 / ITEM_SCALE)).astype(BF16)
        block[to : to + ROWS, LANES:] = (got[at + ROWS : at + PAIR, :] * (1.0 / ITEM_SCALE)).astype(BF16)
        packed[chunk * piece : (chunk + 1) * piece, :] = got[at + PAIR : at + PAIR + piece, :]
        full = full + got[at + PAIR + piece : at + stride, :]
    gram = whole_gram(packed, 1.0 / GRAM_SCALE)
    part = mid[...] - (LR_USER / REST_SCALE) * rest[...]
    now = part - (LR_USER * LAMBDA) * times_gram(users[...], gram)
    mid_out[...] = now
    users_bf[...] = now.astype(BF16)
    grads[...] = jnp.zeros_like(grads)

    def add(col, part):
        at = pl.multiple_of(col * part.shape[0], part.shape[0])
        grads[pl.ds(at, part.shape[0]), :] += part

    item_grads(
        users_bf, block, lambda k: values[1, k], at_step(rows, 1), at_step(cols, 1), count[1],
        errors, None, None, add,
    )
    full = full * (GRAM_SCALE / GRAM_INNER_SCALE / total)
    for chunk in range(chunks):
        at = chunk * (PAIR + piece)
        raw = halves(grads[chunk * ROWS : (chunk + 1) * ROWS, :])
        root = jnp.sqrt(jnp.abs(raw)) * ROOT_SCALE
        sums[at : at + PAIR, :] = jnp.where(raw < 0.0, -root, root)
        sums[at + PAIR : at + PAIR + piece, :] = full


def second_users_kernel(block, now, rows, cols, errors, users_out, grad_users):
    user_grads(block, at_step(rows, 1), at_step(cols, 1), errors, grad_users)
    users_out[...] = now[...] - LR_USER * grad_users[...]


def last_items_kernel(chunks, got, state, out):
    stride = got.shape[0] // chunks
    total = jnp.zeros((PAIR, LANES), F32)
    for chunk in range(chunks):
        root = got[chunk * stride : chunk * stride + PAIR, :]
        total = total + root * jnp.abs(root)
    out[0:ROWS, :], out[ROWS:, :] = update(
        state[0:ROWS, :], state[ROWS:, :], widths(total * ROOT_SCALE**-2)
    )


def last_users_kernel(chunks, got, users, mid, out, packed):
    stride = got.shape[0] // chunks
    piece = stride - PAIR
    for chunk in range(chunks):
        packed[chunk * piece : (chunk + 1) * piece, :] = got[chunk * stride + PAIR : (chunk + 1) * stride, :]
    gram = whole_gram(packed, 1.0 / GRAM_SCALE)
    out[...] = users[...] - (LR_USER * LAMBDA) * times_gram(mid[...], gram)


def call(kernel, out_shape, specs, *args, scratch=(), vmem=44):
    return pl.pallas_call(
        kernel,
        out_shape=out_shape,
        in_specs=specs,
        out_specs=jax.tree.map(lambda _: pl.BlockSpec(memory_space=VMEM), out_shape),
        scratch_shapes=scratch,
        compiler_params=pltpu.CompilerParams(vmem_limit_bytes=vmem * 2**20),
    )(*args)


def exchanged(x, axis):
    return lax.all_to_all(x, axis, 0, 0, tiled=True)


def chunks_exchanged(flat, axis):
    paired = flat.reshape(lax.axis_size(axis), -1, 2, LANES)
    return exchanged(paired, axis).reshape(flat.shape)


def swapped(x):
    return lax.ppermute(x, "pair", [(0, 1), (1, 0)])


def shards(
    user_factors, item_factors, item_accum, tile_values, tile_rows, tile_cols, tile_count, neg_ids
):
    strata = lax.axis_size("stratum")
    inners = lax.axis_size(INNER)
    group = lax.axis_size(GROUP)
    rank = item_factors.shape[1]
    total = float(strata * inners * neg_ids.shape[1])
    piece = piece_rows(inners)
    padded = -(-piece // 8) * 8
    onward = [((s + 1) % strata, s) for s in range(strata)]
    vm = pl.BlockSpec(memory_space=VMEM)
    sm = pl.BlockSpec(memory_space=SMEM)
    shape = jax.ShapeDtypeStruct
    users_shape = shape(user_factors.shape, F32)
    users_f32 = pltpu.VMEM(user_factors.shape, F32)
    users_bf = pltpu.VMEM(user_factors.shape, BF16)
    state_shape = shape((PAIR, rank), F32)
    block_shape = shape((inners * ROWS, rank), BF16)
    errors_shape = shape(tile_values.shape[1:], BF16)
    piece_shape = shape((padded, LANES), F32)
    packed = pltpu.VMEM((inners * piece, LANES), F32)

    slots = tile_values.shape[1]
    tile_count = tile_count.reshape(-1)
    packet_rows = user_factors.shape[0] + slots // 4 * LANES
    sent, packet, packet_too = call(
        start_kernel,
        (
            shape((group * (PAIR + 2), LANES), BF16),
            shape((packet_rows + 16, LANES), BF16),
            shape((packet_rows, LANES), BF16),
        ),
        [pl.BlockSpec(memory_space=pltpu.HBM)] * 7,
        item_factors, neg_ids, user_factors, tile_values, tile_rows, tile_cols, tile_count,
        scratch=[
            pltpu.VMEM(item_factors.shape, F32),
            pltpu.SMEM(neg_ids.shape, jnp.int32),
            users_f32,
            pltpu.VMEM(tile_values.shape[1:], BF16),
            pltpu.SMEM(tile_rows.shape, jnp.int32),
            pltpu.SMEM(tile_cols.shape, jnp.int32),
            pltpu.SMEM(tile_count.shape, jnp.int32),
            pltpu.SemaphoreType.DMA((7,)),
        ],
        vmem=62,
    )
    got = chunks_exchanged(sent, GROUP)
    packet, packet_too = swapped(packet), swapped(packet_too)
    sums, block, errors, their_errors = call(
        first_kernel,
        (shape((group, PAIR, LANES), F32), block_shape, errors_shape, errors_shape),
        [vm, vm, vm, vm, vm, sm, sm, sm],
        got, user_factors, packet, packet_too, tile_values, tile_rows, tile_cols, tile_count,
        scratch=[users_bf, users_bf, pltpu.VMEM(block_shape.shape, F32)],
    )
    sums = exchanged(sums.astype(F16), GROUP).astype(F32)
    mid, rest, gram_piece, their_piece = call(
        first_users_kernel,
        (users_shape, users_shape, piece_shape, piece_shape),
        [vm, vm, vm, sm, sm, vm, vm, vm],
        got, block, user_factors, tile_rows, tile_cols, errors, packet, their_errors,
        scratch=[
            pltpu.VMEM((group, LANES), F32),
            packed,
            pltpu.VMEM((inners, padded, LANES), F32),
            pltpu.VMEM((group * ROWS, rank), BF16),
            users_f32,
        ],
    )
    their_piece = swapped(their_piece)
    rest = swapped((rest * REST_SCALE).astype(F16))
    state, sent = call(
        item_kernel,
        (state_shape, shape((strata, PAIR + 8 + padded, LANES), F32)),
        [vm, vm, vm, vm, vm, sm],
        sums, item_factors, item_accum, gram_piece, their_piece, neg_ids,
    )
    met = exchanged(sent.astype(F16), "stratum")
    met = met.astype(F32)
    sent = call(
        functools.partial(gather_kernel, total),
        shape((inners * (PAIR + 2 * piece), LANES), F32),
        [vm],
        met,
        scratch=[packed],
    ).astype(F16)
    got = chunks_exchanged(sent, INNER)
    state = lax.ppermute(state, "stratum", onward)
    got, rest, state = lax.optimization_barrier((got, rest, state))
    got = got.astype(F32)
    sums, mid, block, errors = call(
        functools.partial(second_kernel, total),
        (shape((inners * (PAIR + piece), LANES), F32), users_shape, block_shape, errors_shape),
        [vm, vm, vm, vm, vm, sm, sm, sm],
        got, user_factors, mid, rest.astype(F32), tile_values, tile_rows, tile_cols, tile_count,
        scratch=[packed, users_bf, pltpu.VMEM(block_shape.shape, F32)],
    )
    got = chunks_exchanged(sums.astype(F16), INNER).astype(F32)
    users = call(
        second_users_kernel, users_shape, [vm, vm, sm, sm, vm],
        block, mid, tile_rows, tile_cols, errors, scratch=[users_f32],
    )
    state = call(functools.partial(last_items_kernel, inners), state_shape, [vm, vm], got, state)
    state = lax.ppermute(state, "stratum", onward)
    users = call(
        functools.partial(last_users_kernel, inners), users_shape, [vm, vm, vm],
        got, users, mid, scratch=[packed],
    )
    return (users, state[:ROWS], state[ROWS:])


def solution(mesh):
    strata, inners = mesh.devices.shape
    fine = jax.sharding.Mesh(
        mesh.devices.reshape(strata, inners // 4, 2, 2), ("stratum",) + INNER
    )
    every = ("stratum",) + INNER
    devices = P(every, None)
    slots = P(None, every)
    return jax.shard_map(
        shards,
        mesh=fine,
        in_specs=(
            devices,
            devices,
            devices,
            P(None, every, None, None),
            slots,
            slots,
            slots,
            slots,
        ),
        out_specs=(devices, devices, devices),
        check_vma=False,
    )
```

```python
import functools

import jax
import jax.numpy as jnp
from jax import lax
from jax.experimental import pallas as pl
from jax.experimental.pallas import tpu as pltpu
from jax.sharding import PartitionSpec as P

LR_USER = 0.005
LR_ITEM = 0.05
LAMBDA = 64.0

LANES = 128
F32 = jnp.float32
BF16 = jnp.bfloat16
F16 = jnp.float16

GRAD_SCALE = 2.0**-7
REST_SCALE = 2.0**-6
ROOT_SCALE = 2.0**-9
ITEM_SCALE = 2.0**12
GRAM_SCALE = 2.0**12
GRAM_STRATUM_SCALE = 2.0**5
GRAM_INNER_SCALE = 2.0**6

ROWS = 16
PAIR = 2 * ROWS
PACKED = 2 * LANES + 1

GROUP = ("far", "near")
INNER = ("far", "near", "pair")

VMEM = pltpu.VMEM
SMEM = pltpu.SMEM


def contract(a, b, dims):
    return lax.dot_general(a, b, ((dims[:1], dims[1:]), ((), ())), preferred_element_type=F32)


def halves(x):
    return jnp.concatenate([x[:, :LANES], x[:, LANES:]], axis=0)


def widths(x):
    rows = x.shape[0] // 2
    return jnp.concatenate([x[:rows], x[rows:]], axis=1)


def piece_rows(chunks):
    return 2 * (-(-PACKED // (2 * chunks)))


def packed_gram(weighed, rows):
    gram = contract(weighed, rows, (0, 0))
    upper, beside, lower = gram[:LANES, :LANES], gram[:LANES, LANES:], gram[LANES:, LANES:]
    row = lax.broadcasted_iota(jnp.int32, (LANES, LANES), 0)
    col = lax.broadcasted_iota(jnp.int32, (LANES, LANES), 1)
    both = jnp.where(col >= row, upper, lower)
    return both, beside, jnp.sum(jnp.where(col == row, lower, 0.0), axis=0, keepdims=True)


def put_packed(packed, weighed, rows, scale):
    both, beside, diagonal = packed_gram(weighed, rows)
    packed[...] = jnp.zeros_like(packed)
    packed[0:LANES, :] = both * scale
    packed[LANES : 2 * LANES, :] = beside * scale
    packed[2 * LANES : 2 * LANES + 1, :] = diagonal * scale


def whole_gram(packed, scale):
    both = packed[0:LANES, :] * scale
    beside = packed[LANES : 2 * LANES, :] * scale
    diagonal = packed[2 * LANES : 2 * LANES + 1, :] * scale
    row = lax.broadcasted_iota(jnp.int32, (LANES, LANES), 0)
    col = lax.broadcasted_iota(jnp.int32, (LANES, LANES), 1)
    above = jnp.where(col > row, both, 0.0)
    below = jnp.where(col < row, both, 0.0)
    upper = above + above.T + jnp.where(col == row, both, 0.0)
    lower = below + below.T + jnp.where(col == row, diagonal, 0.0)
    return jnp.concatenate(
        [jnp.concatenate([upper, beside], axis=1), jnp.concatenate([beside.T, lower], axis=1)], axis=0
    )


def split(x):
    high = x.astype(BF16)
    return high, (x - high.astype(F32)).astype(BF16)


def times_gram(users, gram):
    uh, ul = split(users)
    gh, gl = split(gram)
    return contract(uh, gh, (1, 0)) + (contract(ul, gh, (1, 0)) + contract(uh, gl, (1, 0)))


def pick_row(ids_ref, step):
    row = lax.broadcasted_iota(jnp.int32, (2, LANES), 0)
    lane = lax.broadcasted_iota(jnp.int32, (2, LANES), 1)
    counts = jnp.zeros((2, LANES), F32)
    for n in range(ids_ref.shape[1]):
        counts = counts + jnp.where((lane == ids_ref[step, n]) & (row == 0), 1.0, 0.0)
    return counts


def lane_side():
    lane = lax.broadcasted_iota(jnp.int32, (LANES, LANES), 1)
    return lax.rem(lax.div(lane, ROWS), 2)


def beside(x, side):
    return jnp.where(side == 0, pltpu.roll(x, ROWS, 1), pltpu.roll(x, LANES - ROWS, 1))


def start_kernel(*refs):
    given, (out, *packets), taken, done = refs[:7], refs[7:10], refs[10:17], refs[17]
    held, ids, users, values, rows, cols, count = taken
    copies = []
    for i, (source, target) in enumerate(zip(given, taken, strict=True)):
        source = source.at[0] if target is values else source
        copies.append(pltpu.make_async_copy(source, target, done.at[i]))
    for copy in copies:
        copy.start()
    for copy in copies[:2]:
        copy.wait()
    stride = PAIR + 2
    held_rows = halves(held[...].astype(BF16))
    counts = pick_row(ids, 0).astype(BF16)
    for chunk in range(out.shape[0] // stride):
        at = chunk * stride
        out[at : at + PAIR, :] = held_rows
        out[at + PAIR : at + stride, :] = counts
    for copy in copies[2:]:
        copy.wait()
    size = users.shape[0]
    packets[0][0:size, :] = users[:, :LANES].astype(BF16)
    packets[1][0:size, :] = users[:, LANES:].astype(BF16)
    theirs = 1 - lax.axis_index("pair")
    first = lane_side() == theirs
    slots = values.shape[0]
    for k in range(slots // 2):
        other = beside(values[k + slots // 2].astype(F32), theirs)
        at = size + k // 2 * LANES
        packets[k % 2][at : at + LANES, :] = jnp.where(first, values[k].astype(F32), other).astype(BF16)
    lane = lax.broadcasted_iota(jnp.int32, (16, LANES), 1)
    lists = jnp.where(lane == 2 * slots, count[0], 0)
    for k in range(slots):
        lists = jnp.where(lane == k, rows[0, k], jnp.where(lane == slots + k, cols[0, k], lists))
    at = size + slots // 4 * LANES
    packets[0][at : at + 16, :] = lists.astype(F32).astype(BF16)


def lists_of(packet, slots):
    size = packet.shape[0]
    line = packet[size - 16 : size, :].astype(F32)[0:1]
    lane = lax.broadcasted_iota(jnp.int32, line.shape, 1)
    return [
        jnp.sum(jnp.where(lane == k, line, 0.0)).astype(jnp.int32) for k in range(2 * slots + 1)
    ]


def item_grads(users_bf, block, values, rows, cols, live, errors, owned, scale, add):
    slots, tile_u, tile_i = errors.shape
    for k in range(slots):
        row = pl.multiple_of(rows(k) * tile_u, tile_u)
        col = cols(k)
        user_tile = users_bf[pl.ds(row, tile_u), :]
        item_tile = block[pl.ds(pl.multiple_of(col * tile_i, tile_i), tile_i), :]
        scores = contract(user_tile, item_tile, (1, 1))
        there = k < live if owned is None else owned & (k < live)
        err = jnp.where(there, scores - values(k).astype(F32), 0.0).astype(BF16)
        errors[k] = err
        if scale is not None:
            err = err * jnp.asarray(scale, BF16)
        add(col, contract(err, user_tile, (0, 0)))


def user_grads(block, rows, cols, errors, grad_users):
    slots, tile_u, tile_i = errors.shape
    grad_users[...] = jnp.zeros_like(grad_users)
    for k in range(slots):
        row = pl.multiple_of(rows(k) * tile_u, tile_u)
        col = pl.multiple_of(cols(k) * tile_i, tile_i)
        grad_users[pl.ds(row, tile_u), :] += contract(errors[k], block[pl.ds(col, tile_i), :], (1, 0))


def at_step(ref, step):
    return lambda k: ref[step, k]


def from_list(scalars, first):
    return lambda k: scalars[first + k]


def pair_rows(chunk, side):
    return pl.ds(pl.multiple_of(chunk * 2 * ROWS + side * ROWS, ROWS), ROWS)


def first_kernel(
    got, users, packet, packet_too, values, rows, cols, count,
    sums, block, errors, their_errors, users_bf, their_users, grads,
):
    stride = PAIR + 2
    chunks = got.shape[0] // stride
    side = lax.axis_index("pair")
    slots, tile_u, tile_i = errors.shape
    block[...] = jnp.zeros_like(block)
    for chunk in range(chunks):
        at = chunk * stride
        block[pair_rows(chunk, side), :LANES] = got[at : at + ROWS, :]
        block[pair_rows(chunk, side), LANES:] = got[at + ROWS : at + PAIR, :]
    users_bf[...] = users[...].astype(BF16)
    grads[...] = jnp.zeros_like(grads)
    owned = lane_side() == side
    size = users.shape[0]
    their_users[:, :LANES] = packet[0:size, :]
    their_users[:, LANES:] = packet_too[0:size, :]
    theirs = lists_of(packet, slots)

    def their_values(k):
        at = size + k % (slots // 2) // 2 * tile_u
        shared = (packet, packet_too)[k % 2][at : at + tile_u, :].astype(F32)
        return shared if k < slots // 2 else beside(shared, 1 - side)

    def add(col, part):
        at = pl.multiple_of(col * part.shape[0], part.shape[0])
        grads[pl.ds(at, part.shape[0]), :] += part

    item_grads(
        users_bf, block, lambda k: values[0, k], at_step(rows, 0), at_step(cols, 0), count[0],
        errors, owned, GRAD_SCALE, add,
    )
    item_grads(
        their_users, block, their_values, from_list(theirs, 0), from_list(theirs, slots),
        theirs[2 * slots], their_errors, owned, GRAD_SCALE, add,
    )
    for chunk in range(chunks):
        sums[chunk] = halves(grads[pair_rows(chunk, side), :])


def first_users_kernel(
    got, block, users, rows, cols, errors, packet, their_errors,
    users_out, their_grads, piece_out, their_piece, counts, packed, pieces, mine, grad_users,
):
    stride = PAIR + 2
    chunks = got.shape[0] // stride
    side = lax.axis_index("pair")
    for chunk in range(chunks):
        at = chunk * stride + PAIR
        counts[chunk : chunk + 1, :] = got[at : at + 2, :].astype(F32)[0:1]
        mine[chunk * ROWS : (chunk + 1) * ROWS, :] = block[pair_rows(chunk, side), :]
    shape = (chunks, ROWS, LANES)
    own = lax.broadcasted_iota(jnp.int32, shape, 1) == lax.broadcasted_iota(jnp.int32, shape, 2)
    weight = jnp.sum(jnp.where(own, counts[...][:, None, :], 0.0), axis=2, keepdims=True)
    plain = mine[...]
    left = (plain[:, :LANES].astype(F32).reshape(shape) * weight).reshape(-1, LANES)
    right = (plain[:, LANES:].astype(F32).reshape(shape) * weight).reshape(-1, LANES)
    high, low = split(jnp.concatenate([left, right], axis=1))
    put_packed(
        packed,
        jnp.concatenate([high, low], axis=0),
        jnp.concatenate([plain, plain], axis=0),
        GRAM_STRATUM_SCALE,
    )
    devices = pieces.shape[0]
    piece = packed.shape[0] // devices
    for device in range(devices):
        pieces[device, 0:piece, :] = packed[device * piece : (device + 1) * piece, :]
    me = lax.axis_index(INNER)
    piece_out[...] = pieces[me]
    their_piece[...] = pieces[me + 1 - 2 * side]
    slots = errors.shape[0]
    theirs = lists_of(packet, slots)
    user_grads(block, from_list(theirs, 0), from_list(theirs, slots), their_errors, their_grads)
    user_grads(block, at_step(rows, 0), at_step(cols, 0), errors, grad_users)
    users_out[...] = users[...] - LR_USER * grad_users[...]


def update(held, accum, gradient):
    accum = accum + gradient * gradient
    return held - LR_ITEM * gradient / jnp.sqrt(accum), accum


def pick_counts(ids_ref, step):
    row = lax.broadcasted_iota(jnp.int32, (8, LANES), 0)
    lane = lax.broadcasted_iota(jnp.int32, (8, LANES), 1)
    row = jnp.where(lane < LANES // 2, row, row + 8)
    counts = jnp.zeros((8, LANES), F32)
    for n in range(ids_ref.shape[1]):
        counts = counts + jnp.where(row == ids_ref[step, n], 1.0, 0.0)
    return counts


def item_kernel(got, held, accum, gram_piece, their_piece, ids, state, out):
    side = lax.axis_index("pair")
    strata = out.shape[0]
    gradient = widths(jnp.sum(got[...], axis=0) * (1.0 / GRAD_SCALE))
    new, state[ROWS:, :] = update(held[...], accum[...], gradient)
    state[0:ROWS, :] = new
    items = halves(new.astype(BF16).astype(F32)) * ITEM_SCALE
    counts = pick_counts(ids, 1)
    for to in range(2):
        piece = jnp.where(side == to, gram_piece[...], their_piece[...])
        sent = jnp.concatenate([items, counts, piece], axis=0)
        out[:, to] = jnp.broadcast_to(sent[None], (strata,) + sent.shape)


def gather_kernel(total, all_met, out, packed):
    strata = all_met.shape[0]
    met = all_met.at[:, lax.axis_index("pair")]
    chunks = lax.axis_size(INNER)
    piece = packed.shape[0] // chunks
    stride = PAIR + 2 * piece
    after = lax.rem(lax.axis_index("stratum") + 1, strata)
    items = met[pl.ds(after, 1), 0:PAIR, :][0]
    full = jnp.sum(all_met[:, 0, 40:, :] + all_met[:, 1, 40:, :], axis=0)[0:piece] * (GRAM_SCALE / GRAM_STRATUM_SCALE / total)
    counts = jnp.concatenate([met[-1:, 32:40, :], met[:-1, 32:40, :]], axis=0)
    counts = jnp.concatenate([counts[:, :, 0:1], counts[:, :, 64:65]], axis=1)
    rows = [met[:, 0:ROWS, :] * (1.0 / ITEM_SCALE), met[:, ROWS:PAIR, :] * (1.0 / ITEM_SCALE)]
    weighed = jnp.concatenate([(r * counts).reshape(-1, LANES) for r in rows], axis=1)
    plain = jnp.concatenate([r.reshape(-1, LANES) for r in rows], axis=1).astype(BF16)
    high, low = split(weighed)
    put_packed(
        packed,
        jnp.concatenate([high, low], axis=0),
        jnp.concatenate([plain, plain], axis=0),
        GRAM_INNER_SCALE,
    )
    for chunk in range(chunks):
        at = chunk * stride
        out[at : at + PAIR, :] = items
        out[at + PAIR : at + PAIR + piece, :] = full
        out[at + PAIR + piece : at + stride, :] = packed[chunk * piece : (chunk + 1) * piece, :]


def second_kernel(
    total, got, users, mid, rest, values, rows, cols, count, sums, mid_out, block, errors, packed, users_bf, grads
):
    chunks = block.shape[0] // ROWS
    piece = packed.shape[0] // chunks
    stride = PAIR + 2 * piece
    full = jnp.zeros((piece, LANES), F32)
    for chunk in range(chunks):
        to, at = chunk * ROWS, chunk * stride
        block[to : to + ROWS, :LANES] = (got[at : at + ROWS, :] * (1.0 / ITEM_SCALE)).astype(BF16)
        block[to : to + ROWS, LANES:] = (got[at + ROWS : at + PAIR, :] * (1.0 / ITEM_SCALE)).astype(BF16)
        packed[chunk * piece : (chunk + 1) * piece, :] = got[at + PAIR : at + PAIR + piece, :]
        full = full + got[at + PAIR + piece : at + stride, :]
    gram = whole_gram(packed, 1.0 / GRAM_SCALE)
    part = mid[...] - (LR_USER / REST_SCALE) * rest[...]
    now = part - (LR_USER * LAMBDA) * times_gram(users[...], gram)
    mid_out[...] = now
    users_bf[...] = now.astype(BF16)
    grads[...] = jnp.zeros_like(grads)

    def add(col, part):
        at = pl.multiple_of(col * part.shape[0], part.shape[0])
        grads[pl.ds(at, part.shape[0]), :] += part

    item_grads(
        users_bf, block, lambda k: values[1, k], at_step(rows, 1), at_step(cols, 1), count[1],
        errors, None, None, add,
    )
    full = full * (GRAM_SCALE / GRAM_INNER_SCALE / total)
    for chunk in range(chunks):
        at = chunk * (PAIR + piece)
        raw = halves(grads[chunk * ROWS : (chunk + 1) * ROWS, :])
        root = jnp.sqrt(jnp.abs(raw)) * ROOT_SCALE
        sums[at : at + PAIR, :] = jnp.where(raw < 0.0, -root, root)
        sums[at + PAIR : at + PAIR + piece, :] = full


def second_users_kernel(block, now, rows, cols, errors, users_out, grad_users):
    user_grads(block, at_step(rows, 1), at_step(cols, 1), errors, grad_users)
    users_out[...] = now[...] - LR_USER * grad_users[...]


def last_items_kernel(chunks, got, state, out):
    stride = got.shape[0] // chunks
    total = jnp.zeros((PAIR, LANES), F32)
    for chunk in range(chunks):
        root = got[chunk * stride : chunk * stride + PAIR, :]
        total = total + root * jnp.abs(root)
    out[0:ROWS, :], out[ROWS:, :] = update(
        state[0:ROWS, :], state[ROWS:, :], widths(total * ROOT_SCALE**-2)
    )


def last_users_kernel(chunks, got, users, mid, out, packed):
    stride = got.shape[0] // chunks
    piece = stride - PAIR
    for chunk in range(chunks):
        packed[chunk * piece : (chunk + 1) * piece, :] = got[chunk * stride + PAIR : (chunk + 1) * stride, :]
    gram = whole_gram(packed, 1.0 / GRAM_SCALE)
    out[...] = users[...] - (LR_USER * LAMBDA) * times_gram(mid[...], gram)


def call(kernel, out_shape, specs, *args, scratch=(), vmem=44):
    return pl.pallas_call(
        kernel,
        out_shape=out_shape,
        in_specs=specs,
        out_specs=jax.tree.map(lambda _: pl.BlockSpec(memory_space=VMEM), out_shape),
        scratch_shapes=scratch,
        compiler_params=pltpu.CompilerParams(vmem_limit_bytes=vmem * 2**20),
    )(*args)


def exchanged(x, axis):
    return lax.all_to_all(x, axis, 0, 0, tiled=True)


def chunks_exchanged(flat, axis):
    paired = flat.reshape(lax.axis_size(axis), -1, 2, LANES)
    return exchanged(paired, axis).reshape(flat.shape)


def swapped(x):
    return lax.ppermute(x, "pair", [(0, 1), (1, 0)])


def shards(
    user_factors, item_factors, item_accum, tile_values, tile_rows, tile_cols, tile_count, neg_ids
):
    strata = lax.axis_size("stratum")
    inners = lax.axis_size(INNER)
    group = lax.axis_size(GROUP)
    rank = item_factors.shape[1]
    total = float(strata * inners * neg_ids.shape[1])
    piece = piece_rows(inners)
    padded = -(-piece // 8) * 8
    onward = [((s + 1) % strata, s) for s in range(strata)]
    vm = pl.BlockSpec(memory_space=VMEM)
    sm = pl.BlockSpec(memory_space=SMEM)
    shape = jax.ShapeDtypeStruct
    users_shape = shape(user_factors.shape, F32)
    users_f32 = pltpu.VMEM(user_factors.shape, F32)
    users_bf = pltpu.VMEM(user_factors.shape, BF16)
    state_shape = shape((PAIR, rank), F32)
    block_shape = shape((inners * ROWS, rank), BF16)
    errors_shape = shape(tile_values.shape[1:], BF16)
    piece_shape = shape((padded, LANES), F32)
    packed = pltpu.VMEM((inners * piece, LANES), F32)

    slots = tile_values.shape[1]
    tile_count = tile_count.reshape(-1)
    packet_rows = user_factors.shape[0] + slots // 4 * LANES
    sent, packet, packet_too = call(
        start_kernel,
        (
            shape((group * (PAIR + 2), LANES), BF16),
            shape((packet_rows + 16, LANES), BF16),
            shape((packet_rows, LANES), BF16),
        ),
        [pl.BlockSpec(memory_space=pltpu.HBM)] * 7,
        item_factors, neg_ids, user_factors, tile_values, tile_rows, tile_cols, tile_count,
        scratch=[
            pltpu.VMEM(item_factors.shape, F32),
            pltpu.SMEM(neg_ids.shape, jnp.int32),
            users_f32,
            pltpu.VMEM(tile_values.shape[1:], BF16),
            pltpu.SMEM(tile_rows.shape, jnp.int32),
            pltpu.SMEM(tile_cols.shape, jnp.int32),
            pltpu.SMEM(tile_count.shape, jnp.int32),
            pltpu.SemaphoreType.DMA((7,)),
        ],
        vmem=62,
    )
    got = chunks_exchanged(sent, GROUP)
    packet, packet_too = swapped(packet), swapped(packet_too)
    sums, block, errors, their_errors = call(
        first_kernel,
        (shape((group, PAIR, LANES), F32), block_shape, errors_shape, errors_shape),
        [vm, vm, vm, vm, vm, sm, sm, sm],
        got, user_factors, packet, packet_too, tile_values, tile_rows, tile_cols, tile_count,
        scratch=[users_bf, users_bf, pltpu.VMEM(block_shape.shape, F32)],
    )
    mid, rest, gram_piece, their_piece = call(
        first_users_kernel,
        (users_shape, users_shape, piece_shape, piece_shape),
        [vm, vm, vm, sm, sm, vm, vm, vm],
        got, block, user_factors, tile_rows, tile_cols, errors, packet, their_errors,
        scratch=[
            pltpu.VMEM((group, LANES), F32),
            packed,
            pltpu.VMEM((inners, padded, LANES), F32),
            pltpu.VMEM((group * ROWS, rank), BF16),
            users_f32,
        ],
    )
    sums, mid, rest, gram_piece, their_piece = lax.optimization_barrier(
        (sums.astype(F16), mid, rest, gram_piece, their_piece)
    )
    sums = exchanged(sums, GROUP).astype(F32)
    rest = swapped((rest * REST_SCALE).astype(F16))
    state, sent = call(
        item_kernel,
        (state_shape, shape((strata, 2, PAIR + 8 + padded, LANES), F32)),
        [vm, vm, vm, vm, vm, sm],
        sums, item_factors, item_accum, gram_piece, their_piece, neg_ids,
    )
    met = exchanged(sent.astype(F16).reshape(2 * strata, -1, LANES), ("stratum", "pair"))
    met = met.reshape(sent.shape).astype(F32)
    sent = call(
        functools.partial(gather_kernel, total),
        shape((inners * (PAIR + 2 * piece), LANES), F32),
        [vm],
        met,
        scratch=[packed],
    ).astype(F16)
    got = chunks_exchanged(sent, INNER)
    state = lax.ppermute(state, "stratum", onward)
    got, rest, state = lax.optimization_barrier((got, rest, state))
    got = got.astype(F32)
    sums, mid, block, errors = call(
        functools.partial(second_kernel, total),
        (shape((inners * (PAIR + piece), LANES), F32), users_shape, block_shape, errors_shape),
        [vm, vm, vm, vm, vm, sm, sm, sm],
        got, user_factors, mid, rest.astype(F32), tile_values, tile_rows, tile_cols, tile_count,
        scratch=[packed, users_bf, pltpu.VMEM(block_shape.shape, F32)],
    )
    got = chunks_exchanged(sums.astype(F16), INNER).astype(F32)
    users = call(
        second_users_kernel, users_shape, [vm, vm, sm, sm, vm],
        block, mid, tile_rows, tile_cols, errors, scratch=[users_f32],
    )
    state = call(functools.partial(last_items_kernel, inners), state_shape, [vm, vm], got, state)
    state = lax.ppermute(state, "stratum", onward)
    users = call(
        functools.partial(last_users_kernel, inners), users_shape, [vm, vm, vm],
        got, users, mid, scratch=[packed],
    )
    return (users, state[:ROWS], state[ROWS:])


def solution(mesh):
    strata, inners = mesh.devices.shape
    fine = jax.sharding.Mesh(
        mesh.devices.reshape(strata, inners // 4, 2, 2), ("stratum",) + INNER
    )
    every = ("stratum",) + INNER
    devices = P(every, None)
    slots = P(None, every)
    return jax.shard_map(
        shards,
        mesh=fine,
        in_specs=(
            devices,
            devices,
            devices,
            P(None, every, None, None),
            slots,
            slots,
            slots,
            slots,
        ),
        out_specs=(devices, devices, devices),
        check_vma=False,
    )
```

```python
import functools

import jax
import jax.numpy as jnp
from jax import lax
from jax.experimental import pallas as pl
from jax.experimental.pallas import tpu as pltpu
from jax.sharding import PartitionSpec as P

LR_USER = 0.005
LR_ITEM = 0.05
LAMBDA = 64.0

LANES = 128
F32 = jnp.float32
BF16 = jnp.bfloat16
F16 = jnp.float16

GRAD_SCALE = 2.0**-7
REST_SCALE = 2.0**-6
ROOT_SCALE = 2.0**-9
ITEM_SCALE = 2.0**12
GRAM_SCALE = 2.0**12
GRAM_STRATUM_SCALE = 2.0**5
GRAM_INNER_SCALE = 2.0**6

ROWS = 16
PAIR = 2 * ROWS
PACKED = 2 * LANES + 1

GROUP = ("far", "near")
INNER = ("far", "near", "pair")

VMEM = pltpu.VMEM
SMEM = pltpu.SMEM


def contract(a, b, dims):
    return lax.dot_general(a, b, ((dims[:1], dims[1:]), ((), ())), preferred_element_type=F32)


def halves(x):
    return jnp.concatenate([x[:, :LANES], x[:, LANES:]], axis=0)


def widths(x):
    rows = x.shape[0] // 2
    return jnp.concatenate([x[:rows], x[rows:]], axis=1)


def piece_rows(chunks):
    return 2 * (-(-PACKED // (2 * chunks)))


def packed_gram(weighed, rows):
    gram = contract(weighed, rows, (0, 0))
    upper, beside, lower = gram[:LANES, :LANES], gram[:LANES, LANES:], gram[LANES:, LANES:]
    row = lax.broadcasted_iota(jnp.int32, (LANES, LANES), 0)
    col = lax.broadcasted_iota(jnp.int32, (LANES, LANES), 1)
    both = jnp.where(col >= row, upper, lower)
    return both, beside, jnp.sum(jnp.where(col == row, lower, 0.0), axis=0, keepdims=True)


def put_packed(packed, weighed, rows, scale):
    both, beside, diagonal = packed_gram(weighed, rows)
    packed[...] = jnp.zeros_like(packed)
    packed[0:LANES, :] = both * scale
    packed[LANES : 2 * LANES, :] = beside * scale
    packed[2 * LANES : 2 * LANES + 1, :] = diagonal * scale


def whole_gram(packed, scale):
    both = packed[0:LANES, :] * scale
    beside = packed[LANES : 2 * LANES, :] * scale
    diagonal = packed[2 * LANES : 2 * LANES + 1, :] * scale
    row = lax.broadcasted_iota(jnp.int32, (LANES, LANES), 0)
    col = lax.broadcasted_iota(jnp.int32, (LANES, LANES), 1)
    above = jnp.where(col > row, both, 0.0)
    below = jnp.where(col < row, both, 0.0)
    upper = above + above.T + jnp.where(col == row, both, 0.0)
    lower = below + below.T + jnp.where(col == row, diagonal, 0.0)
    return jnp.concatenate(
        [jnp.concatenate([upper, beside], axis=1), jnp.concatenate([beside.T, lower], axis=1)], axis=0
    )


def split(x):
    high = x.astype(BF16)
    return high, (x - high.astype(F32)).astype(BF16)


def times_gram(users, gram):
    uh, ul = split(users)
    gh, gl = split(gram)
    return contract(uh, gh, (1, 0)) + (contract(ul, gh, (1, 0)) + contract(uh, gl, (1, 0)))


def pick_row(ids_ref, step):
    row = lax.broadcasted_iota(jnp.int32, (2, LANES), 0)
    lane = lax.broadcasted_iota(jnp.int32, (2, LANES), 1)
    counts = jnp.zeros((2, LANES), F32)
    for n in range(ids_ref.shape[1]):
        counts = counts + jnp.where((lane == ids_ref[step, n]) & (row == 0), 1.0, 0.0)
    return counts


def lane_side():
    lane = lax.broadcasted_iota(jnp.int32, (LANES, LANES), 1)
    return lax.rem(lax.div(lane, ROWS), 2)


def beside(x, side):
    return jnp.where(side == 0, pltpu.roll(x, ROWS, 1), pltpu.roll(x, LANES - ROWS, 1))


def start_kernel(*refs):
    given, (out, *packets), taken, done = refs[:7], refs[7:11], refs[11:18], refs[18]
    held, ids, users, values, rows, cols, count = taken
    copies = []
    for i, (source, target) in enumerate(zip(given, taken, strict=True)):
        source = source.at[0] if target is values else source
        copies.append(pltpu.make_async_copy(source, target, done.at[i]))
    for copy in copies:
        copy.start()
    for copy in copies[:2]:
        copy.wait()
    stride = PAIR + 2
    held_rows = halves(held[...].astype(BF16))
    counts = pick_row(ids, 0).astype(BF16)
    for chunk in range(out.shape[0] // stride):
        at = chunk * stride
        out[at : at + PAIR, :] = held_rows
        out[at + PAIR : at + stride, :] = counts
    for copy in copies[2:]:
        copy.wait()
    size = users.shape[0]
    packets[0][0:size, :] = users[:, :LANES].astype(BF16)
    packets[1][0:size, :] = users[:, LANES:].astype(BF16)
    theirs = 1 - lax.axis_index("pair")
    first = lane_side() == theirs
    slots = values.shape[0]
    for k in range(slots // 2):
        other = beside(values[k + slots // 2].astype(F32), theirs)
        packets[2][k * LANES : (k + 1) * LANES, :] = jnp.where(first, values[k].astype(F32), other).astype(BF16)
    lane = lax.broadcasted_iota(jnp.int32, (16, LANES), 1)
    lists = jnp.where(lane == 2 * slots, count[0], 0)
    for k in range(slots):
        lists = jnp.where(lane == k, rows[0, k], jnp.where(lane == slots + k, cols[0, k], lists))
    packets[0][size : size + 16, :] = lists.astype(F32).astype(BF16)


def lists_of(packet, slots):
    size = packet.shape[0]
    line = packet[size - 16 : size, :].astype(F32)[0:1]
    lane = lax.broadcasted_iota(jnp.int32, line.shape, 1)
    return [
        jnp.sum(jnp.where(lane == k, line, 0.0)).astype(jnp.int32) for k in range(2 * slots + 1)
    ]


def item_grads(users_bf, block, values, rows, cols, live, errors, owned, scale, add):
    slots, tile_u, tile_i = errors.shape
    for k in range(slots):
        row = pl.multiple_of(rows(k) * tile_u, tile_u)
        col = cols(k)
        user_tile = users_bf[pl.ds(row, tile_u), :]
        item_tile = block[pl.ds(pl.multiple_of(col * tile_i, tile_i), tile_i), :]
        scores = contract(user_tile, item_tile, (1, 1))
        there = k < live if owned is None else owned & (k < live)
        err = jnp.where(there, scores - values(k).astype(F32), 0.0).astype(BF16)
        errors[k] = err
        if scale is not None:
            err = err * jnp.asarray(scale, BF16)
        add(col, contract(err, user_tile, (0, 0)))


def user_grads(block, rows, cols, errors, grad_users):
    slots, tile_u, tile_i = errors.shape
    grad_users[...] = jnp.zeros_like(grad_users)
    for k in range(slots):
        row = pl.multiple_of(rows(k) * tile_u, tile_u)
        col = pl.multiple_of(cols(k) * tile_i, tile_i)
        grad_users[pl.ds(row, tile_u), :] += contract(errors[k], block[pl.ds(col, tile_i), :], (1, 0))


def at_step(ref, step):
    return lambda k: ref[step, k]


def from_list(scalars, first):
    return lambda k: scalars[first + k]


def pair_rows(chunk, side):
    return pl.ds(pl.multiple_of(chunk * 2 * ROWS + side * ROWS, ROWS), ROWS)


def first_kernel(
    got, users, packet, packet_too, packet_three, values, rows, cols, count,
    sums, block, errors, their_errors, users_bf, their_users, grads,
):
    stride = PAIR + 2
    chunks = got.shape[0] // stride
    side = lax.axis_index("pair")
    slots, tile_u, tile_i = errors.shape
    block[...] = jnp.zeros_like(block)
    for chunk in range(chunks):
        at = chunk * stride
        block[pair_rows(chunk, side), :LANES] = got[at : at + ROWS, :]
        block[pair_rows(chunk, side), LANES:] = got[at + ROWS : at + PAIR, :]
    users_bf[...] = users[...].astype(BF16)
    grads[...] = jnp.zeros_like(grads)
    owned = lane_side() == side
    size = users.shape[0]
    their_users[:, :LANES] = packet[0:size, :]
    their_users[:, LANES:] = packet_too[0:size, :]
    theirs = lists_of(packet, slots)

    def their_values(k):
        at = k % (slots // 2) * tile_u
        shared = packet_three[at : at + tile_u, :].astype(F32)
        return shared if k < slots // 2 else beside(shared, 1 - side)

    def add(col, part):
        at = pl.multiple_of(col * part.shape[0], part.shape[0])
        grads[pl.ds(at, part.shape[0]), :] += part

    item_grads(
        users_bf, block, lambda k: values[0, k], at_step(rows, 0), at_step(cols, 0), count[0],
        errors, owned, GRAD_SCALE, add,
    )
    item_grads(
        their_users, block, their_values, from_list(theirs, 0), from_list(theirs, slots),
        theirs[2 * slots], their_errors, owned, GRAD_SCALE, add,
    )
    for chunk in range(chunks):
        sums[chunk] = halves(grads[pair_rows(chunk, side), :])


def first_users_kernel(
    got, block, users, rows, cols, errors, packet, their_errors,
    users_out, their_grads, piece_out, their_piece, counts, packed, pieces, mine, grad_users,
):
    stride = PAIR + 2
    chunks = got.shape[0] // stride
    side = lax.axis_index("pair")
    for chunk in range(chunks):
        at = chunk * stride + PAIR
        counts[chunk : chunk + 1, :] = got[at : at + 2, :].astype(F32)[0:1]
        mine[chunk * ROWS : (chunk + 1) * ROWS, :] = block[pair_rows(chunk, side), :]
    shape = (chunks, ROWS, LANES)
    own = lax.broadcasted_iota(jnp.int32, shape, 1) == lax.broadcasted_iota(jnp.int32, shape, 2)
    weight = jnp.sum(jnp.where(own, counts[...][:, None, :], 0.0), axis=2, keepdims=True)
    plain = mine[...]
    left = (plain[:, :LANES].astype(F32).reshape(shape) * weight).reshape(-1, LANES)
    right = (plain[:, LANES:].astype(F32).reshape(shape) * weight).reshape(-1, LANES)
    high, low = split(jnp.concatenate([left, right], axis=1))
    put_packed(
        packed,
        jnp.concatenate([high, low], axis=0),
        jnp.concatenate([plain, plain], axis=0),
        GRAM_STRATUM_SCALE,
    )
    devices = pieces.shape[0]
    piece = packed.shape[0] // devices
    for device in range(devices):
        pieces[device, 0:piece, :] = packed[device * piece : (device + 1) * piece, :]
    me = lax.axis_index(INNER)
    piece_out[...] = pieces[me]
    their_piece[...] = pieces[me + 1 - 2 * side]
    slots = errors.shape[0]
    theirs = lists_of(packet, slots)
    user_grads(block, from_list(theirs, 0), from_list(theirs, slots), their_errors, their_grads)
    user_grads(block, at_step(rows, 0), at_step(cols, 0), errors, grad_users)
    users_out[...] = users[...] - LR_USER * grad_users[...]


def update(held, accum, gradient):
    accum = accum + gradient * gradient
    return held - LR_ITEM * gradient / jnp.sqrt(accum), accum


def pick_counts(ids_ref, step):
    row = lax.broadcasted_iota(jnp.int32, (8, LANES), 0)
    lane = lax.broadcasted_iota(jnp.int32, (8, LANES), 1)
    row = jnp.where(lane < LANES // 2, row, row + 8)
    counts = jnp.zeros((8, LANES), F32)
    for n in range(ids_ref.shape[1]):
        counts = counts + jnp.where(row == ids_ref[step, n], 1.0, 0.0)
    return counts


def item_kernel(got, held, accum, gram_piece, their_piece, ids, state, out):
    strata = out.shape[0]
    gradient = widths(got[...] * (1.0 / GRAD_SCALE))
    new, state[ROWS:, :] = update(held[...], accum[...], gradient)
    state[0:ROWS, :] = new
    items = halves(new.astype(BF16).astype(F32)) * ITEM_SCALE
    sent = jnp.concatenate([items, pick_counts(ids, 1), gram_piece[...] + their_piece[...]], axis=0)
    out[...] = jnp.broadcast_to(sent[None], (strata,) + sent.shape)


def gather_kernel(total, met, out, packed):
    strata = met.shape[0]
    chunks = lax.axis_size(INNER)
    piece = packed.shape[0] // chunks
    stride = PAIR + 2 * piece
    after = lax.rem(lax.axis_index("stratum") + 1, strata)
    items = met[pl.ds(after, 1), 0:PAIR, :][0]
    full = jnp.sum(met[:, 40:, :], axis=0)[0:piece] * (GRAM_SCALE / GRAM_STRATUM_SCALE / total)
    counts = jnp.concatenate([met[-1:, 32:40, :], met[:-1, 32:40, :]], axis=0)
    counts = jnp.concatenate([counts[:, :, 0:1], counts[:, :, 64:65]], axis=1)
    rows = [met[:, 0:ROWS, :] * (1.0 / ITEM_SCALE), met[:, ROWS:PAIR, :] * (1.0 / ITEM_SCALE)]
    weighed = jnp.concatenate([(r * counts).reshape(-1, LANES) for r in rows], axis=1)
    plain = jnp.concatenate([r.reshape(-1, LANES) for r in rows], axis=1).astype(BF16)
    high, low = split(weighed)
    put_packed(
        packed,
        jnp.concatenate([high, low], axis=0),
        jnp.concatenate([plain, plain], axis=0),
        GRAM_INNER_SCALE,
    )
    for chunk in range(chunks):
        at = chunk * stride
        out[at : at + PAIR, :] = items
        out[at + PAIR : at + PAIR + piece, :] = full
        out[at + PAIR + piece : at + stride, :] = packed[chunk * piece : (chunk + 1) * piece, :]


def second_kernel(
    total, got, users, mid, rest, values, rows, cols, count, sums, mid_out, block, errors, packed, users_bf, grads
):
    chunks = block.shape[0] // ROWS
    piece = packed.shape[0] // chunks
    stride = PAIR + 2 * piece
    full = jnp.zeros((piece, LANES), F32)
    for chunk in range(chunks):
        to, at = chunk * ROWS, chunk * stride
        block[to : to + ROWS, :LANES] = (got[at : at + ROWS, :] * (1.0 / ITEM_SCALE)).astype(BF16)
        block[to : to + ROWS, LANES:] = (got[at + ROWS : at + PAIR, :] * (1.0 / ITEM_SCALE)).astype(BF16)
        packed[chunk * piece : (chunk + 1) * piece, :] = got[at + PAIR : at + PAIR + piece, :]
        full = full + got[at + PAIR + piece : at + stride, :]
    gram = whole_gram(packed, 1.0 / GRAM_SCALE)
    part = mid[...] - (LR_USER / REST_SCALE) * rest[...]
    now = part - (LR_USER * LAMBDA) * times_gram(users[...], gram)
    mid_out[...] = now
    users_bf[...] = now.astype(BF16)
    grads[...] = jnp.zeros_like(grads)

    def add(col, part):
        at = pl.multiple_of(col * part.shape[0], part.shape[0])
        grads[pl.ds(at, part.shape[0]), :] += part

    item_grads(
        users_bf, block, lambda k: values[1, k], at_step(rows, 1), at_step(cols, 1), count[1],
        errors, None, None, add,
    )
    full = full * (GRAM_SCALE / GRAM_INNER_SCALE / total)
    for chunk in range(chunks):
        at = chunk * (PAIR + piece)
        raw = halves(grads[chunk * ROWS : (chunk + 1) * ROWS, :])
        root = jnp.sqrt(jnp.abs(raw)) * ROOT_SCALE
        sums[at : at + PAIR, :] = jnp.where(raw < 0.0, -root, root)
        sums[at + PAIR : at + PAIR + piece, :] = full


def second_users_kernel(block, now, rows, cols, errors, users_out, grad_users):
    user_grads(block, at_step(rows, 1), at_step(cols, 1), errors, grad_users)
    users_out[...] = now[...] - LR_USER * grad_users[...]


def last_items_kernel(chunks, got, state, out):
    stride = got.shape[0] // chunks
    total = jnp.zeros((PAIR, LANES), F32)
    for chunk in range(chunks):
        root = got[chunk * stride : chunk * stride + PAIR, :]
        total = total + root * jnp.abs(root)
    out[0:ROWS, :], out[ROWS:, :] = update(
        state[0:ROWS, :], state[ROWS:, :], widths(total * ROOT_SCALE**-2)
    )


def last_users_kernel(chunks, got, users, mid, out, packed):
    stride = got.shape[0] // chunks
    piece = stride - PAIR
    for chunk in range(chunks):
        packed[chunk * piece : (chunk + 1) * piece, :] = got[chunk * stride + PAIR : (chunk + 1) * stride, :]
    gram = whole_gram(packed, 1.0 / GRAM_SCALE)
    out[...] = users[...] - (LR_USER * LAMBDA) * times_gram(mid[...], gram)


def call(kernel, out_shape, specs, *args, scratch=(), vmem=44):
    return pl.pallas_call(
        kernel,
        out_shape=out_shape,
        in_specs=specs,
        out_specs=jax.tree.map(lambda _: pl.BlockSpec(memory_space=VMEM), out_shape),
        scratch_shapes=scratch,
        compiler_params=pltpu.CompilerParams(vmem_limit_bytes=vmem * 2**20),
    )(*args)


def exchanged(x, axis):
    return lax.all_to_all(x, axis, 0, 0, tiled=True)


def chunks_exchanged(flat, axis):
    paired = flat.reshape(lax.axis_size(axis), -1, 2, LANES)
    return exchanged(paired, axis).reshape(flat.shape)


def swapped(x):
    return lax.ppermute(x, "pair", [(0, 1), (1, 0)])


def shards(
    user_factors, item_factors, item_accum, tile_values, tile_rows, tile_cols, tile_count, neg_ids
):
    strata = lax.axis_size("stratum")
    inners = lax.axis_size(INNER)
    group = lax.axis_size(GROUP)
    rank = item_factors.shape[1]
    total = float(strata * inners * neg_ids.shape[1])
    piece = piece_rows(inners)
    padded = -(-piece // 8) * 8
    onward = [((s + 1) % strata, s) for s in range(strata)]
    vm = pl.BlockSpec(memory_space=VMEM)
    sm = pl.BlockSpec(memory_space=SMEM)
    shape = jax.ShapeDtypeStruct
    users_shape = shape(user_factors.shape, F32)
    users_f32 = pltpu.VMEM(user_factors.shape, F32)
    users_bf = pltpu.VMEM(user_factors.shape, BF16)
    state_shape = shape((PAIR, rank), F32)
    block_shape = shape((inners * ROWS, rank), BF16)
    errors_shape = shape(tile_values.shape[1:], BF16)
    piece_shape = shape((padded, LANES), F32)
    packed = pltpu.VMEM((inners * piece, LANES), F32)

    slots = tile_values.shape[1]
    tile_count = tile_count.reshape(-1)
    packet_rows = user_factors.shape[0]
    sent, packet, packet_too, packet_three = call(
        start_kernel,
        (
            shape((group * (PAIR + 2), LANES), BF16),
            shape((packet_rows + 16, LANES), BF16),
            shape((packet_rows, LANES), BF16),
            shape((slots // 2 * LANES, LANES), BF16),
        ),
        [pl.BlockSpec(memory_space=pltpu.HBM)] * 7,
        item_factors, neg_ids, user_factors, tile_values, tile_rows, tile_cols, tile_count,
        scratch=[
            pltpu.VMEM(item_factors.shape, F32),
            pltpu.SMEM(neg_ids.shape, jnp.int32),
            users_f32,
            pltpu.VMEM(tile_values.shape[1:], BF16),
            pltpu.SMEM(tile_rows.shape, jnp.int32),
            pltpu.SMEM(tile_cols.shape, jnp.int32),
            pltpu.SMEM(tile_count.shape, jnp.int32),
            pltpu.SemaphoreType.DMA((7,)),
        ],
        vmem=62,
    )
    got = chunks_exchanged(sent, GROUP)
    packet, packet_too, packet_three = swapped(packet), swapped(packet_too), swapped(packet_three)
    sums, block, errors, their_errors = call(
        first_kernel,
        (shape((group, PAIR, LANES), F32), block_shape, errors_shape, errors_shape),
        [vm, vm, vm, vm, vm, vm, sm, sm, sm],
        got, user_factors, packet, packet_too, packet_three, tile_values, tile_rows, tile_cols, tile_count,
        scratch=[users_bf, users_bf, pltpu.VMEM(block_shape.shape, F32)],
    )
    sums = jnp.sum(exchanged(sums.astype(F16), GROUP).astype(F32), axis=0)
    mid, rest, gram_piece, their_piece = call(
        first_users_kernel,
        (users_shape, users_shape, piece_shape, piece_shape),
        [vm, vm, vm, sm, sm, vm, vm, vm],
        got, block, user_factors, tile_rows, tile_cols, errors, packet, their_errors,
        scratch=[
            pltpu.VMEM((group, LANES), F32),
            packed,
            pltpu.VMEM((inners, padded, LANES), F32),
            pltpu.VMEM((group * ROWS, rank), BF16),
            users_f32,
        ],
    )
    their_piece = swapped(their_piece)
    rest = swapped((rest * REST_SCALE).astype(F16))
    state, sent = call(
        item_kernel,
        (state_shape, shape((strata, PAIR + 8 + padded, LANES), F32)),
        [vm, vm, vm, vm, vm, sm],
        sums, item_factors, item_accum, gram_piece, their_piece, neg_ids,
    )
    met = exchanged(sent.astype(F16), "stratum")
    met = met.astype(F32)
    sent = call(
        functools.partial(gather_kernel, total),
        shape((inners * (PAIR + 2 * piece), LANES), F32),
        [vm],
        met,
        scratch=[packed],
    ).astype(F16)
    got = chunks_exchanged(sent, INNER)
    state = lax.ppermute(state, "stratum", onward)
    got, rest, state = lax.optimization_barrier((got, rest, state))
    got = got.astype(F32)
    sums, mid, block, errors = call(
        functools.partial(second_kernel, total),
        (shape((inners * (PAIR + piece), LANES), F32), users_shape, block_shape, errors_shape),
        [vm, vm, vm, vm, vm, sm, sm, sm],
        got, user_factors, mid, rest.astype(F32), tile_values, tile_rows, tile_cols, tile_count,
        scratch=[packed, users_bf, pltpu.VMEM(block_shape.shape, F32)],
    )
    got = chunks_exchanged(sums.astype(F16), INNER).astype(F32)
    users = call(
        second_users_kernel, users_shape, [vm, vm, sm, sm, vm],
        block, mid, tile_rows, tile_cols, errors, scratch=[users_f32],
    )
    state = call(functools.partial(last_items_kernel, inners), state_shape, [vm, vm], got, state)
    state = lax.ppermute(state, "stratum", onward)
    users = call(
        functools.partial(last_users_kernel, inners), users_shape, [vm, vm, vm],
        got, users, mid, scratch=[packed],
    )
    return (users, state[:ROWS], state[ROWS:])


def solution(mesh):
    strata, inners = mesh.devices.shape
    fine = jax.sharding.Mesh(
        mesh.devices.reshape(strata, inners // 4, 2, 2), ("stratum",) + INNER
    )
    every = ("stratum",) + INNER
    devices = P(every, None)
    slots = P(None, every)
    return jax.shard_map(
        shards,
        mesh=fine,
        in_specs=(
            devices,
            devices,
            devices,
            P(None, every, None, None),
            slots,
            slots,
            slots,
            slots,
        ),
        out_specs=(devices, devices, devices),
        check_vma=False,
    )
```
